32 devices in a mesh: org: 8 (over z, y), dst: 4 (over x, core).
Axes of the slice: x: 2, y: 2, z: 4, core: 2. Of those that a mesh axis runs over, the one named last changes fastest.
Arguments:
- od_cells: bfloat16 [16384, 128, 128], P('org', 'dst'), may hold values from -100 to 100
- anchor_edges: int32 [16384, 4], P('org'), may hold values from 0 to 255, all different within a row
- edge_weight: float32 [256], replicated, may hold values from 0.5 to 4
- mixing: bfloat16 [128, 128], replicated, may hold values from -0.5 to 0.5
- dst_edges: int32 [128, 3], replicated, may hold values from 0 to 127, all different within a row
- dst_weight: float32 [128], replicated, may hold values from 0.5 to 4
- out_bias: float32 [128], replicated, may hold values from -1.2 to 1.2
Outputs:
- layer_out: bfloat16 [16384, 128, 128], P(('org', 'dst'))
The draws below stay inside these ranges and needn't reach their ends.
Inputs may be any that keep to these rules, and one draw needn't show every extreme that they name: `anchor_edges`: each anchor zone lists 4 different corridors, and every corridor is listed by at least one anchor zone. `dst_edges`: each destination zone lists 3 different hyperedges, and every hyperedge is listed by at least one destination zone.
All inputs are finite; a program needn't handle non-finite values.
Results may differ from the reference program's by a relative error of at most 0.0066.
Values may be sent and summed in bfloat16 or wider, within the bound.
No kernel may reach another device: no remote copies, remote signals or barrier semaphores. Data moves between devices by JAX's collectives and lax.ppermute only.
A program may use at most 128 MiB of HBM per device.

```python
import math
import jax
import jax.numpy as jnp
from jax import lax

DD = 128
C = 128
E = 256
F = 128
M = 4
MD = 3
ORG_DEV = 2048
ANCHORS = 16384
N_ORG = 8


def level_of(rng, dims, shards, least, high):
    level = 1.0
    for dim, blocks in shards:
        steps = jax.random.uniform(jax.random.fold_in(jax.random.fold_in(rng, 6), dim), (blocks,), jnp.float32, least / len(shards), high / len(shards))
        level = level * jnp.repeat(jnp.exp(steps), dims[dim] // blocks).reshape((-1,) + (1,) * (len(dims) - 1 - dim))
    return level


def picks_of(key, rows, amount, top, lift):
    order = jax.random.permutation(jax.random.fold_in(key, 1), amount)
    pull = order
    for power in range(3):
        pull = pull * pull // amount
    pull = pull * lift // amount
    chance = jax.random.randint(jax.random.fold_in(key, 2), (rows, amount), 0, 4096) + pull
    fixed_rows = jax.random.permutation(jax.random.fold_in(key, 3), rows)[jnp.arange(amount) % rows]
    chance = jnp.where(jnp.arange(rows)[:, None] == fixed_rows[None, :], 1 << 14, chance)
    merit = chance * amount + jnp.arange(amount)
    return lax.top_k(merit.astype(jnp.int32), top)[1].astype(jnp.int32)


def scatter_about(own_key, shape, scale, reach, shards=(), held_as=jnp.bfloat16):
    values = jax.random.normal(own_key, shape, jnp.float32) * scale
    if len(shards) > 0:
        values = level_of(own_key, shape, shards, -0.22, 0.18) * values
    return jnp.clip(values, min=-reach, max=reach).astype(held_as)


def setup_inputs(seed: int = 0) -> dict:
    streams_of = jax.random.split(jax.random.key(seed), 8)
    od_cells = scatter_about(streams_of[0], (ANCHORS, DD, C), 40.0, 100.0, ((0, 8), (1, 4)))
    anchor_edges = picks_of(streams_of[1], ANCHORS, E, M, 256)
    edge_weight = jnp.clip(jnp.exp(jax.random.uniform(streams_of[2], (E,), jnp.float32, math.log(0.5), math.log(4.0))), 0.5, 4.0)
    mixing = scatter_about(streams_of[3], (C, C), C ** -0.5, 0.5)
    dst_edges = picks_of(streams_of[4], DD, F, MD, 192)
    dst_weight = jnp.clip(jnp.exp(jax.random.uniform(streams_of[5], (F,), jnp.float32, math.log(0.5), math.log(4.0))), 0.5, 4.0)
    out_bias = scatter_about(streams_of[6], (C,), 0.3, 1.2, (), jnp.float32)
    return {"od_cells": od_cells, "anchor_edges": anchor_edges, "edge_weight": edge_weight, "mixing": mixing, "dst_edges": dst_edges, "dst_weight": dst_weight, "out_bias": out_bias}


def corridor_table(edge_ids, edge_count):
    columns = jnp.arange(edge_count, dtype=jnp.int32)
    return lax.optimization_barrier(jnp.sum((edge_ids[:, :, None] == columns[None, None, :]).astype(jnp.float32), axis=1))

def anchor_root(member, edge_weight):
    return lax.rsqrt(lax.optimization_barrier(jnp.sum(member * edge_weight[None, :], axis=1)))

def dest_operator(dst_edges, dst_weight):
    dst_member = corridor_table(dst_edges, dst_weight.shape[0])
    dst_degree = lax.optimization_barrier(jnp.sum(dst_member * dst_weight[None, :], axis=1))
    edge_sizes = lax.optimization_barrier(jnp.sum(dst_member, axis=0))
    left_factor = dst_member * lax.rsqrt(dst_degree)[:, None]
    right_factor = left_factor * (dst_weight / edge_sizes)[None, :]
    result = jnp.dot(right_factor, left_factor.T, precision=lax.Precision.HIGHEST)
    return result.astype(jnp.bfloat16)

def reference(od_cells, anchor_edges, edge_weight, mixing, dst_edges, dst_weight, out_bias):
    member = corridor_table(anchor_edges, E)
    inverse_root = anchor_root(member, edge_weight)
    weighted = member.astype(jnp.bfloat16) * inverse_root.astype(jnp.bfloat16)[:, None]
    anchors = od_cells.shape[0]
    flattened = od_cells.reshape(anchors, DD * C)
    edge_sums = jnp.dot(weighted.T, flattened, preferred_element_type=jnp.float32)
    counts = lax.optimization_barrier(jnp.sum(member, axis=0))
    totals = (edge_sums * (edge_weight / counts)[:, None]).astype(jnp.bfloat16)
    dst_matrix = dest_operator(dst_edges, dst_weight)
    member_hot = member.astype(jnp.bfloat16)

    def block_out(first_row):
        block_rows = lax.dynamic_slice_in_dim(member_hot, first_row, ORG_DEV, 0)
        block_root = lax.dynamic_slice_in_dim(inverse_root, first_row, ORG_DEV, 0)
        spread = jnp.dot(block_rows, totals, preferred_element_type=jnp.float32)
        first_layer = (spread * block_root[:, None]).astype(jnp.bfloat16)
        mixed_rows = jnp.dot(first_layer.reshape(ORG_DEV * DD, C), mixing, preferred_element_type=jnp.float32)
        mixed_rows = mixed_rows.astype(jnp.bfloat16).reshape(ORG_DEV, DD, C)
        convolved = jnp.einsum('de,oec->odc', dst_matrix.astype(jnp.float32), mixed_rows.astype(jnp.float32))
        return jnp.maximum(convolved + out_bias[None, None, :], 0.0).astype(jnp.bfloat16)
    starts = (jnp.arange(N_ORG, dtype=jnp.int32) * ORG_DEV).astype(jnp.int32)
    blocks = lax.map(block_out, starts)
    return blocks.reshape(anchors, DD, C)
```

```python
import jax
import jax.numpy as jnp
from jax import lax
from jax.sharding import PartitionSpec as P


def corridor_table(edge_ids, edge_count):
    columns = jnp.arange(edge_count, dtype=jnp.int32)
    return jnp.sum((edge_ids[:, :, None] == columns[None, None, :]).astype(jnp.float32), axis=1)


def dest_operator(dst_edges, dst_weight):
    dst_member = corridor_table(dst_edges, dst_weight.shape[0])
    dst_degree = jnp.sum(dst_member * dst_weight[None, :], axis=1)
    edge_sizes = jnp.sum(dst_member, axis=0)
    left_factor = dst_member * lax.rsqrt(dst_degree)[:, None]
    right_factor = left_factor * (dst_weight / edge_sizes)[None, :]
    result = jnp.dot(right_factor, left_factor.T, precision=lax.Precision.HIGHEST)
    return result.astype(jnp.bfloat16)


def shards(od_cells, anchor_edges, edge_weight, mixing, dst_edges, dst_weight, out_bias):
    edge_count = edge_weight.shape[0]
    n_org = lax.axis_size("org")
    n_dst = lax.axis_size("dst")
    member = corridor_table(anchor_edges, edge_count)
    inverse_root = lax.rsqrt(jnp.sum(member * edge_weight[None, :], axis=1))
    member_hot = member.astype(jnp.bfloat16)
    weighted = member_hot * inverse_root.astype(jnp.bfloat16)[:, None]
    whole_counts = lax.psum(jnp.sum(member, axis=0), "org")
    partial_sums = jnp.einsum("oe,odc->edc", weighted, od_cells, preferred_element_type=jnp.float32)
    own = edge_count // n_org
    parts = partial_sums.astype(jnp.bfloat16).reshape((n_org, own) + partial_sums.shape[1:])
    parts = lax.all_to_all(parts, "org", split_axis=0, concat_axis=0, tiled=True)
    sums = jnp.sum(parts.astype(jnp.float32), axis=0)
    first = lax.axis_index("org") * own
    scale = lax.dynamic_slice_in_dim(edge_weight / whole_counts, first, own, 0)
    totals = (sums * scale[:, None, None]).astype(jnp.bfloat16)
    mixed = jnp.einsum("ekc,cf->ekf", totals, mixing, preferred_element_type=jnp.float32).astype(jnp.bfloat16)
    mixed = lax.all_to_all(mixed, "dst", split_axis=0, concat_axis=1, tiled=True)
    dst_matrix = dest_operator(dst_edges, dst_weight)
    table = jnp.einsum("dk,ekc->edc", dst_matrix, mixed, preferred_element_type=jnp.float32).astype(jnp.bfloat16)
    table = lax.all_gather(table, ("org", "dst"), axis=0, tiled=True)
    rows = anchor_edges.shape[0] // n_dst
    start = lax.axis_index("dst") * rows
    own_member = lax.dynamic_slice_in_dim(member_hot, start, rows, 0)
    own_root = lax.dynamic_slice_in_dim(inverse_root, start, rows, 0)
    spread = jnp.einsum("re,edc->rdc", own_member, table, preferred_element_type=jnp.float32)
    result = spread * own_root[:, None, None] + out_bias[None, None, :]
    return jnp.maximum(result, 0.0).astype(jnp.bfloat16)


def solution(mesh):
    in_specs = (P("org", "dst", None), P("org", None), P(), P(), P(), P(), P())
    out_specs = P(("org", "dst"), None, None)
    return jax.shard_map(shards, mesh=mesh, in_specs=in_specs, out_specs=out_specs, check_vma=False)
```

```python
import functools

import jax
import jax.numpy as jnp
from jax import lax
from jax.experimental import pallas as pl
from jax.experimental.pallas import tpu as pltpu
from jax.sharding import Mesh, PartitionSpec as P

BF16 = jnp.bfloat16
F32 = jnp.float32
COUNT_BASE = 128.0
HEAD = 16


def corridor_table(edge_ids, edge_count):
    columns = jnp.arange(edge_count, dtype=jnp.int32)
    return jnp.sum((edge_ids[:, :, None] == columns[None, None, :]).astype(F32), axis=1)


def dest_operator(dst_edges, dst_weight):
    dst_member = corridor_table(dst_edges, dst_weight.shape[0])
    dst_degree = jnp.sum(dst_member * dst_weight[None, :], axis=1)
    edge_sizes = jnp.sum(dst_member, axis=0)
    left_factor = dst_member * lax.rsqrt(dst_degree)[:, None]
    right_factor = left_factor * (dst_weight / edge_sizes)[None, :]
    result = jnp.dot(right_factor, left_factor.T, precision=lax.Precision.HIGHEST)
    return result.astype(BF16)


def gather_kernel(own, edges_ref, weight_ref, cells_ref, out_ref, root_ref, wide_ref, total_ref, count_ref):
    step = pl.program_id(0)
    last = pl.num_programs(0) - 1
    rows, zones, lanes = cells_ref.shape
    edges = weight_ref.shape[0]

    @pl.when(step == 0)
    def _():
        total_ref[...] = jnp.zeros_like(total_ref)
        count_ref[...] = jnp.zeros_like(count_ref)

    columns = lax.broadcasted_iota(jnp.int32, (edges, rows), 0)
    ids = edges_ref[...]
    member = columns == ids[0:1, :]
    for j in range(1, ids.shape[0]):
        member = jnp.logical_or(member, columns == ids[j : j + 1, :])
    root = lax.rsqrt(jnp.sum(jnp.where(member, weight_ref[...], 0.0), axis=0, keepdims=True))
    root_ref[...] = root
    rounded = root.astype(BF16).astype(F32)
    weighted = jnp.where(member, rounded, 0.0).astype(BF16)
    hot = jnp.where(member, 1.0, 0.0).astype(BF16)
    count_ref[...] += jnp.dot(hot, jnp.ones((rows, lanes), BF16), preferred_element_type=F32)

    part = min(rows, 16)

    def widen(i, carry):
        piece = cells_ref[pl.ds(i * part, part)].astype(F32)
        wide_ref[pl.ds(i * part * zones, part * zones), :] = piece.reshape(part * zones, lanes)
        return carry

    lax.fori_loop(0, rows // part, widen, 0)
    for pair in range(zones // 2):
        left = wide_ref[pl.ds(2 * pair, rows, stride=zones), :].astype(BF16)
        right = wide_ref[pl.ds(2 * pair + 1, rows, stride=zones), :].astype(BF16)
        both = jnp.concatenate([left, right], axis=1)
        total_ref[pair] += jnp.dot(weighted, both, preferred_element_type=F32)

    @pl.when(step == last)
    def _():
        for d in range(zones):
            column = total_ref[d // 2, :, (d % 2) * lanes : (d % 2 + 1) * lanes]
            wide_ref[pl.ds(d, edges, stride=zones), :] = column
        counts = count_ref[...]
        high = jnp.floor(counts * (1.0 / COUNT_BASE))
        low = counts - high * COUNT_BASE
        for block in range(edges // own):
            first = block * own
            data = wide_ref[first * zones : (first + own) * zones, :].astype(BF16)
            out_ref[block, HEAD : HEAD + own * zones, :] = data
            pad = jnp.zeros((HEAD // 2 - own, lanes), F32) if own < HEAD // 2 else None
            head = [high[first : first + own], low[first : first + own]]
            if pad is not None:
                head = [head[0], pad, head[1], pad]
            out_ref[block, 0:HEAD, :] = jnp.concatenate(head, axis=0).astype(BF16)


def partial_sums(cells, edges_t, edge_weight, own):
    anchors, zones, lanes = cells.shape
    edges = edge_weight.shape[0]
    rows = min(512, anchors)
    blocks = edges // own
    wide = max(rows, edges) * zones
    return pl.pallas_call(
        functools.partial(gather_kernel, own),
        grid=(anchors // rows,),
        in_specs=[
            pl.BlockSpec((edges_t.shape[0], rows), lambda i: (0, i)),
            pl.BlockSpec((edges, 1), lambda i: (0, 0)),
            pl.BlockSpec((rows, zones, lanes), lambda i: (i, 0, 0)),
        ],
        out_specs=[
            pl.BlockSpec((blocks, HEAD + own * zones, lanes), lambda i: (0, 0, 0)),
            pl.BlockSpec((1, rows), lambda i: (0, i)),
        ],
        out_shape=[
            jax.ShapeDtypeStruct((blocks, HEAD + own * zones, lanes), BF16),
            jax.ShapeDtypeStruct((1, anchors), F32),
        ],
        scratch_shapes=[
            pltpu.VMEM((wide, lanes), F32),
            pltpu.VMEM((zones // 2, edges, 2 * lanes), F32),
            pltpu.VMEM((edges, lanes), F32),
        ],
        compiler_params=pltpu.CompilerParams(vmem_limit_bytes=48 * 1024 * 1024),
        cost_estimate=pl.CostEstimate(
            flops=2 * anchors * edges * zones * lanes, bytes_accessed=2 * anchors * zones * lanes, transcendentals=0
        ),
    )(edges_t, edge_weight[:, None], cells)


def table_kernel(own, n_org, n_dst, parts_ref, weight_ref, mixing_ref, matrix_ref, out_ref):
    lanes = parts_ref.shape[2]
    zones = (parts_ref.shape[1] - HEAD) // own
    head = parts_ref[0, 0:HEAD, :].astype(F32)
    for j in range(1, n_org):
        head = head + parts_ref[j * n_dst, 0:HEAD, :].astype(F32)
    half = HEAD // 2
    counts = head[0:half] * COUNT_BASE + head[half:HEAD]
    for e in range(own):
        scale = weight_ref[e : e + 1, :] / counts[e : e + 1, :]
        pieces = []
        for k in range(n_dst):
            at = slice(HEAD + e * zones, HEAD + (e + 1) * zones)
            total = parts_ref[k, at, :].astype(F32)
            for j in range(1, n_org):
                total = total + parts_ref[j * n_dst + k, at, :].astype(F32)
            pieces.append(total * scale)
        totals = jnp.concatenate(pieces, axis=0).astype(BF16)
        mixed = jnp.dot(totals, mixing_ref[...], preferred_element_type=F32)
        high = mixed.astype(BF16)
        low = (mixed - high.astype(F32)).astype(BF16)
        both = jnp.dot(matrix_ref[...], jnp.concatenate([high, low], axis=1), preferred_element_type=F32)
        out_ref[e] = (both[:, 0:lanes] + both[:, lanes : 2 * lanes]).astype(BF16)


def table_rows(parts, weight_rows, mixing, matrix, own, n_org, n_dst):
    zones = matrix.shape[0]
    lanes = parts.shape[2]
    whole = pl.BlockSpec(memory_space=pltpu.VMEM)
    return pl.pallas_call(
        functools.partial(table_kernel, own, n_org, n_dst),
        in_specs=[whole] * 4,
        out_specs=whole,
        out_shape=jax.ShapeDtypeStruct((own, zones, lanes), BF16),
        compiler_params=pltpu.CompilerParams(vmem_limit_bytes=32 * 1024 * 1024),
        cost_estimate=pl.CostEstimate(flops=8 * own * zones * lanes * lanes, bytes_accessed=parts.size * 2, transcendentals=0),
    )(parts, weight_rows, mixing, matrix)


def spread_kernel(places_ref, root_ref, near_ref, far_ref, bias_ref, out_ref, table_ref, sems):
    step = pl.program_id(0)
    rows, zones, lanes = out_ref.shape
    half = near_ref.shape[0]

    @pl.when(step == 0)
    def _():
        first = pltpu.make_async_copy(near_ref, table_ref.at[pl.ds(0, half)], sems.at[0])
        second = pltpu.make_async_copy(far_ref, table_ref.at[pl.ds(half, half)], sems.at[1])
        first.start()
        second.start()
        first.wait()
        second.wait()

    bias = bias_ref[...]
    count = places_ref.shape[0]

    def one(i, carry):
        at = step * rows + i
        scale = root_ref[0, at]
        total = table_ref[places_ref[0, at]].astype(F32)
        for j in range(1, count):
            total = total + table_ref[places_ref[j, at]].astype(F32)
        out_ref[i] = jnp.maximum(total * scale + bias, 0.0).astype(BF16)
        return carry

    lax.fori_loop(0, rows, one, 0)


def spread(places, root, near, far, bias):
    anchors = places.shape[1]
    half, zones, lanes = near.shape
    rows = min(32, anchors)
    return pl.pallas_call(
        spread_kernel,
        grid=(anchors // rows,),
        in_specs=[
            pl.BlockSpec(memory_space=pltpu.SMEM),
            pl.BlockSpec(memory_space=pltpu.SMEM),
            pl.BlockSpec(memory_space=pl.ANY),
            pl.BlockSpec(memory_space=pl.ANY),
            pl.BlockSpec((1, lanes), lambda i: (0, 0)),
        ],
        out_specs=pl.BlockSpec((rows, zones, lanes), lambda i: (i, 0, 0)),
        out_shape=jax.ShapeDtypeStruct((anchors, zones, lanes), BF16),
        scratch_shapes=[pltpu.VMEM((2 * half, zones, lanes), BF16), pltpu.SemaphoreType.DMA((2,))],
        compiler_params=pltpu.CompilerParams(vmem_limit_bytes=32 * 1024 * 1024),
        cost_estimate=pl.CostEstimate(
            flops=8 * anchors * zones * lanes, bytes_accessed=2 * (anchors + 2 * half) * zones * lanes, transcendentals=0
        ),
    )(places, root, near, far, bias)


def shards(od_cells, anchor_edges, edge_weight, mixing, dst_edges, dst_weight, out_bias):
    n_org = lax.axis_size("org")
    n_core = lax.axis_size("core")
    n_dst = lax.axis_size("far") * n_core
    own = edge_weight.shape[0] // (n_org * n_dst)
    everyone = ("org", "far", "core")
    edges_t = anchor_edges.T
    parts, roots = partial_sums(od_cells, edges_t, edge_weight, own)
    parts = lax.all_to_all(parts, everyone, split_axis=0, concat_axis=0, tiled=True)
    own_weight = lax.dynamic_slice_in_dim(edge_weight, lax.axis_index(everyone) * own, own, 0)
    weight_rows = jnp.broadcast_to(own_weight[:, None], (own, parts.shape[2]))
    matrix = dest_operator(dst_edges, dst_weight)
    block = table_rows(parts, weight_rows, mixing, matrix, own, n_org, n_dst)
    near = lax.all_gather(block, ("org", "far"), axis=0, tiled=True)
    far = lax.ppermute(near, "core", [(c, (c + 1) % n_core) for c in range(n_core)])
    rows = anchor_edges.shape[0] // n_dst
    start = lax.axis_index(("far", "core")) * rows
    ids = lax.dynamic_slice_in_dim(edges_t, start, rows, 1)
    holder = ids // own
    places = (holder // n_core) * own + ids % own
    places = places + jnp.where(holder % n_core == lax.axis_index("core"), 0, near.shape[0])
    own_root = lax.dynamic_slice_in_dim(roots, start, rows, 1)
    return spread(places, own_root, near, far, out_bias[None, :])


def solution(mesh):
    n_org, n_dst = mesh.devices.shape
    fine = Mesh(mesh.devices.reshape(n_org, n_dst // 2, 2), ("org", "far", "core"))
    dst = ("far", "core")
    in_specs = (P("org", dst, None), P("org", None), P(), P(), P(), P(), P())
    out_specs = P(("org",) + dst, None, None)
    return jax.shard_map(shards, mesh=fine, in_specs=in_specs, out_specs=out_specs, check_vma=False)
```

```python
import functools

import jax
import jax.numpy as jnp
from jax import lax
from jax.experimental import pallas as pl
from jax.experimental.pallas import tpu as pltpu
from jax.sharding import Mesh, PartitionSpec as P

BF16 = jnp.bfloat16
F32 = jnp.float32
COUNT_BASE = 128.0
HEAD = 16


def corridor_table(edge_ids, edge_count):
    columns = jnp.arange(edge_count, dtype=jnp.int32)
    return jnp.sum((edge_ids[:, :, None] == columns[None, None, :]).astype(F32), axis=1)


def dest_operator(dst_edges, dst_weight):
    dst_member = corridor_table(dst_edges, dst_weight.shape[0])
    dst_degree = jnp.sum(dst_member * dst_weight[None, :], axis=1)
    edge_sizes = jnp.sum(dst_member, axis=0)
    left_factor = dst_member * lax.rsqrt(dst_degree)[:, None]
    right_factor = left_factor * (dst_weight / edge_sizes)[None, :]
    result = jnp.dot(right_factor, left_factor.T, precision=lax.Precision.HIGHEST)
    return result.astype(BF16)


def gather_kernel(own, group, pitch, edges_ref, weight_ref, cells_ref, out_ref, root_ref, wide_ref, total_ref, count_ref):
    step = pl.program_id(0)
    last = pl.num_programs(0) - 1
    rows, zones, lanes = cells_ref.shape
    edges = total_ref.shape[1]

    @pl.when(step == 0)
    def _():
        total_ref[...] = jnp.zeros_like(total_ref)
        count_ref[...] = jnp.zeros_like(count_ref)

    columns = lax.broadcasted_iota(jnp.int32, (edges, rows), 0)
    ids = edges_ref[...]
    member = columns == ids[0:1, :]
    for j in range(1, ids.shape[0]):
        member = jnp.logical_or(member, columns == ids[j : j + 1, :])
    upright = jnp.transpose(jnp.broadcast_to(weight_ref[...], (lanes, edges)))
    upright = jnp.concatenate([upright] * (rows // lanes), axis=1)
    root = lax.rsqrt(jnp.sum(jnp.where(member, upright, 0.0), axis=0, keepdims=True))
    root_ref[...] = root
    rounded = root.astype(BF16).astype(F32)
    weighted = jnp.where(member, rounded, 0.0).astype(BF16)
    hot = jnp.where(member, 1.0, 0.0).astype(BF16)
    count_ref[...] += jnp.dot(hot, jnp.ones((rows, lanes), BF16), preferred_element_type=F32)

    part = 32
    groups = zones // group
    pairs = group // 2

    def widen(g, first):
        piece = cells_ref[pl.ds(first, part), g * group : (g + 1) * group, :].astype(F32)
        for i in range(part):
            wide_ref[g, pl.ds(pl.multiple_of((first + i) * pitch, 8), group), :] = piece[i]

    def widen_first(i, carry):
        widen(0, i * part)
        return carry

    lax.fori_loop(0, rows // part, widen_first, 0)
    share = rows // part // pairs
    for g in range(groups):
        for pair in range(pairs):
            if g + 1 < groups:
                for i in range(share):
                    widen(g + 1, (pair * share + i) * part)
            left = wide_ref[g, pl.ds(2 * pair, rows, stride=pitch), :].astype(BF16)
            right = wide_ref[g, pl.ds(2 * pair + 1, rows, stride=pitch), :].astype(BF16)
            both = jnp.concatenate([left, right], axis=1)
            total_ref[g * pairs + pair] += jnp.dot(weighted, both, preferred_element_type=F32)

    @pl.when(step == last)
    def _():
        counts = count_ref[...]
        high = jnp.floor(counts * (1.0 / COUNT_BASE))
        low = counts - high * COUNT_BASE
        for block in range(edges // own):
            at = slice(block * own, (block + 1) * own)
            head = [high[at], low[at]]
            if own < HEAD // 2:
                pad = jnp.zeros((HEAD // 2 - own, lanes), F32)
                head = [head[0], pad, head[1], pad]
            out_ref[block, 0:HEAD, :] = jnp.concatenate(head, axis=0).astype(BF16)
            data = []
            for d in range(zones):
                data.append(total_ref[d // 2, at, (d % 2) * lanes : (d % 2 + 1) * lanes])
            out_ref[block, HEAD : HEAD + own * zones, :] = jnp.concatenate(data, axis=0).astype(BF16)


def partial_sums(cells, edges_t, edge_weight, own):
    anchors, zones, lanes = cells.shape
    edges = edge_weight.shape[0]
    rows = min(512, anchors)
    blocks = edges // own
    group = min(zones, 16)
    pitch = group + 8
    return pl.pallas_call(
        functools.partial(gather_kernel, own, group, pitch),
        grid=(anchors // rows,),
        in_specs=[
            pl.BlockSpec((edges_t.shape[0], rows), lambda i: (0, i)),
            pl.BlockSpec((1, edges), lambda i: (0, 0)),
            pl.BlockSpec((rows, zones, lanes), lambda i: (i, 0, 0)),
        ],
        out_specs=[
            pl.BlockSpec((blocks, HEAD + own * zones, lanes), lambda i: (0, 0, 0)),
            pl.BlockSpec((1, rows), lambda i: (0, i)),
        ],
        out_shape=[
            jax.ShapeDtypeStruct((blocks, HEAD + own * zones, lanes), BF16),
            jax.ShapeDtypeStruct((1, anchors), F32),
        ],
        scratch_shapes=[
            pltpu.VMEM((zones // group, rows * pitch, lanes), F32),
            pltpu.VMEM((zones // 2, edges, 2 * lanes), F32),
            pltpu.VMEM((edges, lanes), F32),
        ],
        compiler_params=pltpu.CompilerParams(vmem_limit_bytes=48 * 1024 * 1024),
        cost_estimate=pl.CostEstimate(
            flops=2 * anchors * edges * zones * lanes, bytes_accessed=2 * anchors * zones * lanes, transcendentals=0
        ),
    )(edges_t, edge_weight[None, :], cells)


def table_kernel(own, n_org, n_dst, parts_ref, weight_ref, mixing_ref, matrix_ref, keep_ref, give_ref, mixed_ref):
    lanes = parts_ref.shape[2]
    rows = parts_ref.shape[1] - HEAD
    zones = rows // own
    head = parts_ref[0, 0:HEAD, :].astype(F32)
    for j in range(1, n_org):
        head = head + parts_ref[j * n_dst, 0:HEAD, :].astype(F32)
    half = HEAD // 2
    counts = head[0:half] * COUNT_BASE + head[half:HEAD]
    scale = jnp.concatenate([weight_ref[...] / counts[0:own]] * zones, axis=0)
    for k in range(n_dst):
        total = parts_ref[k, HEAD:, :].astype(F32)
        for j in range(1, n_org):
            total = total + parts_ref[j * n_dst + k, HEAD:, :].astype(F32)
        totals = (total * scale).astype(BF16)
        mixed_ref[k * rows : (k + 1) * rows, :] = jnp.dot(totals, mixing_ref[...], preferred_element_type=F32)
    whole = n_dst * zones
    for e in range(own):
        mixed = mixed_ref[pl.ds(e, whole, stride=own), :] if own > 1 else mixed_ref[...]
        high = mixed.astype(BF16)
        low = (mixed - high.astype(F32)).astype(BF16)
        both = jnp.dot(matrix_ref[...], jnp.concatenate([high, low], axis=1), preferred_element_type=F32)
        result = (both[:, 0:lanes] + both[:, lanes : 2 * lanes]).astype(BF16)
        keep_ref[e] = result[0 : whole // 2]
        give_ref[e] = result[whole // 2 :]


def table_rows(parts, weight_rows, mixing, matrix, own, n_org, n_dst):
    zones = matrix.shape[0]
    lanes = parts.shape[2]
    whole = pl.BlockSpec(memory_space=pltpu.VMEM)
    half = jax.ShapeDtypeStruct((own, zones // 2, lanes), BF16)
    return pl.pallas_call(
        functools.partial(table_kernel, own, n_org, n_dst),
        in_specs=[whole] * 4,
        out_specs=[whole] * 2,
        out_shape=[half, half],
        scratch_shapes=[pltpu.VMEM((zones * own, lanes), F32)],
        compiler_params=pltpu.CompilerParams(vmem_limit_bytes=32 * 1024 * 1024),
        cost_estimate=pl.CostEstimate(flops=8 * own * zones * lanes * lanes, bytes_accessed=parts.size * 2, transcendentals=0),
    )(parts, weight_rows, mixing, matrix)


def spread_kernel(n_long, n_short, half_ref, long_at_ref, short_at_ref, root_ref, bias_ref, *refs):
    longs = refs[:n_long]
    shorts = refs[n_long : n_long + n_short]
    out_ref, long_ref, short_ref, sems = refs[-4:]
    step = pl.program_id(0)
    rows, zones, lanes = out_ref.shape

    @pl.when(step == 0)
    def _():
        copies = []
        for table, sources in ((long_ref, longs), (short_ref, shorts)):
            size = sources[0].shape[0]
            for i, source in enumerate(sources):
                copies.append(pltpu.make_async_copy(source, table.at[pl.ds(i * size, size)], sems.at[len(copies)]))
        for copy in copies:
            copy.start()
        for copy in copies:
            copy.wait()

    bias = bias_ref[...]
    count = long_at_ref.shape[0]
    tile = 16

    def one(i, carry):
        at = step * rows + i
        scale = root_ref[0, at]
        start = 0
        for table, places in ((long_ref, long_at_ref), (short_ref, short_at_ref)):
            spots = [places[j, at] for j in range(count)]
            for first in range(0, table.shape[1], tile):
                total = table[spots[0], first : first + tile, :].astype(F32)
                for spot in spots[1:]:
                    total = total + table[spot, first : first + tile, :].astype(F32)
                value = jnp.maximum(total * scale + bias, 0.0).astype(BF16)
                out_ref[i, start : start + tile, :] = value
                start += tile
        return carry

    lax.fori_loop(0, rows, one, 0, unroll=4)


def spread(half, long_at, short_at, root, bias, longs, shorts, before=None):
    anchors = long_at.shape[1]
    lanes = bias.shape[1]
    zones = longs[0].shape[1] + shorts[0].shape[1]
    rows = min(32, anchors)
    smem = pl.BlockSpec(memory_space=pltpu.SMEM)
    anywhere = pl.BlockSpec(memory_space=pl.ANY)
    tables = [pltpu.VMEM((len(pieces) * pieces[0].shape[0],) + pieces[0].shape[1:], BF16) for pieces in (longs, shorts)]
    operands = [half, long_at, short_at, root, bias] + longs + shorts
    specs = [smem, smem, smem, pl.BlockSpec((1, lanes), lambda i, h: (0, 0))] + [anywhere] * len(longs + shorts)
    aliases = {}
    if before is not None:
        aliases = {len(operands): 0}
        operands.append(before)
        specs.append(anywhere)
    return pl.pallas_call(
        functools.partial(spread_kernel, len(longs), len(shorts)),
        grid_spec=pltpu.PrefetchScalarGridSpec(
            num_scalar_prefetch=1,
            grid=(anchors // rows,),
            in_specs=specs,
            out_specs=pl.BlockSpec((rows, zones, lanes), lambda i, h: (i, h[0], 0)),
            scratch_shapes=tables + [pltpu.SemaphoreType.DMA((len(longs) + len(shorts),))],
        ),
        out_shape=jax.ShapeDtypeStruct((anchors, 2 * zones, lanes), BF16),
        input_output_aliases=aliases,
        compiler_params=pltpu.CompilerParams(vmem_limit_bytes=24 * 1024 * 1024),
        cost_estimate=pl.CostEstimate(
            flops=8 * anchors * zones * lanes, bytes_accessed=2 * anchors * zones * lanes, transcendentals=0
        ),
    )(*operands)


LINE = ("slow", "rest")
SQUARE = ("mid", "near", "core")


def shifted(x, amount):
    size = lax.axis_size(LINE)
    return lax.ppermute(x, LINE, [(i, (i + amount) % size) for i in range(size)])


def crossed(x, turn):
    pairs = []
    for device in range(8):
        core = device % 2
        pairs.append((device, device ^ (2 if core == turn else 4)))
    return lax.ppermute(x, SQUARE, pairs)


def swapped(x):
    return lax.ppermute(x, "core", [(0, 1), (1, 0)])


def gather_table(keep, give):
    size = lax.axis_size(LINE)
    block = jnp.concatenate([keep, swapped(give)], axis=0)
    split = block.shape[1] * 3 // 4
    long, short = block[:, :split], block[:, split:]
    line = [long] + [shifted(long, k) for k in range(1, size)]
    short = jnp.concatenate([short, crossed(short, 0)], axis=0)
    short = jnp.concatenate([short, crossed(short, 1)], axis=0)
    long = jnp.concatenate(line, axis=0)
    first = crossed(long, 0)
    second = crossed(long, 1)
    both = crossed(first, 1)
    shorts = [short] + [shifted(short, k) for k in range(1, size)]
    return [long, first, second, both], shorts


def places_of(ids, core, own):
    rest, size = lax.axis_size("rest"), lax.axis_size(LINE)
    owner = ids // own
    slot = jnp.where(owner % 2 == core, 0, own) + ids % own
    near = jnp.bitwise_xor(owner // 2 % 2, lax.axis_index("near"))
    mid = jnp.bitwise_xor(owner // (4 * rest) % 2, lax.axis_index("mid"))
    line = owner // (8 * rest) * rest + owner // 4 % rest
    line = lax.rem(lax.axis_index(LINE) - line + size, size)
    square = jnp.where(core == 0, 2 * mid + near, 2 * near + mid)
    return (square * size + line) * (2 * own) + slot, (line * 4 + square) * (2 * own) + slot


def shards(od_cells, anchor_edges, edge_weight, mixing, dst_edges, dst_weight, out_bias):
    n_org = lax.axis_size("slow") * lax.axis_size("mid")
    n_dst = lax.axis_size("rest") * lax.axis_size("near") * lax.axis_size("core")
    own = edge_weight.shape[0] // (n_org * n_dst)
    everyone = ("slow", "mid", "rest", "near", "core")
    core = lax.axis_index("core")
    edges_t = anchor_edges.T
    parts, roots = partial_sums(od_cells, edges_t, edge_weight, own)
    parts = lax.all_to_all(parts, everyone, split_axis=0, concat_axis=0, tiled=True)
    own_weight = lax.dynamic_slice_in_dim(edge_weight, lax.axis_index(everyone) * own, own, 0)
    weight_rows = jnp.broadcast_to(own_weight[:, None], (own, parts.shape[2]))
    matrix = dest_operator(dst_edges, dst_weight)
    half = matrix.shape[0] // 2
    matrix = jnp.where(core == 0, matrix, jnp.concatenate([matrix[half:], matrix[:half]], axis=0))
    keep, give = table_rows(parts, weight_rows, mixing, matrix, own, n_org, n_dst)
    longs, shorts = gather_table(keep, give)
    rows = anchor_edges.shape[0] // n_dst
    start = lax.axis_index(("rest", "near", "core")) * rows
    ids = lax.dynamic_slice_in_dim(edges_t, start, rows, 1)
    own_root = lax.dynamic_slice_in_dim(roots, start, rows, 1)
    bias = out_bias[None, :]
    other = 1 - core
    result = spread(core[None], *places_of(ids, core, own), own_root, bias, longs, shorts)
    longs, shorts = [swapped(x) for x in longs], [swapped(x) for x in shorts]
    return spread(other[None], *places_of(ids, other, own), own_root, bias, longs, shorts, result)


def solution(mesh):
    n_org, n_dst = mesh.devices.shape
    fine = Mesh(mesh.devices.reshape(n_org // 2, 2, n_dst // 4, 2, 2), ("slow", "mid", "rest", "near", "core"))
    org, dst = ("slow", "mid"), ("rest", "near", "core")
    in_specs = (P(org, dst, None), P(org, None), P(), P(), P(), P(), P())
    out_specs = P(org + dst, None, None)
    return jax.shard_map(shards, mesh=fine, in_specs=in_specs, out_specs=out_specs, check_vma=False)
```

```python
import functools

import jax
import jax.numpy as jnp
from jax import lax
from jax.experimental import pallas as pl
from jax.experimental.pallas import tpu as pltpu
from jax.sharding import Mesh, PartitionSpec as P

BF16 = jnp.bfloat16
F32 = jnp.float32
COUNT_BASE = 128.0
HEAD = 16


def corridor_table(edge_ids, edge_count):
    columns = jnp.arange(edge_count, dtype=jnp.int32)
    return jnp.sum((edge_ids[:, :, None] == columns[None, None, :]).astype(F32), axis=1)


def dest_operator(dst_edges, dst_weight):
    dst_member = corridor_table(dst_edges, dst_weight.shape[0])
    dst_degree = jnp.sum(dst_member * dst_weight[None, :], axis=1)
    edge_sizes = jnp.sum(dst_member, axis=0)
    left_factor = dst_member * lax.rsqrt(dst_degree)[:, None]
    right_factor = left_factor * (dst_weight / edge_sizes)[None, :]
    result = jnp.dot(right_factor, left_factor.T, precision=lax.Precision.HIGHEST)
    return result.astype(BF16)


def gather_kernel(own, group, pitch, edges_ref, weight_ref, cells_ref, out_ref, root_ref, wide_ref, total_ref, count_ref):
    step = pl.program_id(0)
    last = pl.num_programs(0) - 1
    rows, zones, lanes = cells_ref.shape
    edges = total_ref.shape[1]

    @pl.when(step == 0)
    def _():
        total_ref[...] = jnp.zeros_like(total_ref)
        count_ref[...] = jnp.zeros_like(count_ref)

    columns = lax.broadcasted_iota(jnp.int32, (edges, rows), 0)
    ids = edges_ref[...]
    member = columns == ids[0:1, :]
    for j in range(1, ids.shape[0]):
        member = jnp.logical_or(member, columns == ids[j : j + 1, :])
    upright = jnp.transpose(jnp.broadcast_to(weight_ref[...], (lanes, edges)))
    upright = jnp.concatenate([upright] * (rows // lanes), axis=1)
    root = lax.rsqrt(jnp.sum(jnp.where(member, upright, 0.0), axis=0, keepdims=True))
    root_ref[...] = root
    rounded = root.astype(BF16).astype(F32)
    weighted = jnp.where(member, rounded, 0.0).astype(BF16)
    hot = jnp.where(member, 1.0, 0.0).astype(BF16)
    count_ref[...] += jnp.dot(hot, jnp.ones((rows, lanes), BF16), preferred_element_type=F32)

    part = 32
    groups = zones // group
    pairs = group // 2

    def widen(g, first):
        piece = cells_ref[pl.ds(first, part), g * group : (g + 1) * group, :].astype(F32)
        for i in range(part):
            wide_ref[g, pl.ds(pl.multiple_of((first + i) * pitch, 8), group), :] = piece[i]

    def widen_first(i, carry):
        widen(0, i * part)
        return carry

    lax.fori_loop(0, rows // part, widen_first, 0)
    share = rows // part // pairs
    for g in range(groups):
        for pair in range(pairs):
            if g + 1 < groups:
                for i in range(share):
                    widen(g + 1, (pair * share + i) * part)
            left = wide_ref[g, pl.ds(2 * pair, rows, stride=pitch), :].astype(BF16)
            right = wide_ref[g, pl.ds(2 * pair + 1, rows, stride=pitch), :].astype(BF16)
            both = jnp.concatenate([left, right], axis=1)
            total_ref[g * pairs + pair] += jnp.dot(weighted, both, preferred_element_type=F32)

    @pl.when(step == last)
    def _():
        counts = count_ref[...]
        high = jnp.floor(counts * (1.0 / COUNT_BASE))
        low = counts - high * COUNT_BASE
        for block in range(edges // own):
            at = slice(block * own, (block + 1) * own)
            head = [high[at], low[at]]
            if own < HEAD // 2:
                pad = jnp.zeros((HEAD // 2 - own, lanes), F32)
                head = [head[0], pad, head[1], pad]
            out_ref[block, 0:HEAD, :] = jnp.concatenate(head, axis=0).astype(BF16)
            data = []
            for d in range(zones):
                data.append(total_ref[d // 2, at, (d % 2) * lanes : (d % 2 + 1) * lanes])
            out_ref[block, HEAD : HEAD + own * zones, :] = jnp.concatenate(data, axis=0).astype(BF16)


def partial_sums(cells, edges_t, edge_weight, own):
    anchors, zones, lanes = cells.shape
    edges = edge_weight.shape[0]
    rows = min(512, anchors)
    blocks = edges // own
    group = min(zones, 16)
    pitch = group + 8
    return pl.pallas_call(
        functools.partial(gather_kernel, own, group, pitch),
        grid=(anchors // rows,),
        in_specs=[
            pl.BlockSpec((edges_t.shape[0], rows), lambda i: (0, i)),
            pl.BlockSpec((1, edges), lambda i: (0, 0)),
            pl.BlockSpec((rows, zones, lanes), lambda i: (i, 0, 0)),
        ],
        out_specs=[
            pl.BlockSpec((blocks, HEAD + own * zones, lanes), lambda i: (0, 0, 0)),
            pl.BlockSpec((1, rows), lambda i: (0, i)),
        ],
        out_shape=[
            jax.ShapeDtypeStruct((blocks, HEAD + own * zones, lanes), BF16),
            jax.ShapeDtypeStruct((1, anchors), F32),
        ],
        scratch_shapes=[
            pltpu.VMEM((zones // group, rows * pitch, lanes), F32),
            pltpu.VMEM((zones // 2, edges, 2 * lanes), F32),
            pltpu.VMEM((edges, lanes), F32),
        ],
        compiler_params=pltpu.CompilerParams(vmem_limit_bytes=48 * 1024 * 1024),
        cost_estimate=pl.CostEstimate(
            flops=2 * anchors * edges * zones * lanes, bytes_accessed=2 * anchors * zones * lanes, transcendentals=0
        ),
    )(edges_t, edge_weight[None, :], cells)


def table_kernel(own, n_org, n_dst, parts_ref, weight_ref, mixing_ref, matrix_ref, keep_ref, give_ref, mixed_ref):
    lanes = parts_ref.shape[2]
    rows = parts_ref.shape[1] - HEAD
    zones = rows // own
    head = parts_ref[0, 0:HEAD, :].astype(F32)
    for j in range(1, n_org):
        head = head + parts_ref[j * n_dst, 0:HEAD, :].astype(F32)
    half = HEAD // 2
    counts = head[0:half] * COUNT_BASE + head[half:HEAD]
    scale = jnp.concatenate([weight_ref[...] / counts[0:own]] * zones, axis=0)
    for k in range(n_dst):
        total = parts_ref[k, HEAD:, :].astype(F32)
        for j in range(1, n_org):
            total = total + parts_ref[j * n_dst + k, HEAD:, :].astype(F32)
        totals = (total * scale).astype(BF16)
        mixed_ref[k * rows : (k + 1) * rows, :] = jnp.dot(totals, mixing_ref[...], preferred_element_type=F32)
    whole = n_dst * zones
    for e in range(own):
        mixed = mixed_ref[pl.ds(e, whole, stride=own), :] if own > 1 else mixed_ref[...]
        high = mixed.astype(BF16)
        low = (mixed - high.astype(F32)).astype(BF16)
        both = jnp.dot(matrix_ref[...], jnp.concatenate([high, low], axis=1), preferred_element_type=F32)
        result = (both[:, 0:lanes] + both[:, lanes : 2 * lanes]).astype(BF16)
        keep_ref[e] = result[0 : whole // 2]
        give_ref[e] = result[whole // 2 :]


def table_rows(parts, weight_rows, mixing, matrix, own, n_org, n_dst):
    zones = matrix.shape[0]
    lanes = parts.shape[2]
    whole = pl.BlockSpec(memory_space=pltpu.VMEM)
    half = jax.ShapeDtypeStruct((own, zones // 2, lanes), BF16)
    return pl.pallas_call(
        functools.partial(table_kernel, own, n_org, n_dst),
        in_specs=[whole] * 4,
        out_specs=[whole] * 2,
        out_shape=[half, half],
        scratch_shapes=[pltpu.VMEM((zones * own, lanes), F32)],
        compiler_params=pltpu.CompilerParams(vmem_limit_bytes=32 * 1024 * 1024),
        cost_estimate=pl.CostEstimate(flops=8 * own * zones * lanes * lanes, bytes_accessed=parts.size * 2, transcendentals=0),
    )(parts, weight_rows, mixing, matrix)


def spread_kernel(n_long, n_short, half_ref, long_at_ref, short_at_ref, root_ref, bias_ref, *refs):
    longs = refs[:n_long]
    shorts = refs[n_long : n_long + n_short]
    out_ref, long_ref, short_ref, sems = refs[-4:]
    step = pl.program_id(0)
    rows, zones, lanes = out_ref.shape

    @pl.when(step == 0)
    def _():
        copies = []
        for table, sources in ((long_ref, longs), (short_ref, shorts)):
            size = sources[0].shape[0]
            for i, source in enumerate(sources):
                copies.append(pltpu.make_async_copy(source, table.at[pl.ds(i * size, size)], sems.at[len(copies)]))
        for copy in copies:
            copy.start()
        for copy in copies:
            copy.wait()

    bias = bias_ref[...]
    count = long_at_ref.shape[0]
    tile = 16

    def one(i, carry):
        at = step * rows + i
        scale = root_ref[0, at]
        start = 0
        for table, places in ((long_ref, long_at_ref), (short_ref, short_at_ref)):
            spots = [places[j, at] for j in range(count)]
            for first in range(0, table.shape[1], tile):
                pieces = [table[spot, first : first + tile, :] for spot in spots]
                pieces = [(a + b).astype(F32) for a, b in zip(pieces[0::2], pieces[1::2])]
                total = sum(pieces[1:], pieces[0])
                value = jnp.maximum((total * scale + bias).astype(BF16), BF16(0.0))
                out_ref[i, start : start + tile, :] = value
                start += tile
        return carry

    lax.fori_loop(0, rows, one, 0, unroll=4)


def spread(half, long_at, short_at, root, bias, longs, shorts, before=None):
    anchors = long_at.shape[1]
    lanes = bias.shape[1]
    zones = longs[0].shape[1] + shorts[0].shape[1]
    rows = min(32, anchors)
    smem = pl.BlockSpec(memory_space=pltpu.SMEM)
    anywhere = pl.BlockSpec(memory_space=pltpu.HBM)
    tables = [pltpu.VMEM((len(pieces) * pieces[0].shape[0],) + pieces[0].shape[1:], BF16) for pieces in (longs, shorts)]
    operands = [half, long_at, short_at, root, bias] + longs + shorts
    specs = [smem, smem, smem, pl.BlockSpec((1, lanes), lambda i, h: (0, 0))] + [anywhere] * len(longs + shorts)
    aliases = {}
    if before is not None:
        aliases = {len(operands): 0}
        operands.append(before)
        specs.append(anywhere)
    return pl.pallas_call(
        functools.partial(spread_kernel, len(longs), len(shorts)),
        grid_spec=pltpu.PrefetchScalarGridSpec(
            num_scalar_prefetch=1,
            grid=(anchors // rows,),
            in_specs=specs,
            out_specs=pl.BlockSpec((rows, zones, lanes), lambda i, h: (i, h[0], 0)),
            scratch_shapes=tables + [pltpu.SemaphoreType.DMA((len(longs) + len(shorts),))],
        ),
        out_shape=jax.ShapeDtypeStruct((anchors, 2 * zones, lanes), BF16),
        input_output_aliases=aliases,
        compiler_params=pltpu.CompilerParams(vmem_limit_bytes=24 * 1024 * 1024),
        cost_estimate=pl.CostEstimate(
            flops=4096 * anchors * zones * lanes, bytes_accessed=4 * anchors * zones * lanes, transcendentals=0
        ),
    )(*operands)


LINE = ("slow", "rest")
SQUARE = ("mid", "near", "core")


def shifted(x, amount):
    size = lax.axis_size(LINE)
    return lax.ppermute(x, LINE, [(i, (i + amount) % size) for i in range(size)])


def crossed(x, turn):
    pairs = []
    for device in range(8):
        core = device % 2
        pairs.append((device, device ^ (2 if core == turn else 4)))
    return lax.ppermute(x, SQUARE, pairs)


def swapped(x):
    return lax.ppermute(x, "core", [(0, 1), (1, 0)])


def gather_table(keep, give):
    size = lax.axis_size(LINE)
    block = jnp.concatenate([keep, swapped(give)], axis=0)
    split = block.shape[1] * 3 // 4
    long, short = block[:, :split], block[:, split:]
    line = [long] + [shifted(long, k) for k in range(1, size - 1)]
    short = jnp.concatenate([short, crossed(short, 0)], axis=0)
    short, long = lax.optimization_barrier((short, long))
    line.append(shifted(long, size - 1))
    short = jnp.concatenate([short, crossed(short, 1)], axis=0)
    long = jnp.concatenate(line, axis=0)
    short, long = lax.optimization_barrier((short, long))
    first = crossed(long, 0)
    second = crossed(long, 1)
    both = crossed(first, 1)
    shorts = [short] + [shifted(short, k) for k in range(1, size)]
    return [long, first, second, both], shorts


def places_of(ids, core, own):
    rest, size = lax.axis_size("rest"), lax.axis_size(LINE)
    owner = ids // own
    slot = jnp.where(owner % 2 == core, 0, own) + ids % own
    near = jnp.bitwise_xor(owner // 2 % 2, lax.axis_index("near"))
    mid = jnp.bitwise_xor(owner // (4 * rest) % 2, lax.axis_index("mid"))
    line = owner // (8 * rest) * rest + owner // 4 % rest
    line = lax.rem(lax.axis_index(LINE) - line + size, size)
    square = jnp.where(core == 0, 2 * mid + near, 2 * near + mid)
    return (square * size + line) * (2 * own) + slot, (line * 4 + square) * (2 * own) + slot


def shards(od_cells, anchor_edges, edge_weight, mixing, dst_edges, dst_weight, out_bias):
    n_org = lax.axis_size("slow") * lax.axis_size("mid")
    n_dst = lax.axis_size("rest") * lax.axis_size("near") * lax.axis_size("core")
    own = edge_weight.shape[0] // (n_org * n_dst)
    everyone = ("slow", "mid", "rest", "near", "core")
    core = lax.axis_index("core")
    edges_t = anchor_edges.T
    parts, roots = partial_sums(od_cells, edges_t, edge_weight, own)
    parts = lax.all_to_all(parts, everyone, split_axis=0, concat_axis=0, tiled=True)
    own_weight = lax.dynamic_slice_in_dim(edge_weight, lax.axis_index(everyone) * own, own, 0)
    weight_rows = jnp.broadcast_to(own_weight[:, None], (own, parts.shape[2]))
    matrix = dest_operator(dst_edges, dst_weight)
    half = matrix.shape[0] // 2
    matrix = jnp.where(core == 0, matrix, jnp.concatenate([matrix[half:], matrix[:half]], axis=0))
    keep, give = table_rows(parts, weight_rows, mixing, matrix, own, n_org, n_dst)
    longs, shorts = gather_table(keep, give)
    rows = anchor_edges.shape[0] // n_dst
    start = lax.axis_index(("rest", "near", "core")) * rows
    ids = lax.dynamic_slice_in_dim(edges_t, start, rows, 1)
    own_root = lax.dynamic_slice_in_dim(roots, start, rows, 1)
    bias = out_bias[None, :]
    other = 1 - core
    result = spread(core[None], *places_of(ids, core, own), own_root, bias, longs, shorts)
    longs, shorts = [swapped(x) for x in longs], [swapped(x) for x in shorts]
    return spread(other[None], *places_of(ids, other, own), own_root, bias, longs, shorts, result)


def solution(mesh):
    n_org, n_dst = mesh.devices.shape
    fine = Mesh(mesh.devices.reshape(n_org // 2, 2, n_dst // 4, 2, 2), ("slow", "mid", "rest", "near", "core"))
    org, dst = ("slow", "mid"), ("rest", "near", "core")
    in_specs = (P(org, dst, None), P(org, None), P(), P(), P(), P(), P())
    out_specs = P(org + dst, None, None)
    return jax.shard_map(shards, mesh=fine, in_specs=in_specs, out_specs=out_specs, check_vma=False)
```

```python
import functools

import jax
import jax.numpy as jnp
from jax import lax
from jax.experimental import pallas as pl
from jax.experimental.pallas import tpu as pltpu
from jax.sharding import Mesh, PartitionSpec as P

BF16 = jnp.bfloat16
F32 = jnp.float32
COUNT_BASE = 128.0
HEAD = 16


def corridor_table(edge_ids, edge_count):
    columns = jnp.arange(edge_count, dtype=jnp.int32)
    return jnp.sum((edge_ids[:, :, None] == columns[None, None, :]).astype(F32), axis=1)


def dest_operator(dst_edges, dst_weight):
    dst_member = corridor_table(dst_edges, dst_weight.shape[0])
    dst_degree = jnp.sum(dst_member * dst_weight[None, :], axis=1)
    edge_sizes = jnp.sum(dst_member, axis=0)
    left_factor = dst_member * lax.rsqrt(dst_degree)[:, None]
    right_factor = left_factor * (dst_weight / edge_sizes)[None, :]
    result = jnp.dot(right_factor, left_factor.T, precision=lax.Precision.HIGHEST)
    return result.astype(BF16)


def gather_kernel(own, group, pitch, edges_ref, weight_ref, cells_ref, out_ref, root_ref, total_ref, count_ref, *wide_refs):
    step = pl.program_id(0)
    last = pl.num_programs(0) - 1
    rows, zones, lanes = cells_ref.shape
    edges = total_ref.shape[1]

    @pl.when(step == 0)
    def _():
        total_ref[...] = jnp.zeros_like(total_ref)
        count_ref[...] = jnp.zeros_like(count_ref)

    columns = lax.broadcasted_iota(jnp.int32, (edges, rows), 0)
    ids = edges_ref[...]
    member = columns == ids[0:1, :]
    for j in range(1, ids.shape[0]):
        member = jnp.logical_or(member, columns == ids[j : j + 1, :])
    upright = jnp.transpose(jnp.broadcast_to(weight_ref[...], (lanes, edges)))
    upright = jnp.concatenate([upright] * (rows // lanes), axis=1)
    root = lax.rsqrt(jnp.sum(jnp.where(member, upright, 0.0), axis=0, keepdims=True))
    root_ref[...] = root
    rounded = root.astype(BF16).astype(F32)
    weighted = jnp.where(member, rounded, 0.0).astype(BF16)
    hot = jnp.where(member, 1.0, 0.0).astype(BF16)
    count_ref[...] += jnp.dot(hot, jnp.ones((rows, lanes), BF16), preferred_element_type=F32)

    part = 32
    groups = zones // group
    pairs = group // 2

    def load(g, first):
        return cells_ref[pl.ds(first, part), g * group : (g + 1) * group, :].astype(F32)

    def store(g, first, piece):
        for i in range(part):
            wide_refs[g][pl.ds(pl.multiple_of((first + i) * pitch, 8), group), :] = piece[i]

    def widen_first(i, carry):
        store(0, i * part, load(0, i * part))
        return carry

    lax.fori_loop(0, rows // part, widen_first, 0)
    share = rows // part // pairs
    for g in range(groups):
        for pair in range(pairs):
            left = wide_refs[g][pl.ds(2 * pair, rows, stride=pitch), :].astype(BF16)
            right = wide_refs[g][pl.ds(2 * pair + 1, rows, stride=pitch), :].astype(BF16)
            both = jnp.concatenate([left, right], axis=1)
            if g + 1 < groups:
                for i in range(share):
                    first = (pair * share + i) * part
                    store(g + 1, first, load(g + 1, first))
            total_ref[g * pairs + pair] += jnp.dot(weighted, both, preferred_element_type=F32)

    @pl.when(step == last)
    def _():
        counts = count_ref[...]
        high = jnp.floor(counts * (1.0 / COUNT_BASE))
        low = counts - high * COUNT_BASE
        for block in range(edges // own):
            at = slice(block * own, (block + 1) * own)
            head = [high[at], low[at]]
            if own < HEAD // 2:
                pad = jnp.zeros((HEAD // 2 - own, lanes), F32)
                head = [head[0], pad, head[1], pad]
            out_ref[block, 0:HEAD, :] = jnp.concatenate(head, axis=0).astype(BF16)
            data = []
            for d in range(zones):
                data.append(total_ref[d // 2, at, (d % 2) * lanes : (d % 2 + 1) * lanes])
            out_ref[block, HEAD : HEAD + own * zones, :] = jnp.concatenate(data, axis=0).astype(BF16)


def partial_sums(cells, edges_t, edge_weight, own):
    anchors, zones, lanes = cells.shape
    edges = edge_weight.shape[0]
    rows = min(512, anchors)
    blocks = edges // own
    group = min(zones, 16)
    pitch = group + 8
    return pl.pallas_call(
        functools.partial(gather_kernel, own, group, pitch),
        grid=(anchors // rows,),
        in_specs=[
            pl.BlockSpec((edges_t.shape[0], rows), lambda i: (0, i)),
            pl.BlockSpec((1, edges), lambda i: (0, 0)),
            pl.BlockSpec((rows, zones, lanes), lambda i: (i, 0, 0)),
        ],
        out_specs=[
            pl.BlockSpec((blocks, HEAD + own * zones, lanes), lambda i: (0, 0, 0)),
            pl.BlockSpec((1, rows), lambda i: (0, i)),
        ],
        out_shape=[
            jax.ShapeDtypeStruct((blocks, HEAD + own * zones, lanes), BF16),
            jax.ShapeDtypeStruct((1, anchors), F32),
        ],
        scratch_shapes=[
            pltpu.VMEM((zones // 2, edges, 2 * lanes), F32),
            pltpu.VMEM((edges, lanes), F32),
        ]
        + [pltpu.VMEM((rows * pitch, lanes), F32)] * (zones // group),
        compiler_params=pltpu.CompilerParams(vmem_limit_bytes=48 * 1024 * 1024),
        cost_estimate=pl.CostEstimate(
            flops=2 * anchors * edges * zones * lanes, bytes_accessed=2 * anchors * zones * lanes, transcendentals=0
        ),
    )(edges_t, edge_weight[None, :], cells)


def table_kernel(own, n_org, n_dst, parts_ref, weight_ref, mixing_ref, matrix_ref, keep_ref, give_ref, mixed_ref):
    lanes = parts_ref.shape[2]
    rows = parts_ref.shape[1] - HEAD
    zones = rows // own
    head = parts_ref[0, 0:HEAD, :].astype(F32)
    for j in range(1, n_org):
        head = head + parts_ref[j * n_dst, 0:HEAD, :].astype(F32)
    half = HEAD // 2
    counts = head[0:half] * COUNT_BASE + head[half:HEAD]
    scale = jnp.concatenate([weight_ref[...] / counts[0:own]] * zones, axis=0)
    for k in range(n_dst):
        total = parts_ref[k, HEAD:, :].astype(F32)
        for j in range(1, n_org):
            total = total + parts_ref[j * n_dst + k, HEAD:, :].astype(F32)
        totals = (total * scale).astype(BF16)
        mixed_ref[k * rows : (k + 1) * rows, :] = jnp.dot(totals, mixing_ref[...], preferred_element_type=F32)
    whole = n_dst * zones
    for e in range(own):
        mixed = mixed_ref[pl.ds(e, whole, stride=own), :] if own > 1 else mixed_ref[...]
        high = mixed.astype(BF16)
        low = (mixed - high.astype(F32)).astype(BF16)
        both = jnp.dot(matrix_ref[...], jnp.concatenate([high, low], axis=1), preferred_element_type=F32)
        result = (both[:, 0:lanes] + both[:, lanes : 2 * lanes]).astype(BF16)
        keep_ref[e] = result[0 : whole // 2]
        give_ref[e] = result[whole // 2 :]


def table_rows(parts, weight_rows, mixing, matrix, own, n_org, n_dst):
    zones = matrix.shape[0]
    lanes = parts.shape[2]
    whole = pl.BlockSpec(memory_space=pltpu.VMEM)
    half = jax.ShapeDtypeStruct((own, zones // 2, lanes), BF16)
    return pl.pallas_call(
        functools.partial(table_kernel, own, n_org, n_dst),
        in_specs=[whole] * 4,
        out_specs=[whole] * 2,
        out_shape=[half, half],
        scratch_shapes=[pltpu.VMEM((zones * own, lanes), F32)],
        compiler_params=pltpu.CompilerParams(vmem_limit_bytes=32 * 1024 * 1024),
        cost_estimate=pl.CostEstimate(flops=8 * own * zones * lanes * lanes, bytes_accessed=parts.size * 2, transcendentals=0),
    )(parts, weight_rows, mixing, matrix)


def spread_kernel(n_long, n_short, half_ref, long_at_ref, short_at_ref, root_ref, bias_ref, *refs):
    longs = refs[:n_long]
    shorts = refs[n_long : n_long + n_short]
    out_ref, long_ref, short_ref, sems = refs[-4:]
    step = pl.program_id(0)
    rows, zones, lanes = out_ref.shape

    @pl.when(step == 0)
    def _():
        copies = []
        for table, sources in ((long_ref, longs), (short_ref, shorts)):
            size = sources[0].shape[0]
            for i, source in enumerate(sources):
                copies.append(pltpu.make_async_copy(source, table.at[pl.ds(i * size, size)], sems.at[len(copies)]))
        for copy in copies:
            copy.start()
        for copy in copies:
            copy.wait()

    bias = bias_ref[...]
    count = long_at_ref.shape[0]
    tile = 16
    batch = 4

    def several(group, carry):
        values = []
        for i in range(batch):
            at = step * rows + group * batch + i
            scale = root_ref[0, at]
            for table, places in ((long_ref, long_at_ref), (short_ref, short_at_ref)):
                spots = [places[j, at] for j in range(count)]
                for first in range(0, table.shape[1], tile):
                    pieces = [table[spot, first : first + tile, :] for spot in spots]
                    pieces = [(a + b).astype(F32) for a, b in zip(pieces[0::2], pieces[1::2])]
                    total = sum(pieces[1:], pieces[0])
                    values.append(jnp.maximum((total * scale + bias).astype(BF16), BF16(0.0)))
        tiles = zones // tile
        for n, value in enumerate(values):
            start = n % tiles * tile
            out_ref[group * batch + n // tiles, start : start + tile, :] = value
        return carry

    lax.fori_loop(0, rows // batch, several, 0)


def spread(half, long_at, short_at, root, bias, longs, shorts, before=None):
    anchors = long_at.shape[1]
    lanes = bias.shape[1]
    zones = longs[0].shape[1] + shorts[0].shape[1]
    rows = min(32, anchors)
    smem = pl.BlockSpec(memory_space=pltpu.SMEM)
    anywhere = pl.BlockSpec(memory_space=pltpu.HBM)
    tables = [pltpu.VMEM((len(pieces) * pieces[0].shape[0],) + pieces[0].shape[1:], BF16) for pieces in (longs, shorts)]
    operands = [half, long_at, short_at, root, bias] + longs + shorts
    specs = [smem, smem, smem, pl.BlockSpec((1, lanes), lambda i, h: (0, 0))] + [anywhere] * len(longs + shorts)
    aliases = {}
    if before is not None:
        aliases = {len(operands): 0}
        operands.append(before)
        specs.append(anywhere)
    return pl.pallas_call(
        functools.partial(spread_kernel, len(longs), len(shorts)),
        grid_spec=pltpu.PrefetchScalarGridSpec(
            num_scalar_prefetch=1,
            grid=(anchors // rows,),
            in_specs=specs,
            out_specs=pl.BlockSpec((rows, zones, lanes), lambda i, h: (i, h[0], 0)),
            scratch_shapes=tables + [pltpu.SemaphoreType.DMA((len(longs) + len(shorts),))],
        ),
        out_shape=jax.ShapeDtypeStruct((anchors, 2 * zones, lanes), BF16),
        input_output_aliases=aliases,
        compiler_params=pltpu.CompilerParams(vmem_limit_bytes=24 * 1024 * 1024),
        cost_estimate=pl.CostEstimate(
            flops=4096 * anchors * zones * lanes, bytes_accessed=4 * anchors * zones * lanes, transcendentals=0
        ),
    )(*operands)


LINE = ("slow", "rest")
SQUARE = ("mid", "near", "core")


def shifted(x, amount):
    size = lax.axis_size(LINE)
    return lax.ppermute(x, LINE, [(i, (i + amount) % size) for i in range(size)])


def crossed(x, turn):
    pairs = []
    for device in range(8):
        core = device % 2
        pairs.append((device, device ^ (2 if core == turn else 4)))
    return lax.ppermute(x, SQUARE, pairs)


def swapped(x):
    return lax.ppermute(x, "core", [(0, 1), (1, 0)])


def gather_table(keep, give):
    size = lax.axis_size(LINE)
    block = jnp.concatenate([keep, swapped(give)], axis=0)
    split = block.shape[1] * 3 // 4
    long, short = block[:, :split], block[:, split:]
    line = [long] + [shifted(long, k) for k in range(1, size - 1)]
    short = jnp.concatenate([short, crossed(short, 0)], axis=0)
    short, long = lax.optimization_barrier((short, long))
    line.append(shifted(long, size - 1))
    short = jnp.concatenate([short, crossed(short, 1)], axis=0)
    long = jnp.concatenate(line, axis=0)
    short, long = lax.optimization_barrier((short, long))
    first = crossed(long, 0)
    second = crossed(long, 1)
    shorts = [short] + [shifted(short, k) for k in range(1, size)]
    first, *shorts[1:-1] = lax.optimization_barrier((first, *shorts[1:-1]))
    both = crossed(first, 1)
    return [long, first, second, both], shorts


def places_of(ids, core, own):
    rest, size = lax.axis_size("rest"), lax.axis_size(LINE)
    owner = ids // own
    slot = jnp.where(owner % 2 == core, 0, own) + ids % own
    near = jnp.bitwise_xor(owner // 2 % 2, lax.axis_index("near"))
    mid = jnp.bitwise_xor(owner // (4 * rest) % 2, lax.axis_index("mid"))
    line = owner // (8 * rest) * rest + owner // 4 % rest
    line = lax.rem(lax.axis_index(LINE) - line + size, size)
    square = jnp.where(core == 0, 2 * mid + near, 2 * near + mid)
    return (square * size + line) * (2 * own) + slot, (line * 4 + square) * (2 * own) + slot


def shards(od_cells, anchor_edges, edge_weight, mixing, dst_edges, dst_weight, out_bias):
    n_org = lax.axis_size("slow") * lax.axis_size("mid")
    n_dst = lax.axis_size("rest") * lax.axis_size("near") * lax.axis_size("core")
    own = edge_weight.shape[0] // (n_org * n_dst)
    everyone = ("slow", "mid", "rest", "near", "core")
    core = lax.axis_index("core")
    edges_t = anchor_edges.T
    parts, roots = partial_sums(od_cells, edges_t, edge_weight, own)
    parts = lax.all_to_all(parts, everyone, split_axis=0, concat_axis=0, tiled=True)
    own_weight = lax.dynamic_slice_in_dim(edge_weight, lax.axis_index(everyone) * own, own, 0)
    weight_rows = jnp.broadcast_to(own_weight[:, None], (own, parts.shape[2]))
    matrix = dest_operator(dst_edges, dst_weight)
    half = matrix.shape[0] // 2
    matrix = jnp.where(core == 0, matrix, jnp.concatenate([matrix[half:], matrix[:half]], axis=0))
    keep, give = table_rows(parts, weight_rows, mixing, matrix, own, n_org, n_dst)
    longs, shorts = gather_table(keep, give)
    rows = anchor_edges.shape[0] // n_dst
    start = lax.axis_index(("rest", "near", "core")) * rows
    ids = lax.dynamic_slice_in_dim(edges_t, start, rows, 1)
    own_root = lax.dynamic_slice_in_dim(roots, start, rows, 1)
    bias = out_bias[None, :]
    other = 1 - core
    result = spread(core[None], *places_of(ids, core, own), own_root, bias, longs, shorts)
    longs, shorts = [swapped(x) for x in longs], [swapped(x) for x in shorts]
    return spread(other[None], *places_of(ids, other, own), own_root, bias, longs, shorts, result)


def solution(mesh):
    n_org, n_dst = mesh.devices.shape
    fine = Mesh(mesh.devices.reshape(n_org // 2, 2, n_dst // 4, 2, 2), ("slow", "mid", "rest", "near", "core"))
    org, dst = ("slow", "mid"), ("rest", "near", "core")
    in_specs = (P(org, dst, None), P(org, None), P(), P(), P(), P(), P())
    out_specs = P(org + dst, None, None)
    return jax.shard_map(shards, mesh=fine, in_specs=in_specs, out_specs=out_specs, check_vma=False)
```

```python
import functools

import jax
import jax.numpy as jnp
from jax import lax
from jax.experimental import pallas as pl
from jax.experimental.pallas import tpu as pltpu
from jax.sharding import Mesh, PartitionSpec as P

BF16 = jnp.bfloat16
F32 = jnp.float32
COUNT_BASE = 256.0
HEAD = 16


def corridor_table(edge_ids, edge_count):
    columns = jnp.arange(edge_count, dtype=jnp.int32)
    return jnp.sum((edge_ids[:, :, None] == columns[None, None, :]).astype(F32), axis=1)


def dest_operator(dst_edges, dst_weight):
    dst_member = corridor_table(dst_edges, dst_weight.shape[0])
    dst_degree = jnp.sum(dst_member * dst_weight[None, :], axis=1)
    edge_sizes = jnp.sum(dst_member, axis=0)
    left_factor = dst_member * lax.rsqrt(dst_degree)[:, None]
    right_factor = left_factor * (dst_weight / edge_sizes)[None, :]
    result = jnp.dot(right_factor, left_factor.T, precision=lax.Precision.HIGHEST)
    return result.astype(BF16)


class Plan:
    def __init__(self, zones, own, rest, line, anchors):
        self.own = own
        self.rest = rest
        self.line = line
        self.cut = zones * 5 // 8
        self.first_rows = self.cut * own
        self.second_rows = HEAD + (zones - self.cut) * own
        self.streams = 4 if anchors % 512 == 0 else 1

    def spot(self, device):
        core, near = device % 2, device // 2 % 2
        rest, mid, slow = device // 4 % self.rest, device // (4 * self.rest) % 2, device // (8 * self.rest)
        return mid * 4 + near * 2 + core, slow * self.rest + rest


def halves_of(counts):
    high = jnp.floor(counts * (1.0 / COUNT_BASE))
    return high, counts - high * COUNT_BASE


def head_rows(high, low):
    parts = [high, low]
    if high.shape[0] < HEAD // 2:
        pad = jnp.zeros((HEAD // 2 - high.shape[0], high.shape[1]), F32)
        parts = [high, pad, low, pad]
    return jnp.concatenate(parts, axis=0).astype(BF16)


def gather_kernel(own, group, pitch, plan, edges_ref, weight_ref, *refs):
    n_cells = plan.streams
    cells_refs = refs[:n_cells]
    first_ref, second_ref, root_ref, total_ref, count_ref = refs[n_cells : n_cells + 5]
    wide_refs = refs[n_cells + 5 :]
    step = pl.program_id(0)
    last = pl.num_programs(0) - 1
    strip, zones, lanes = cells_refs[0].shape
    rows = strip * n_cells
    edges = total_ref.shape[1]

    @pl.when(step == 0)
    def _():
        total_ref[...] = jnp.zeros_like(total_ref)
        count_ref[...] = jnp.zeros_like(count_ref)

    columns = lax.broadcasted_iota(jnp.int32, (edges, rows), 0)
    ids = edges_ref[...]
    member = columns == ids[0:1, :]
    for j in range(1, ids.shape[0]):
        member = jnp.logical_or(member, columns == ids[j : j + 1, :])
    upright = jnp.transpose(jnp.broadcast_to(weight_ref[...], (lanes, edges)))
    upright = jnp.concatenate([upright] * (rows // lanes), axis=1)
    root = lax.rsqrt(jnp.sum(jnp.where(member, upright, 0.0), axis=0, keepdims=True))
    root_ref[...] = root
    rounded = root.astype(BF16).astype(F32)
    weighted = jnp.where(member, rounded, 0.0).astype(BF16)
    hot = jnp.where(member, 1.0, 0.0).astype(BF16)
    count_ref[...] += jnp.dot(hot, jnp.ones((rows, lanes), BF16), preferred_element_type=F32)

    part = 32
    groups = zones // group
    pairs = group // 2

    def load(g, stream, first):
        return cells_refs[stream][pl.ds(first, part), g * group : (g + 1) * group, :].astype(F32)

    def store(g, first, piece):
        for i in range(part):
            wide_refs[g][pl.ds(pl.multiple_of((first + i) * pitch, 8), group), :] = piece[i]

    for stream in range(n_cells):

        def widen_first(i, carry):
            store(0, stream * strip + i * part, load(0, stream, i * part))
            return carry

        lax.fori_loop(0, strip // part, widen_first, 0)
    share = rows // part // pairs
    for g in range(groups):
        for pair in range(pairs):
            left = wide_refs[g][pl.ds(2 * pair, rows, stride=pitch), :].astype(BF16)
            right = wide_refs[g][pl.ds(2 * pair + 1, rows, stride=pitch), :].astype(BF16)
            both = jnp.concatenate([left, right], axis=1)
            if g + 1 < groups:
                for i in range(share):
                    first = (pair * share + i) * part
                    store(g + 1, first, load(g + 1, first // strip, first % strip))
            total_ref[g * pairs + pair] += jnp.dot(weighted, both, preferred_element_type=F32)

    @pl.when(step == last)
    def _():
        high, low = halves_of(count_ref[...])
        for device in range(edges // own):
            square, line = plan.spot(device)
            at = slice(device * own, (device + 1) * own)

            def columns_of(start, stop):
                data = []
                for d in range(start, stop):
                    data.append(total_ref[d // 2, at, (d % 2) * lanes : (d % 2 + 1) * lanes])
                return jnp.concatenate(data, axis=0).astype(BF16)

            first_ref[square, line] = columns_of(0, plan.cut)
            second_ref[line, square, HEAD:, :] = columns_of(plan.cut, zones)
            second_ref[line, square, 0:HEAD, :] = head_rows(high[at], low[at])


def partial_sums(cells, edges_t, edge_weight, plan):
    anchors, zones, lanes = cells.shape
    edges = edge_weight.shape[0]
    rows = min(512, anchors)
    strip = rows // plan.streams
    group = min(zones, 16)
    pitch = group + 8
    specs = []
    for stream in range(plan.streams):
        specs.append(pl.BlockSpec((strip, zones, lanes), lambda i, stream=stream: (i * plan.streams + stream, 0, 0)))
    shapes = [(8, plan.line, plan.first_rows, lanes), (plan.line, 8, plan.second_rows, lanes)]
    return pl.pallas_call(
        functools.partial(gather_kernel, plan.own, group, pitch, plan),
        grid=(anchors // rows,),
        in_specs=[
            pl.BlockSpec((edges_t.shape[0], rows), lambda i: (0, i)),
            pl.BlockSpec((1, edges), lambda i: (0, 0)),
        ]
        + specs,
        out_specs=[pl.BlockSpec(shape, lambda i: (0, 0, 0, 0)) for shape in shapes]
        + [pl.BlockSpec((1, rows), lambda i: (0, i))],
        out_shape=[jax.ShapeDtypeStruct(shape, BF16) for shape in shapes] + [jax.ShapeDtypeStruct((1, anchors), F32)],
        scratch_shapes=[
            pltpu.VMEM((zones // 2, edges, 2 * lanes), F32),
            pltpu.VMEM((edges, lanes), F32),
        ]
        + [pltpu.VMEM((rows * pitch, lanes), F32)] * (zones // group),
        compiler_params=pltpu.CompilerParams(vmem_limit_bytes=48 * 1024 * 1024),
        cost_estimate=pl.CostEstimate(
            flops=2 * anchors * edges * zones * lanes, bytes_accessed=2 * anchors * zones * lanes, transcendentals=0
        ),
    )(edges_t, edge_weight[None, :], *([cells] * plan.streams))


def add_rows(ref, spots):
    total = ref[spots[0]].astype(F32)
    for spot in spots[1:]:
        total = total + ref[spot].astype(F32)
    return total


def fold_first_kernel(plan, parts_ref, out_ref):
    for line in range(plan.line):
        for quarter in range(4):
            out_ref[line, quarter] = add_rows(parts_ref, [(quarter, line), (4 + quarter, line)]).astype(BF16)


def fold_second_kernel(plan, parts_ref, out_ref):
    for square in range(8):
        for rest in range(plan.rest):
            spots = [(line, square) for line in range(rest, plan.line, plan.rest)]
            total = add_rows(parts_ref, spots)
            half = HEAD // 2
            high, low = halves_of(total[0:half] * COUNT_BASE + total[half:HEAD])
            out_ref[square, rest, 0:HEAD, :] = head_rows(high, low)
            out_ref[square, rest, HEAD:, :] = total[HEAD:].astype(BF16)


def fold(kernel, plan, parts, shape):
    whole = pl.BlockSpec(memory_space=pltpu.VMEM)
    return pl.pallas_call(
        functools.partial(kernel, plan),
        in_specs=[whole],
        out_specs=whole,
        out_shape=jax.ShapeDtypeStruct(shape, BF16),
        compiler_params=pltpu.CompilerParams(vmem_limit_bytes=16 * 1024 * 1024),
        cost_estimate=pl.CostEstimate(flops=parts.size, bytes_accessed=parts.size * 4, transcendentals=0),
    )(parts)


def org_sums(first, second, plan):
    lanes = first.shape[-1]
    first = lax.all_to_all(first, SQUARE, split_axis=0, concat_axis=0, tiled=True)
    second = lax.all_to_all(second, LINE, split_axis=0, concat_axis=0, tiled=True)
    second = fold(fold_second_kernel, plan, second, (8, plan.rest, plan.second_rows, lanes))
    first = fold(fold_first_kernel, plan, first, (plan.line, 4, plan.first_rows, lanes))
    second = lax.all_to_all(second, SQUARE, split_axis=0, concat_axis=0, tiled=True)
    first = lax.all_to_all(first, LINE, split_axis=0, concat_axis=0, tiled=True)
    return first, second


def table_kernel(plan, first_ref, second_ref, weight_ref, mixing_ref, matrix_ref, keep_ref, give_ref, mixed_ref):
    own = plan.own
    lanes = first_ref.shape[-1]
    head_lines = [second_ref[mid * 4, 0, 0:HEAD, :].astype(F32) for mid in range(2)]
    head = head_lines[0] + head_lines[1]
    half = HEAD // 2
    counts = head[0:half] * COUNT_BASE + head[half:HEAD]
    scale = weight_ref[...] / counts[0:own]
    rows = plan.first_rows + plan.second_rows - HEAD
    zones = rows // own
    n_dst = 4 * plan.rest
    for k in range(n_dst):
        rest, quarter = k // 4, k % 4
        first = add_rows(first_ref, [(line, quarter) for line in range(rest, plan.line, plan.rest)])
        second = add_rows(second_ref, [(quarter, rest), (4 + quarter, rest)])[HEAD:]
        start = k * rows
        for total in (first, second):
            size = total.shape[0]
            totals = (total * jnp.concatenate([scale] * (size // own), axis=0)).astype(BF16)
            mixed = jnp.dot(totals, mixing_ref[...], preferred_element_type=F32)
            mixed_ref[start : start + size, :] = mixed
            start += size
    whole = n_dst * zones
    for e in range(own):
        mixed = mixed_ref[pl.ds(e, whole, stride=own), :] if own > 1 else mixed_ref[...]
        high = mixed.astype(BF16)
        low = (mixed - high.astype(F32)).astype(BF16)
        both = jnp.dot(matrix_ref[...], jnp.concatenate([high, low], axis=1), preferred_element_type=F32)
        result = (both[:, 0:lanes] + both[:, lanes : 2 * lanes]).astype(BF16)
        keep_ref[e] = result[0 : whole // 2]
        give_ref[e] = result[whole // 2 :]


def table_rows(first, second, weight_rows, mixing, matrix, plan):
    zones = matrix.shape[0]
    lanes = first.shape[-1]
    whole = pl.BlockSpec(memory_space=pltpu.VMEM)
    half = jax.ShapeDtypeStruct((plan.own, zones // 2, lanes), BF16)
    return pl.pallas_call(
        functools.partial(table_kernel, plan),
        in_specs=[whole] * 5,
        out_specs=[whole] * 2,
        out_shape=[half, half],
        scratch_shapes=[pltpu.VMEM((zones * plan.own, lanes), F32)],
        compiler_params=pltpu.CompilerParams(vmem_limit_bytes=32 * 1024 * 1024),
        cost_estimate=pl.CostEstimate(
            flops=8 * plan.own * zones * lanes * lanes, bytes_accessed=first.size * 4, transcendentals=0
        ),
    )(first, second, weight_rows, mixing, matrix)


def spread_kernel(n_long, n_short, half_ref, long_at_ref, short_at_ref, root_ref, bias_ref, *refs):
    longs = refs[:n_long]
    shorts = refs[n_long : n_long + n_short]
    out_ref, long_ref, short_ref, ring_ref, sems, ring_sems = refs[-6:]
    slots, rows, zones, lanes = ring_ref.shape
    steps = out_ref.shape[0] // rows
    half = half_ref[0]

    copies = []
    for table, sources in ((long_ref, longs), (short_ref, shorts)):
        size = sources[0].shape[0]
        for i, source in enumerate(sources):
            copies.append(pltpu.make_async_copy(source, table.at[pl.ds(i * size, size)], sems.at[len(copies)]))
    for copy in copies:
        copy.start()
    for copy in copies:
        copy.wait()

    bias = bias_ref[...]
    count = long_at_ref.shape[0]
    tile = 16
    batch = 4
    tiles = zones // tile

    def leaving(step, slot):
        place = out_ref.at[pl.ds(step * rows, rows), pl.ds(pl.multiple_of(half * zones, zones), zones), :]
        return pltpu.make_async_copy(ring_ref.at[slot], place, ring_sems.at[slot])

    def one_step(step, carry):
        slot = lax.rem(step, slots)

        @pl.when(step >= slots)
        def _():
            leaving(step - slots, slot).wait()

        def several(group, inner):
            values = []
            for i in range(batch):
                at = step * rows + group * batch + i
                scale = root_ref[0, at]
                for table, places in ((long_ref, long_at_ref), (short_ref, short_at_ref)):
                    spots = [places[j, at] for j in range(count)]
                    for first in range(0, table.shape[1], tile):
                        pieces = [table[spot, first : first + tile, :] for spot in spots]
                        pieces = [(a + b).astype(F32) for a, b in zip(pieces[0::2], pieces[1::2])]
                        total = sum(pieces[1:], pieces[0])
                        values.append(jnp.maximum((total * scale + bias).astype(BF16), BF16(0.0)))
            for n, value in enumerate(values):
                start = n % tiles * tile
                ring_ref[slot, group * batch + n // tiles, start : start + tile, :] = value
            return inner

        lax.fori_loop(0, rows // batch, several, 0)
        leaving(step, slot).start()
        return carry

    lax.fori_loop(0, steps, one_step, 0)
    for step in range(steps - slots, steps):
        leaving(step, step % slots).wait()


def spread(half, long_at, short_at, root, bias, longs, shorts, before=None):
    anchors = long_at.shape[1]
    lanes = bias.shape[1]
    zones = longs[0].shape[1] + shorts[0].shape[1]
    rows = min(16, anchors // 8)
    slots = min(8, anchors // rows)
    smem = pl.BlockSpec(memory_space=pltpu.SMEM)
    anywhere = pl.BlockSpec(memory_space=pltpu.HBM)
    tables = [pltpu.VMEM((len(pieces) * pieces[0].shape[0],) + pieces[0].shape[1:], BF16) for pieces in (longs, shorts)]
    operands = [half, long_at, short_at, root, bias] + longs + shorts
    specs = [smem, smem, smem, smem, pl.BlockSpec(memory_space=pltpu.VMEM)] + [anywhere] * len(longs + shorts)
    aliases = {}
    if before is not None:
        aliases = {len(operands): 0}
        operands.append(before)
        specs.append(anywhere)
    return pl.pallas_call(
        functools.partial(spread_kernel, len(longs), len(shorts)),
        in_specs=specs,
        out_specs=anywhere,
        out_shape=jax.ShapeDtypeStruct((anchors, 2 * zones, lanes), BF16),
        scratch_shapes=tables
        + [
            pltpu.VMEM((slots, rows, zones, lanes), BF16),
            pltpu.SemaphoreType.DMA((len(longs) + len(shorts),)),
            pltpu.SemaphoreType.DMA((slots,)),
        ],
        input_output_aliases=aliases,
        compiler_params=pltpu.CompilerParams(vmem_limit_bytes=24 * 1024 * 1024),
        cost_estimate=pl.CostEstimate(
            flops=4096 * anchors * zones * lanes, bytes_accessed=4 * anchors * zones * lanes, transcendentals=0
        ),
    )(*operands)


LINE = ("slow", "rest")
SQUARE = ("mid", "near", "core")


def shifted(x, amount):
    size = lax.axis_size(LINE)
    return lax.ppermute(x, LINE, [(i, (i + amount) % size) for i in range(size)])


def crossed(x, turn):
    pairs = []
    for device in range(8):
        core = device % 2
        pairs.append((device, device ^ (2 if core == turn else 4)))
    return lax.ppermute(x, SQUARE, pairs)


def swapped(x):
    return lax.ppermute(x, "core", [(0, 1), (1, 0)])


def gather_table(keep, give):
    size = lax.axis_size(LINE)
    block = jnp.concatenate([keep, swapped(give)], axis=0)
    split = block.shape[1] * 3 // 4
    long, short = block[:, :split], block[:, split:]
    line = [long] + [shifted(long, k) for k in range(1, size - 1)]
    short = jnp.concatenate([short, crossed(short, 0)], axis=0)
    short, long = lax.optimization_barrier((short, long))
    line.append(shifted(long, size - 1))
    short = jnp.concatenate([short, crossed(short, 1)], axis=0)
    long = jnp.concatenate(line, axis=0)
    short, long = lax.optimization_barrier((short, long))
    first = crossed(long, 0)
    second = crossed(long, 1)
    shorts = [short] + [shifted(short, k) for k in range(1, size)]
    first, *shorts[1:-1] = lax.optimization_barrier((first, *shorts[1:-1]))
    both = crossed(first, 1)
    return [long, first, second, both], shorts


def places_of(ids, core, own):
    rest, size = lax.axis_size("rest"), lax.axis_size(LINE)
    owner = ids // own
    slot = jnp.where(owner % 2 == core, 0, own) + ids % own
    near = jnp.bitwise_xor(owner // 2 % 2, lax.axis_index("near"))
    mid = jnp.bitwise_xor(owner // (4 * rest) % 2, lax.axis_index("mid"))
    line = owner // (8 * rest) * rest + owner // 4 % rest
    line = lax.rem(lax.axis_index(LINE) - line + size, size)
    square = jnp.where(core == 0, 2 * mid + near, 2 * near + mid)
    return (square * size + line) * (2 * own) + slot, (line * 4 + square) * (2 * own) + slot


def shards(od_cells, anchor_edges, edge_weight, mixing, dst_edges, dst_weight, out_bias):
    n_org = lax.axis_size("slow") * lax.axis_size("mid")
    n_dst = lax.axis_size("rest") * lax.axis_size("near") * lax.axis_size("core")
    own = edge_weight.shape[0] // (n_org * n_dst)
    everyone = ("slow", "mid", "rest", "near", "core")
    core = lax.axis_index("core")
    edges_t = anchor_edges.T
    plan = Plan(od_cells.shape[1], own, lax.axis_size("rest"), lax.axis_size(LINE), od_cells.shape[0])
    first, second, roots = partial_sums(od_cells, edges_t, edge_weight, plan)
    first, second = org_sums(first, second, plan)
    own_weight = lax.dynamic_slice_in_dim(edge_weight, lax.axis_index(everyone) * own, own, 0)
    weight_rows = jnp.broadcast_to(own_weight[:, None], (own, mixing.shape[0]))
    matrix = dest_operator(dst_edges, dst_weight)
    half = matrix.shape[0] // 2
    matrix = jnp.where(core == 0, matrix, jnp.concatenate([matrix[half:], matrix[:half]], axis=0))
    keep, give = table_rows(first, second, weight_rows, mixing, matrix, plan)
    longs, shorts = gather_table(keep, give)
    rows = anchor_edges.shape[0] // n_dst
    start = lax.axis_index(("rest", "near", "core")) * rows
    ids = lax.dynamic_slice_in_dim(edges_t, start, rows, 1)
    own_root = lax.dynamic_slice_in_dim(roots, start, rows, 1)
    bias = out_bias[None, :]
    other = 1 - core
    result = spread(core[None], *places_of(ids, core, own), own_root, bias, longs, shorts)
    longs, shorts = [swapped(x) for x in longs], [swapped(x) for x in shorts]
    return spread(other[None], *places_of(ids, other, own), own_root, bias, longs, shorts, result)


def solution(mesh):
    n_org, n_dst = mesh.devices.shape
    fine = Mesh(mesh.devices.reshape(n_org // 2, 2, n_dst // 4, 2, 2), ("slow", "mid", "rest", "near", "core"))
    org, dst = ("slow", "mid"), ("rest", "near", "core")
    in_specs = (P(org, dst, None), P(org, None), P(), P(), P(), P(), P())
    out_specs = P(org + dst, None, None)
    return jax.shard_map(shards, mesh=fine, in_specs=in_specs, out_specs=out_specs, check_vma=False)
```

```python
import functools

import jax
import jax.numpy as jnp
from jax import lax
from jax.experimental import pallas as pl
from jax.experimental.pallas import tpu as pltpu
from jax.sharding import Mesh, PartitionSpec as P

BF16 = jnp.bfloat16
F32 = jnp.float32
COUNT_BASE = 256.0
HEAD = 16


def corridor_table(edge_ids, edge_count):
    columns = jnp.arange(edge_count, dtype=jnp.int32)
    return jnp.sum((edge_ids[:, :, None] == columns[None, None, :]).astype(F32), axis=1)


def dest_operator(dst_edges, dst_weight):
    dst_member = corridor_table(dst_edges, dst_weight.shape[0])
    dst_degree = jnp.sum(dst_member * dst_weight[None, :], axis=1)
    edge_sizes = jnp.sum(dst_member, axis=0)
    left_factor = dst_member * lax.rsqrt(dst_degree)[:, None]
    right_factor = left_factor * (dst_weight / edge_sizes)[None, :]
    result = jnp.dot(right_factor, left_factor.T, precision=lax.Precision.HIGHEST)
    return result.astype(BF16)


class Plan:
    def __init__(self, zones, own, rest, line):
        self.own = own
        self.rest = rest
        self.line = line
        self.cut = zones * 5 // 8
        self.first_rows = self.cut * own
        self.second_rows = HEAD + (zones - self.cut) * own

        self.relative = own % 8 == 0

    def device(self, square, line):
        core, near, mid = square % 2, square // 2 % 2, square // 4
        if isinstance(line, int):
            slow, rest = line // self.rest, line % self.rest
        else:
            slow, rest = lax.div(line, self.rest), lax.rem(line, self.rest)
        return (((slow * 2 + mid) * self.rest + rest) * 2 + near) * 2 + core


def halves_of(counts):
    high = jnp.floor(counts * (1.0 / COUNT_BASE))
    return high, counts - high * COUNT_BASE


def head_rows(high, low):
    parts = [high, low]
    if high.shape[0] < HEAD // 2:
        pad = jnp.zeros((HEAD // 2 - high.shape[0], high.shape[1]), F32)
        parts = [high, pad, low, pad]
    return jnp.concatenate(parts, axis=0).astype(BF16)


def gather_kernel(plan, group, pitch, line_ref, edges_ref, weight_ref, cells_ref, *refs):
    own = plan.own
    first_ref = refs[0]
    second_refs = refs[1 : 1 + plan.line]
    root_ref, total_ref, count_ref = refs[1 + plan.line : 4 + plan.line]
    wide_refs = refs[4 + plan.line :]
    step = pl.program_id(0)
    last = pl.num_programs(0) - 1
    rows, zones, lanes = cells_ref.shape
    edges = total_ref.shape[1]

    @pl.when(step == 0)
    def _():
        total_ref[...] = jnp.zeros_like(total_ref)
        count_ref[...] = jnp.zeros_like(count_ref)

    columns = lax.broadcasted_iota(jnp.int32, (edges, rows), 0)
    ids = edges_ref[...]
    member = columns == ids[0:1, :]
    for j in range(1, ids.shape[0]):
        member = jnp.logical_or(member, columns == ids[j : j + 1, :])
    upright = jnp.transpose(jnp.broadcast_to(weight_ref[...], (lanes, edges)))
    upright = jnp.concatenate([upright] * (rows // lanes), axis=1)
    root = lax.rsqrt(jnp.sum(jnp.where(member, upright, 0.0), axis=0, keepdims=True))
    root_ref[...] = root
    rounded = root.astype(BF16).astype(F32)
    weighted = jnp.where(member, rounded, 0.0).astype(BF16)
    hot = jnp.where(member, 1.0, 0.0).astype(BF16)
    count_ref[...] += jnp.dot(hot, jnp.ones((rows, lanes), BF16), preferred_element_type=F32)

    part = 32
    groups = zones // group
    pairs = group // 2

    def load(g, first):
        return cells_ref[pl.ds(first, part), g * group : (g + 1) * group, :].astype(F32)

    def store(g, first, piece):
        for i in range(part):
            wide_refs[g][pl.ds(pl.multiple_of((first + i) * pitch, 8), group), :] = piece[i]

    def widen_first(i, carry):
        store(0, i * part, load(0, i * part))
        return carry

    lax.fori_loop(0, rows // part, widen_first, 0)
    share = rows // part // pairs
    for g in range(groups):
        for pair in range(pairs):
            left = wide_refs[g][pl.ds(2 * pair, rows, stride=pitch), :].astype(BF16)
            right = wide_refs[g][pl.ds(2 * pair + 1, rows, stride=pitch), :].astype(BF16)
            both = jnp.concatenate([left, right], axis=1)
            if g + 1 < groups:
                for i in range(share):
                    first = (pair * share + i) * part
                    store(g + 1, first, load(g + 1, first))
            total_ref[g * pairs + pair] += jnp.dot(weighted, both, preferred_element_type=F32)

    @pl.when(step == last)
    def _():
        for square in range(8):
            for shift in range(plan.line):
                if plan.relative:
                    device = plan.device(square, lax.rem(line_ref[0] + shift, plan.line))
                    at = pl.ds(pl.multiple_of(device * own, own), own)
                else:
                    device = plan.device(square, shift)
                    at = slice(device * own, (device + 1) * own)

                def columns_of(start, stop):
                    data = []
                    for d in range(start, stop):
                        data.append(total_ref[d // 2, at, (d % 2) * lanes : (d % 2 + 1) * lanes])
                    return jnp.concatenate(data, axis=0).astype(BF16)

                first_ref[square, shift] = columns_of(0, plan.cut)
                second_refs[shift][square, HEAD:, :] = columns_of(plan.cut, zones)
                second_refs[shift][square, 0:HEAD, :] = head_rows(*halves_of(count_ref[at, :]))


def partial_sums(line, cells, edges_t, edge_weight, plan):
    anchors, zones, lanes = cells.shape
    edges = edge_weight.shape[0]
    rows = min(512, anchors)
    group = min(zones, 16)
    pitch = group + 8
    shapes = [(8, plan.line, plan.first_rows, lanes)] + [(8, plan.second_rows, lanes)] * plan.line
    outs = pl.pallas_call(
        functools.partial(gather_kernel, plan, group, pitch),
        grid=(anchors // rows,),
        in_specs=[
            pl.BlockSpec(memory_space=pltpu.SMEM),
            pl.BlockSpec((edges_t.shape[0], rows), lambda i: (0, i)),
            pl.BlockSpec((1, edges), lambda i: (0, 0)),
            pl.BlockSpec((rows, zones, lanes), lambda i: (i, 0, 0)),
        ],
        out_specs=[pl.BlockSpec(shape, lambda i, zeros=(0,) * len(shape): zeros) for shape in shapes]
        + [pl.BlockSpec((1, rows), lambda i: (0, i))],
        out_shape=[jax.ShapeDtypeStruct(shape, BF16) for shape in shapes] + [jax.ShapeDtypeStruct((1, anchors), F32)],
        scratch_shapes=[
            pltpu.VMEM((zones // 2, edges, 2 * lanes), F32),
            pltpu.VMEM((edges, lanes), F32),
        ]
        + [pltpu.VMEM((rows * pitch, lanes), F32)] * (zones // group),
        compiler_params=pltpu.CompilerParams(vmem_limit_bytes=48 * 1024 * 1024),
        cost_estimate=pl.CostEstimate(
            flops=2 * anchors * edges * zones * lanes, bytes_accessed=2 * anchors * zones * lanes, transcendentals=0
        ),
    )(line[None], edges_t, edge_weight[None, :], cells)
    first, seconds = outs[0], outs[1:-1]
    if not plan.relative:
        first = lax.dynamic_slice_in_dim(jnp.concatenate([first, first], axis=1), line, plan.line, 1)
        seconds = jnp.stack(seconds * 2)
        seconds = [lax.dynamic_index_in_dim(seconds, line + k, 0, keepdims=False) for k in range(plan.line)]
    return first, seconds, outs[-1]


def add_up(pieces):
    total = pieces[0].astype(F32)
    for piece in pieces[1:]:
        total = total + piece.astype(F32)
    return total


def fold_first_kernel(plan, part_ref, *outs):
    for shift in range(plan.line):
        for quarter in range(4):
            outs[shift][quarter] = add_up([part_ref[quarter, shift], part_ref[4 + quarter, shift]]).astype(BF16)


def fold_second_kernel(plan, *refs):
    parts, out_ref = refs[: plan.line], refs[plan.line]
    for square in range(8):
        for rest in range(plan.rest):
            total = add_up([parts[shift][square] for shift in range(rest, plan.line, plan.rest)])
            half = HEAD // 2
            out_ref[square, rest, 0:HEAD, :] = head_rows(*halves_of(total[0:half] * COUNT_BASE + total[half:HEAD]))
            out_ref[square, rest, HEAD:, :] = total[HEAD:].astype(BF16)


def fold(kernel, plan, parts, shapes):
    whole = pl.BlockSpec(memory_space=pltpu.VMEM)
    size = sum(part.size for part in parts)
    return pl.pallas_call(
        functools.partial(kernel, plan),
        in_specs=[whole] * len(parts),
        out_specs=[whole] * len(shapes),
        out_shape=[jax.ShapeDtypeStruct(shape, BF16) for shape in shapes],
        compiler_params=pltpu.CompilerParams(vmem_limit_bytes=16 * 1024 * 1024),
        cost_estimate=pl.CostEstimate(flops=size, bytes_accessed=size * 4, transcendentals=0),
    )(*parts)


def org_sums(first, seconds, plan):
    lanes = first.shape[-1]
    seconds = [shifted(part, shift) if shift else part for shift, part in enumerate(seconds)]
    first = lax.all_to_all(first, SQUARE, split_axis=0, concat_axis=0, tiled=True)
    second = fold(fold_second_kernel, plan, seconds, [(8, plan.rest, plan.second_rows, lanes)])[0]
    firsts = fold(fold_first_kernel, plan, [first], [(4, plan.first_rows, lanes)] * plan.line)
    firsts = [shifted(part, shift) if shift else part for shift, part in enumerate(firsts)]
    second = lax.all_to_all(second, SQUARE, split_axis=0, concat_axis=0, tiled=True)
    return firsts, second


def table_kernel(plan, weight_ref, mixing_ref, matrix_ref, *refs):
    firsts = refs[: plan.line]
    second_ref, keep_ref, give_ref, mixed_ref = refs[plan.line :]
    own = plan.own
    lanes = mixing_ref.shape[0]
    half = HEAD // 2
    head = add_up([second_ref[0, 0, 0:HEAD, :], second_ref[4, 0, 0:HEAD, :]])
    counts = head[0:half] * COUNT_BASE + head[half:HEAD]
    scale = weight_ref[...] / counts[0:own]
    rows = plan.first_rows + plan.second_rows - HEAD
    zones = rows // own
    n_dst = 4 * plan.rest
    for k in range(n_dst):
        rest, quarter = k // 4, k % 4
        first = add_up([firsts[shift][quarter] for shift in range(rest, plan.line, plan.rest)])
        second = add_up([second_ref[quarter, rest, HEAD:, :], second_ref[4 + quarter, rest, HEAD:, :]])
        start = k * rows
        for total in (first, second):
            size = total.shape[0]
            totals = (total * jnp.concatenate([scale] * (size // own), axis=0)).astype(BF16)
            mixed = jnp.dot(totals, mixing_ref[...], preferred_element_type=F32)
            mixed_ref[start : start + size, :] = mixed
            start += size
    whole = n_dst * zones
    for e in range(own):
        mixed = mixed_ref[pl.ds(e, whole, stride=own), :] if own > 1 else mixed_ref[...]
        high = mixed.astype(BF16)
        low = (mixed - high.astype(F32)).astype(BF16)
        both = jnp.dot(matrix_ref[...], jnp.concatenate([high, low], axis=1), preferred_element_type=F32)
        result = (both[:, 0:lanes] + both[:, lanes : 2 * lanes]).astype(BF16)
        keep_ref[e] = result[0 : whole // 2]
        give_ref[e] = result[whole // 2 :]


def table_rows(firsts, second, weight_rows, mixing, matrix, plan):
    zones = matrix.shape[0]
    lanes = mixing.shape[0]
    whole = pl.BlockSpec(memory_space=pltpu.VMEM)
    half = jax.ShapeDtypeStruct((plan.own, zones // 2, lanes), BF16)
    return pl.pallas_call(
        functools.partial(table_kernel, plan),
        in_specs=[whole] * (4 + len(firsts)),
        out_specs=[whole] * 2,
        out_shape=[half, half],
        scratch_shapes=[pltpu.VMEM((zones * plan.own, lanes), F32)],
        compiler_params=pltpu.CompilerParams(vmem_limit_bytes=32 * 1024 * 1024),
        cost_estimate=pl.CostEstimate(
            flops=8 * plan.own * zones * lanes * lanes, bytes_accessed=4 * zones * plan.own * lanes, transcendentals=0
        ),
    )(weight_rows, mixing, matrix, *firsts, second)


def spread_kernel(n_long, n_short, half_ref, places_ref, root_ref, bias_ref, *refs):
    longs = refs[:n_long]
    shorts = refs[n_long : n_long + n_short]
    out_ref, table_ref, ring_ref, sems, ring_sems = refs[-5:]
    slots, rows, zones, lanes = ring_ref.shape
    steps = out_ref.shape[0] // rows
    half = half_ref[0]

    copies = []

    def bring(source, first, start):
        place = table_ref.at[pl.ds(first, source.shape[0]), pl.ds(start, source.shape[1]), :]
        copies.append(pltpu.make_async_copy(source, place, sems.at[len(copies)]))

    split = longs[0].shape[1]
    size = shorts[0].shape[0] // n_long
    for square, source in enumerate(longs):
        bring(source, square * n_short * size, 0)
    for shift, source in enumerate(shorts):
        for square in range(n_long):
            bring(source.at[pl.ds(square * size, size)], (square * n_short + shift) * size, split)
    for copy in copies:
        copy.start()
    for copy in copies:
        copy.wait()

    bias = bias_ref[...]
    count = places_ref.shape[0]
    tile = 16
    batch = min(8, rows)
    tiles = zones // tile

    def leaving(step, slot):
        place = out_ref.at[pl.ds(step * rows, rows), pl.ds(pl.multiple_of(half * zones, zones), zones), :]
        return pltpu.make_async_copy(ring_ref.at[slot], place, ring_sems.at[slot])

    def one_step(step, carry):
        slot = lax.rem(step, slots)

        @pl.when(step >= slots)
        def _():
            leaving(step - slots, slot).wait()

        def several(group, inner):
            values = []
            for i in range(batch):
                at = step * rows + group * batch + i
                scale = root_ref[0, at]
                spots = [places_ref[j, at] for j in range(count)]
                for first in range(0, zones, tile):
                    pieces = [table_ref[spot, first : first + tile, :] for spot in spots]
                    pieces = [(a + b).astype(F32) for a, b in zip(pieces[0::2], pieces[1::2])]
                    total = sum(pieces[1:], pieces[0])
                    values.append(jnp.maximum((total * scale + bias).astype(BF16), BF16(0.0)))
            for n, value in enumerate(values):
                start = n % tiles * tile
                ring_ref[slot, group * batch + n // tiles, start : start + tile, :] = value
            return inner

        lax.fori_loop(0, rows // batch, several, 0)
        leaving(step, slot).start()
        return carry

    lax.fori_loop(0, steps, one_step, 0)
    for step in range(steps - slots, steps):
        leaving(step, step % slots).wait()


def spread(half, places, root, bias, longs, shorts, before=None):
    anchors = places.shape[1]
    lanes = bias.shape[1]
    zones = longs[0].shape[1] + shorts[0].shape[1]
    rows = min(16, anchors // 8)
    slots = min(8, anchors // rows)
    smem = pl.BlockSpec(memory_space=pltpu.SMEM)
    anywhere = pl.BlockSpec(memory_space=pltpu.HBM)
    pieces = longs + shorts
    operands = [half, places, root, bias] + pieces
    specs = [smem, smem, smem, pl.BlockSpec(memory_space=pltpu.VMEM)] + [anywhere] * len(pieces)
    aliases = {}
    if before is not None:
        aliases = {len(operands): 0}
        operands.append(before)
        specs.append(anywhere)
    return pl.pallas_call(
        functools.partial(spread_kernel, len(longs), len(shorts)),
        in_specs=specs,
        out_specs=anywhere,
        out_shape=jax.ShapeDtypeStruct((anchors, 2 * zones, lanes), BF16),
        scratch_shapes=[
            pltpu.VMEM((len(longs) * longs[0].shape[0], zones, lanes), BF16),
            pltpu.VMEM((slots, rows, zones, lanes), BF16),
            pltpu.SemaphoreType.DMA((len(longs) * (1 + len(shorts)),)),
            pltpu.SemaphoreType.DMA((slots,)),
        ],
        input_output_aliases=aliases,
        compiler_params=pltpu.CompilerParams(vmem_limit_bytes=24 * 1024 * 1024),
        cost_estimate=pl.CostEstimate(
            flops=4096 * anchors * zones * lanes, bytes_accessed=4 * anchors * zones * lanes, transcendentals=0
        ),
    )(*operands)


LINE = ("slow", "rest")
SQUARE = ("mid", "near", "core")


def shifted(x, amount):
    size = lax.axis_size(LINE)
    return lax.ppermute(x, LINE, [(i, (i + amount) % size) for i in range(size)])


def crossed(x, turn):
    pairs = []
    for device in range(8):
        core = device % 2
        pairs.append((device, device ^ (2 if core == turn else 4)))
    return lax.ppermute(x, SQUARE, pairs)


def masked(x, mask):
    return lax.ppermute(x, SQUARE, [(device, device ^ mask) for device in range(8)])


def swapped(x):
    return lax.ppermute(x, "core", [(0, 1), (1, 0)])


def gather_table(keep, give):
    size = lax.axis_size(LINE)
    block = jnp.concatenate([keep, swapped(give)], axis=0)
    split = block.shape[1] * 3 // 4
    long, short = block[:, :split], block[:, split:]
    line = [long] + [shifted(long, k) for k in range(1, size)]
    short = jnp.concatenate([short, crossed(short, 0), crossed(short, 1), masked(short, 6)], axis=0)
    long = jnp.concatenate(line, axis=0)
    short, long = lax.optimization_barrier((short, long))
    first = crossed(long, 0)
    second = crossed(long, 1)
    shorts = [short] + [shifted(short, k) for k in range(1, size)]
    first, *shorts[1:-1] = lax.optimization_barrier((first, *shorts[1:-1]))
    both = crossed(first, 1)
    return [long, first, second, both], shorts


def places_of(ids, core, own):
    rest, size = lax.axis_size("rest"), lax.axis_size(LINE)
    owner = ids // own
    slot = jnp.where(owner % 2 == core, 0, own) + ids % own
    near = jnp.bitwise_xor(owner // 2 % 2, lax.axis_index("near"))
    mid = jnp.bitwise_xor(owner // (4 * rest) % 2, lax.axis_index("mid"))
    line = owner // (8 * rest) * rest + owner // 4 % rest
    line = lax.rem(lax.axis_index(LINE) - line + size, size)
    square = jnp.where(core == 0, 2 * mid + near, 2 * near + mid)
    return (square * size + line) * (2 * own) + slot


def relative_columns(matrix):
    zones, rest = matrix.shape[0], lax.axis_size("rest")
    if rest == 1:
        return matrix
    back = jnp.flip(matrix.reshape(zones, rest, -1), 1)
    back = jnp.concatenate([back, back], axis=1)
    return lax.dynamic_slice_in_dim(back, rest - 1 - lax.axis_index("rest"), rest, 1).reshape(zones, zones)


def shards(od_cells, anchor_edges, edge_weight, mixing, dst_edges, dst_weight, out_bias):
    n_org = lax.axis_size("slow") * lax.axis_size("mid")
    n_dst = lax.axis_size("rest") * lax.axis_size("near") * lax.axis_size("core")
    own = edge_weight.shape[0] // (n_org * n_dst)
    everyone = ("slow", "mid", "rest", "near", "core")
    core = lax.axis_index("core")
    edges_t = anchor_edges.T
    plan = Plan(od_cells.shape[1], own, lax.axis_size("rest"), lax.axis_size(LINE))
    first, seconds, roots = partial_sums(lax.axis_index(LINE), od_cells, edges_t, edge_weight, plan)
    firsts, second = org_sums(first, seconds, plan)
    own_weight = lax.dynamic_slice_in_dim(edge_weight, lax.axis_index(everyone) * own, own, 0)
    weight_rows = jnp.broadcast_to(own_weight[:, None], (own, mixing.shape[0]))
    matrix = relative_columns(dest_operator(dst_edges, dst_weight))
    half = matrix.shape[0] // 2
    matrix = jnp.where(core == 0, matrix, jnp.concatenate([matrix[half:], matrix[:half]], axis=0))
    keep, give = table_rows(firsts, second, weight_rows, mixing, matrix, plan)
    longs, shorts = gather_table(keep, give)
    rows = anchor_edges.shape[0] // n_dst
    start = lax.axis_index(("rest", "near", "core")) * rows
    ids = lax.dynamic_slice_in_dim(edges_t, start, rows, 1)
    own_root = lax.dynamic_slice_in_dim(roots, start, rows, 1)
    bias = out_bias[None, :]
    other = 1 - core
    result = spread(core[None], places_of(ids, core, own), own_root, bias, longs, shorts)
    longs, shorts = [swapped(x) for x in longs], [swapped(x) for x in shorts]
    return spread(other[None], places_of(ids, other, own), own_root, bias, longs, shorts, result)


def solution(mesh):
    n_org, n_dst = mesh.devices.shape
    fine = Mesh(mesh.devices.reshape(n_org // 2, 2, n_dst // 4, 2, 2), ("slow", "mid", "rest", "near", "core"))
    org, dst = ("slow", "mid"), ("rest", "near", "core")
    in_specs = (P(org, dst, None), P(org, None), P(), P(), P(), P(), P())
    out_specs = P(org + dst, None, None)
    return jax.shard_map(shards, mesh=fine, in_specs=in_specs, out_specs=out_specs, check_vma=False)
```

```python
import functools

import jax
import jax.numpy as jnp
from jax import lax
from jax.experimental import pallas as pl
from jax.experimental.pallas import tpu as pltpu
from jax.sharding import Mesh, PartitionSpec as P

BF16 = jnp.bfloat16
F32 = jnp.float32
COUNT_BASE = 256.0
HEAD = 16


def corridor_table(edge_ids, edge_count):
    columns = jnp.arange(edge_count, dtype=jnp.int32)
    return jnp.sum((edge_ids[:, :, None] == columns[None, None, :]).astype(F32), axis=1)


def dest_operator(dst_edges, dst_weight):
    dst_member = corridor_table(dst_edges, dst_weight.shape[0])
    dst_degree = jnp.sum(dst_member * dst_weight[None, :], axis=1)
    edge_sizes = jnp.sum(dst_member, axis=0)
    left_factor = dst_member * lax.rsqrt(dst_degree)[:, None]
    right_factor = left_factor * (dst_weight / edge_sizes)[None, :]
    result = jnp.dot(right_factor, left_factor.T, precision=lax.Precision.HIGHEST)
    return result.astype(BF16)


class Plan:
    def __init__(self, zones, edges, own, rest, line):
        self.edges = edges
        self.own = own
        self.rest = rest
        self.line = line
        self.cut = zones // 2
        self.first_rows = self.cut * own
        self.second_rows = HEAD + (zones - self.cut) * own

        self.relative = own % 8 == 0

    def device(self, square, line):
        core, near, mid = square % 2, square // 2 % 2, square // 4
        if isinstance(line, int):
            slow, rest = line // self.rest, line % self.rest
        else:
            slow, rest = lax.div(line, self.rest), lax.rem(line, self.rest)
        return (((slow * 2 + mid) * self.rest + rest) * 2 + near) * 2 + core


def halves_of(counts):
    high = jnp.floor(counts * (1.0 / COUNT_BASE))
    return high, counts - high * COUNT_BASE


def head_rows(high, low):
    parts = [high, low]
    if high.shape[0] < HEAD // 2:
        pad = jnp.zeros((HEAD // 2 - high.shape[0], high.shape[1]), F32)
        parts = [high, pad, low, pad]
    return jnp.concatenate(parts, axis=0).astype(BF16)


def one_hot(edges_ref, weight_ref, edges, lanes):
    ids = edges_ref[...]
    rows = ids.shape[1]
    columns = lax.broadcasted_iota(jnp.int32, (edges, rows), 0)
    member = columns == ids[0:1, :]
    for j in range(1, ids.shape[0]):
        member = jnp.logical_or(member, columns == ids[j : j + 1, :])
    upright = jnp.transpose(jnp.broadcast_to(weight_ref[...], (lanes, edges)))
    upright = jnp.concatenate([upright] * (rows // lanes), axis=1)
    root = lax.rsqrt(jnp.sum(jnp.where(member, upright, 0.0), axis=0, keepdims=True))
    rounded = root.astype(BF16).astype(F32)
    weighted = jnp.where(member, rounded, 0.0).astype(BF16)
    hot = jnp.where(member, 1.0, 0.0).astype(BF16)
    return root, weighted, jnp.dot(hot, jnp.ones((rows, lanes), BF16), preferred_element_type=F32)


def accumulate(weighted, cells_ref, begin, zones, pitch, total_ref, wide_ref):
    rows, _, lanes = cells_ref.shape
    part = 32

    def widen(i, carry):
        first = i * part
        piece = cells_ref[pl.ds(first, part), begin : begin + zones, :].astype(F32)
        for j in range(part):
            wide_ref[pl.ds(pl.multiple_of((first + j) * pitch, 8), zones), :] = piece[j]
        return carry

    lax.fori_loop(0, rows // part, widen, 0)
    for pair in range(zones // 2):
        left = wide_ref[pl.ds(2 * pair, rows, stride=pitch), :].astype(BF16)
        right = wide_ref[pl.ds(2 * pair + 1, rows, stride=pitch), :].astype(BF16)
        both = jnp.concatenate([left, right], axis=1)
        total_ref[pair] += jnp.dot(weighted, both, preferred_element_type=F32)


def columns_of(total_ref, at, zones, lanes):
    data = []
    for d in range(zones):
        data.append(total_ref[d // 2, at, (d % 2) * lanes : (d % 2 + 1) * lanes])
    return jnp.concatenate(data, axis=0).astype(BF16)


def rows_for(plan, square, shift, line_ref):
    own = plan.own
    if plan.relative:
        device = plan.device(square, lax.rem(line_ref[0] + shift, plan.line))
        return pl.ds(pl.multiple_of(device * own, own), own)
    device = plan.device(square, shift)
    return slice(device * own, (device + 1) * own)


def second_kernel(plan, begin, zones, pitch, line_ref, edges_ref, weight_ref, cells_ref, *refs):
    out_refs = refs[: plan.line]
    root_ref, weighted_ref, total_ref, count_ref, wide_ref = refs[plan.line :]
    lanes = cells_ref.shape[2]

    @pl.when(pl.program_id(0) == 0)
    def _():
        total_ref[...] = jnp.zeros_like(total_ref)
        count_ref[...] = jnp.zeros_like(count_ref)

    root, weighted, counts = one_hot(edges_ref, weight_ref, total_ref.shape[1], lanes)
    root_ref[...] = root
    weighted_ref[...] = weighted
    count_ref[...] += counts
    accumulate(weighted, cells_ref, begin, zones, pitch, total_ref, wide_ref)

    @pl.when(pl.program_id(0) == pl.num_programs(0) - 1)
    def _():
        for square in range(8):
            for shift in range(plan.line):
                at = rows_for(plan, square, shift, line_ref)
                out_refs[shift][square, HEAD:, :] = columns_of(total_ref, at, zones, lanes)
                out_refs[shift][square, 0:HEAD, :] = head_rows(*halves_of(count_ref[at, :]))


def first_kernel(plan, begin, zones, pitch, line_ref, weighted_ref, cells_ref, out_ref, total_ref, wide_ref):
    @pl.when(pl.program_id(0) == 0)
    def _():
        total_ref[...] = jnp.zeros_like(total_ref)

    accumulate(weighted_ref[...], cells_ref, begin, zones, pitch, total_ref, wide_ref)

    @pl.when(pl.program_id(0) == pl.num_programs(0) - 1)
    def _():
        for square in range(8):
            for shift in range(plan.line):
                at = rows_for(plan, square, shift, line_ref)
                out_ref[square, shift] = columns_of(total_ref, at, zones, cells_ref.shape[2])


def fixed(shape):
    return pl.BlockSpec(shape, lambda i: (0,) * len(shape))


def half_sums(kernel, plan, part, line, cells, operands, specs, outs, out_specs, counted):
    anchors, zones, lanes = cells.shape
    edges = plan.edges
    half = zones // 2
    rows = min(512, anchors)
    pitch = -(-half // 8) * 8 + 8
    if half % 16 == 0:
        block, begin = pl.BlockSpec((rows, half, lanes), lambda i: (i, part, 0)), 0
    else:
        block, begin = pl.BlockSpec((rows, zones, lanes), lambda i: (i, 0, 0)), part * half
    counts = [pltpu.VMEM((edges, lanes), F32)] if counted else []
    return pl.pallas_call(
        functools.partial(kernel, plan, begin, half, pitch),
        grid=(anchors // rows,),
        in_specs=[pl.BlockSpec(memory_space=pltpu.SMEM)] + specs + [block],
        out_specs=out_specs,
        out_shape=outs,
        scratch_shapes=[pltpu.VMEM((half // 2, edges, 2 * lanes), F32)] + counts + [pltpu.VMEM((rows * pitch, lanes), F32)],
        compiler_params=pltpu.CompilerParams(vmem_limit_bytes=40 * 1024 * 1024),
        cost_estimate=pl.CostEstimate(
            flops=4 * anchors * edges * zones * lanes, bytes_accessed=2 * anchors * zones * lanes, transcendentals=0
        ),
    )(line[None], *operands, cells)


def second_sums(line, cells, edges_t, edge_weight, plan):
    anchors, _, lanes = cells.shape
    rows = min(512, anchors)
    edges = plan.edges
    shape = (8, plan.second_rows, lanes)
    outs = [jax.ShapeDtypeStruct(shape, BF16)] * plan.line
    outs += [jax.ShapeDtypeStruct((1, anchors), F32), jax.ShapeDtypeStruct((edges, anchors), BF16)]
    out_specs = [fixed(shape)] * plan.line
    out_specs += [pl.BlockSpec((1, rows), lambda i: (0, i)), pl.BlockSpec((edges, rows), lambda i: (0, i))]
    specs = [pl.BlockSpec((edges_t.shape[0], rows), lambda i: (0, i)), fixed((1, edges))]
    operands = (edges_t, edge_weight[None, :])
    *seconds, roots, weighted = half_sums(second_kernel, plan, 1, line, cells, operands, specs, outs, out_specs, True)
    if not plan.relative:
        seconds = jnp.stack(seconds * 2)
        seconds = [lax.dynamic_index_in_dim(seconds, line + k, 0, keepdims=False) for k in range(plan.line)]
    return seconds, roots, weighted


def first_sums(line, cells, weighted, plan):
    rows = min(512, cells.shape[0])
    shape = (8, plan.line, plan.first_rows, cells.shape[2])
    specs = [pl.BlockSpec((plan.edges, rows), lambda i: (0, i))]
    out = jax.ShapeDtypeStruct(shape, BF16)
    first = half_sums(first_kernel, plan, 0, line, cells, (weighted,), specs, out, fixed(shape), False)
    if not plan.relative:
        first = lax.dynamic_slice_in_dim(jnp.concatenate([first, first], axis=1), line, plan.line, 1)
    return first


def add_up(pieces):
    total = pieces[0].astype(F32)
    for piece in pieces[1:]:
        total = total + piece.astype(F32)
    return total


def fold_first_kernel(plan, part_ref, *outs):
    for shift in range(plan.line):
        for quarter in range(4):
            outs[shift][quarter] = add_up([part_ref[quarter, shift], part_ref[4 + quarter, shift]]).astype(BF16)


def fold_second_kernel(plan, *refs):
    parts, out_ref = refs[: plan.line], refs[plan.line]
    for square in range(8):
        for rest in range(plan.rest):
            total = add_up([parts[shift][square] for shift in range(rest, plan.line, plan.rest)])
            half = HEAD // 2
            out_ref[square, rest, 0:HEAD, :] = head_rows(*halves_of(total[0:half] * COUNT_BASE + total[half:HEAD]))
            out_ref[square, rest, HEAD:, :] = total[HEAD:].astype(BF16)


def fold(kernel, plan, parts, shapes):
    whole = pl.BlockSpec(memory_space=pltpu.VMEM)
    size = sum(part.size for part in parts)
    return pl.pallas_call(
        functools.partial(kernel, plan),
        in_specs=[whole] * len(parts),
        out_specs=[whole] * len(shapes),
        out_shape=[jax.ShapeDtypeStruct(shape, BF16) for shape in shapes],
        compiler_params=pltpu.CompilerParams(vmem_limit_bytes=16 * 1024 * 1024),
        cost_estimate=pl.CostEstimate(flops=size, bytes_accessed=size * 4, transcendentals=0),
    )(*parts)


def org_sums(line, cells, edges_t, edge_weight, plan):
    lanes = cells.shape[-1]
    seconds, roots, weighted = second_sums(line, cells, edges_t, edge_weight, plan)
    seconds = [shifted(part, shift) if shift else part for shift, part in enumerate(seconds)]
    first = first_sums(line, cells, weighted, plan)
    first = lax.all_to_all(first, SQUARE, split_axis=0, concat_axis=0, tiled=True)
    second = fold(fold_second_kernel, plan, seconds, [(8, plan.rest, plan.second_rows, lanes)])[0]
    firsts = fold(fold_first_kernel, plan, [first], [(4, plan.first_rows, lanes)] * plan.line)
    firsts = [shifted(part, shift) if shift else part for shift, part in enumerate(firsts)]
    second = lax.all_to_all(second, SQUARE, split_axis=0, concat_axis=0, tiled=True)
    return firsts, second, roots


def table_kernel(plan, weight_ref, mixing_ref, matrix_ref, *refs):
    firsts = refs[: plan.line]
    second_ref, keep_ref, give_ref, mixed_ref = refs[plan.line :]
    own = plan.own
    lanes = mixing_ref.shape[0]
    half = HEAD // 2
    head = add_up([second_ref[0, 0, 0:HEAD, :], second_ref[4, 0, 0:HEAD, :]])
    counts = head[0:half] * COUNT_BASE + head[half:HEAD]
    scale = weight_ref[...] / counts[0:own]
    rows = plan.first_rows + plan.second_rows - HEAD
    zones = rows // own
    n_dst = 4 * plan.rest
    for k in range(n_dst):
        rest, quarter = k // 4, k % 4
        first = add_up([firsts[shift][quarter] for shift in range(rest, plan.line, plan.rest)])
        second = add_up([second_ref[quarter, rest, HEAD:, :], second_ref[4 + quarter, rest, HEAD:, :]])
        start = k * rows
        for total in (first, second):
            size = total.shape[0]
            totals = (total * jnp.concatenate([scale] * (size // own), axis=0)).astype(BF16)
            mixed = jnp.dot(totals, mixing_ref[...], preferred_element_type=F32)
            mixed_ref[start : start + size, :] = mixed
            start += size
    whole = n_dst * zones
    for e in range(own):
        mixed = mixed_ref[pl.ds(e, whole, stride=own), :] if own > 1 else mixed_ref[...]
        high = mixed.astype(BF16)
        low = (mixed - high.astype(F32)).astype(BF16)
        both = jnp.dot(matrix_ref[...], jnp.concatenate([high, low], axis=1), preferred_element_type=F32)
        result = (both[:, 0:lanes] + both[:, lanes : 2 * lanes]).astype(BF16)
        keep_ref[e] = result[0 : whole // 2]
        give_ref[e] = result[whole // 2 :]


def table_rows(firsts, second, weight_rows, mixing, matrix, plan):
    zones = matrix.shape[0]
    lanes = mixing.shape[0]
    whole = pl.BlockSpec(memory_space=pltpu.VMEM)
    half = jax.ShapeDtypeStruct((plan.own, zones // 2, lanes), BF16)
    return pl.pallas_call(
        functools.partial(table_kernel, plan),
        in_specs=[whole] * (4 + len(firsts)),
        out_specs=[whole] * 2,
        out_shape=[half, half],
        scratch_shapes=[pltpu.VMEM((zones * plan.own, lanes), F32)],
        compiler_params=pltpu.CompilerParams(vmem_limit_bytes=32 * 1024 * 1024),
        cost_estimate=pl.CostEstimate(
            flops=8 * plan.own * zones * lanes * lanes, bytes_accessed=4 * zones * plan.own * lanes, transcendentals=0
        ),
    )(weight_rows, mixing, matrix, *firsts, second)


def spread_kernel(n_long, n_short, half_ref, places_ref, root_ref, bias_ref, *refs):
    longs = refs[:n_long]
    shorts = refs[n_long : n_long + n_short]
    out_ref, table_ref, ring_ref, sems, ring_sems = refs[-5:]
    slots, rows, zones, lanes = ring_ref.shape
    steps = out_ref.shape[0] // rows
    half = half_ref[0]

    copies = []

    def bring(source, first, start):
        place = table_ref.at[pl.ds(first, source.shape[0]), pl.ds(start, source.shape[1]), :]
        copies.append(pltpu.make_async_copy(source, place, sems.at[len(copies)]))

    split = longs[0].shape[1]
    size = shorts[0].shape[0] // n_long
    for square, source in enumerate(longs):
        bring(source, square * n_short * size, 0)
    for shift, source in enumerate(shorts):
        for square in range(n_long):
            bring(source.at[pl.ds(square * size, size)], (square * n_short + shift) * size, split)
    for copy in copies:
        copy.start()
    for copy in copies:
        copy.wait()

    bias = bias_ref[...]
    count = places_ref.shape[0]
    tile = 16
    batch = min(8, rows)
    tiles = zones // tile

    def leaving(step, slot):
        place = out_ref.at[pl.ds(step * rows, rows), pl.ds(pl.multiple_of(half * zones, zones), zones), :]
        return pltpu.make_async_copy(ring_ref.at[slot], place, ring_sems.at[slot])

    def one_step(step, carry):
        slot = lax.rem(step, slots)

        @pl.when(step >= slots)
        def _():
            leaving(step - slots, slot).wait()

        def several(group, inner):
            values = []
            for i in range(batch):
                at = step * rows + group * batch + i
                scale = root_ref[0, at]
                spots = [places_ref[j, at] for j in range(count)]
                for first in range(0, zones, tile):
                    pieces = [table_ref[spot, first : first + tile, :] for spot in spots]
                    pieces = [(a + b).astype(F32) for a, b in zip(pieces[0::2], pieces[1::2])]
                    total = sum(pieces[1:], pieces[0])
                    values.append(jnp.maximum((total * scale + bias).astype(BF16), BF16(0.0)))
            for n, value in enumerate(values):
                start = n % tiles * tile
                ring_ref[slot, group * batch + n // tiles, start : start + tile, :] = value
            return inner

        lax.fori_loop(0, rows // batch, several, 0)
        leaving(step, slot).start()
        return carry

    lax.fori_loop(0, steps, one_step, 0)
    for step in range(steps - slots, steps):
        leaving(step, step % slots).wait()


def spread(half, places, root, bias, longs, shorts, before=None):
    anchors = places.shape[1]
    lanes = bias.shape[1]
    zones = longs[0].shape[1] + shorts[0].shape[1]
    rows = min(16, anchors // 8)
    slots = min(8, anchors // rows)
    smem = pl.BlockSpec(memory_space=pltpu.SMEM)
    anywhere = pl.BlockSpec(memory_space=pltpu.HBM)
    pieces = longs + shorts
    operands = [half, places, root, bias] + pieces
    specs = [smem, smem, smem, pl.BlockSpec(memory_space=pltpu.VMEM)] + [anywhere] * len(pieces)
    aliases = {}
    if before is not None:
        aliases = {len(operands): 0}
        operands.append(before)
        specs.append(anywhere)
    return pl.pallas_call(
        functools.partial(spread_kernel, len(longs), len(shorts)),
        in_specs=specs,
        out_specs=anywhere,
        out_shape=jax.ShapeDtypeStruct((anchors, 2 * zones, lanes), BF16),
        scratch_shapes=[
            pltpu.VMEM((len(longs) * longs[0].shape[0], zones, lanes), BF16),
            pltpu.VMEM((slots, rows, zones, lanes), BF16),
            pltpu.SemaphoreType.DMA((len(longs) * (1 + len(shorts)),)),
            pltpu.SemaphoreType.DMA((slots,)),
        ],
        input_output_aliases=aliases,
        compiler_params=pltpu.CompilerParams(vmem_limit_bytes=24 * 1024 * 1024),
        cost_estimate=pl.CostEstimate(
            flops=4096 * anchors * zones * lanes, bytes_accessed=4 * anchors * zones * lanes, transcendentals=0
        ),
    )(*operands)


LINE = ("slow", "rest")
SQUARE = ("mid", "near", "core")


def shifted(x, amount):
    size = lax.axis_size(LINE)
    return lax.ppermute(x, LINE, [(i, (i + amount) % size) for i in range(size)])


def crossed(x, turn):
    pairs = []
    for device in range(8):
        core = device % 2
        pairs.append((device, device ^ (2 if core == turn else 4)))
    return lax.ppermute(x, SQUARE, pairs)


def masked(x, mask):
    return lax.ppermute(x, SQUARE, [(device, device ^ mask) for device in range(8)])


def swapped(x):
    return lax.ppermute(x, "core", [(0, 1), (1, 0)])


def gather_table(keep, give):
    size = lax.axis_size(LINE)
    block = jnp.concatenate([keep, swapped(give)], axis=0)
    split = block.shape[1] * 3 // 4
    long, short = block[:, :split], block[:, split:]
    line = [long] + [shifted(long, k) for k in range(1, size)]
    short = jnp.concatenate([short, crossed(short, 0), crossed(short, 1), masked(short, 6)], axis=0)
    long = jnp.concatenate(line, axis=0)
    short, long = lax.optimization_barrier((short, long))
    first = crossed(long, 0)
    second = crossed(long, 1)
    shorts = [short] + [shifted(short, k) for k in range(1, size)]
    first, *shorts[1:-1] = lax.optimization_barrier((first, *shorts[1:-1]))
    both = crossed(first, 1)
    return [long, first, second, both], shorts


def places_of(ids, core, own):
    rest, size = lax.axis_size("rest"), lax.axis_size(LINE)
    owner = ids // own
    slot = jnp.where(owner % 2 == core, 0, own) + ids % own
    near = jnp.bitwise_xor(owner // 2 % 2, lax.axis_index("near"))
    mid = jnp.bitwise_xor(owner // (4 * rest) % 2, lax.axis_index("mid"))
    line = owner // (8 * rest) * rest + owner // 4 % rest
    line = lax.rem(lax.axis_index(LINE) - line + size, size)
    square = jnp.where(core == 0, 2 * mid + near, 2 * near + mid)
    return (square * size + line) * (2 * own) + slot


def relative_columns(matrix):
    zones, rest = matrix.shape[0], lax.axis_size("rest")
    if rest == 1:
        return matrix
    back = jnp.flip(matrix.reshape(zones, rest, -1), 1)
    back = jnp.concatenate([back, back], axis=1)
    return lax.dynamic_slice_in_dim(back, rest - 1 - lax.axis_index("rest"), rest, 1).reshape(zones, zones)


def shards(od_cells, anchor_edges, edge_weight, mixing, dst_edges, dst_weight, out_bias):
    n_org = lax.axis_size("slow") * lax.axis_size("mid")
    n_dst = lax.axis_size("rest") * lax.axis_size("near") * lax.axis_size("core")
    own = edge_weight.shape[0] // (n_org * n_dst)
    everyone = ("slow", "mid", "rest", "near", "core")
    core = lax.axis_index("core")
    edges_t = anchor_edges.T
    plan = Plan(od_cells.shape[1], edge_weight.shape[0], own, lax.axis_size("rest"), lax.axis_size(LINE))
    firsts, second, roots = org_sums(lax.axis_index(LINE), od_cells, edges_t, edge_weight, plan)
    own_weight = lax.dynamic_slice_in_dim(edge_weight, lax.axis_index(everyone) * own, own, 0)
    weight_rows = jnp.broadcast_to(own_weight[:, None], (own, mixing.shape[0]))
    matrix = relative_columns(dest_operator(dst_edges, dst_weight))
    half = matrix.shape[0] // 2
    matrix = jnp.where(core == 0, matrix, jnp.concatenate([matrix[half:], matrix[:half]], axis=0))
    keep, give = table_rows(firsts, second, weight_rows, mixing, matrix, plan)
    longs, shorts = gather_table(keep, give)
    rows = anchor_edges.shape[0] // n_dst
    start = lax.axis_index(("rest", "near", "core")) * rows
    ids = lax.dynamic_slice_in_dim(edges_t, start, rows, 1)
    own_root = lax.dynamic_slice_in_dim(roots, start, rows, 1)
    bias = out_bias[None, :]
    other = 1 - core
    result = spread(core[None], places_of(ids, core, own), own_root, bias, longs, shorts)
    longs, shorts = [swapped(x) for x in longs], [swapped(x) for x in shorts]
    return spread(other[None], places_of(ids, other, own), own_root, bias, longs, shorts, result)


def solution(mesh):
    n_org, n_dst = mesh.devices.shape
    fine = Mesh(mesh.devices.reshape(n_org // 2, 2, n_dst // 4, 2, 2), ("slow", "mid", "rest", "near", "core"))
    org, dst = ("slow", "mid"), ("rest", "near", "core")
    in_specs = (P(org, dst, None), P(org, None), P(), P(), P(), P(), P())
    out_specs = P(org + dst, None, None)
    return jax.shard_map(shards, mesh=fine, in_specs=in_specs, out_specs=out_specs, check_vma=False)
```

```python
import functools

import jax
import jax.numpy as jnp
from jax import lax
from jax.experimental import pallas as pl
from jax.experimental.pallas import tpu as pltpu
from jax.sharding import Mesh, PartitionSpec as P

BF16 = jnp.bfloat16
F32 = jnp.float32
COUNT_BASE = 256.0
HEAD = 16


def corridor_table(edge_ids, edge_count):
    columns = jnp.arange(edge_count, dtype=jnp.int32)
    return jnp.sum((edge_ids[:, :, None] == columns[None, None, :]).astype(F32), axis=1)


def dest_operator(dst_edges, dst_weight):
    dst_member = corridor_table(dst_edges, dst_weight.shape[0])
    dst_degree = jnp.sum(dst_member * dst_weight[None, :], axis=1)
    edge_sizes = jnp.sum(dst_member, axis=0)
    left_factor = dst_member * lax.rsqrt(dst_degree)[:, None]
    right_factor = left_factor * (dst_weight / edge_sizes)[None, :]
    result = jnp.dot(right_factor, left_factor.T, precision=lax.Precision.HIGHEST)
    return result.astype(BF16)


class Plan:
    def __init__(self, zones, edges, own, rest, line):
        self.edges = edges
        self.own = own
        self.rest = rest
        self.line = line
        self.cut = zones // 2
        self.first_rows = self.cut * own
        self.second_rows = HEAD + (zones - self.cut) * own

        self.relative = own % 8 == 0

    def device(self, square, line):
        core, near, mid = square % 2, square // 2 % 2, square // 4
        if isinstance(line, int):
            slow, rest = line // self.rest, line % self.rest
        else:
            slow, rest = lax.div(line, self.rest), lax.rem(line, self.rest)
        return (((slow * 2 + mid) * self.rest + rest) * 2 + near) * 2 + core


def halves_of(counts):
    high = jnp.floor(counts * (1.0 / COUNT_BASE))
    return high, counts - high * COUNT_BASE


def head_rows(high, low):
    parts = [high, low]
    if high.shape[0] < HEAD // 2:
        pad = jnp.zeros((HEAD // 2 - high.shape[0], high.shape[1]), F32)
        parts = [high, pad, low, pad]
    return jnp.concatenate(parts, axis=0).astype(BF16)


def one_hot(edges_ref, weight_ref, edges, lanes):
    ids = edges_ref[...]
    rows = ids.shape[1]
    columns = lax.broadcasted_iota(jnp.int32, (edges, rows), 0)
    member = columns == ids[0:1, :]
    for j in range(1, ids.shape[0]):
        member = jnp.logical_or(member, columns == ids[j : j + 1, :])
    upright = jnp.transpose(jnp.broadcast_to(weight_ref[...], (lanes, edges)))
    upright = jnp.concatenate([upright] * (rows // lanes), axis=1)
    root = lax.rsqrt(jnp.sum(jnp.where(member, upright, 0.0), axis=0, keepdims=True))
    rounded = root.astype(BF16).astype(F32)
    weighted = jnp.where(member, rounded, 0.0).astype(BF16)
    hot = jnp.where(member, 1.0, 0.0).astype(BF16)
    return root, weighted, jnp.dot(hot, jnp.ones((rows, lanes), BF16), preferred_element_type=F32)


def accumulate(weighted, cells_ref, begin, zones, pitch, total_ref, wide_ref):
    rows, _, lanes = cells_ref.shape
    part = 32

    def widen(i, carry):
        first = i * part
        piece = cells_ref[pl.ds(first, part), begin : begin + zones, :].astype(F32)
        for j in range(part):
            wide_ref[pl.ds(pl.multiple_of((first + j) * pitch, 8), zones), :] = piece[j]
        return carry

    lax.fori_loop(0, rows // part, widen, 0)
    for pair in range(zones // 2):
        left = wide_ref[pl.ds(2 * pair, rows, stride=pitch), :].astype(BF16)
        right = wide_ref[pl.ds(2 * pair + 1, rows, stride=pitch), :].astype(BF16)
        both = jnp.concatenate([left, right], axis=1)
        total_ref[pair] += jnp.dot(weighted, both, preferred_element_type=F32)


def columns_of(total_ref, at, zones, lanes):
    data = []
    for d in range(zones):
        data.append(total_ref[d // 2, at, (d % 2) * lanes : (d % 2 + 1) * lanes])
    return jnp.concatenate(data, axis=0).astype(BF16)


def rows_for(plan, square, shift, line_ref):
    own = plan.own
    if plan.relative:
        device = plan.device(square, lax.rem(line_ref[0] + shift, plan.line))
        return pl.ds(pl.multiple_of(device * own, own), own)
    device = plan.device(square, shift)
    return slice(device * own, (device + 1) * own)


def second_kernel(plan, begin, zones, pitch, line_ref, edges_ref, weight_ref, cells_ref, *refs):
    out_refs = refs[: plan.line]
    root_ref, weighted_ref, total_ref, count_ref, wide_ref = refs[plan.line :]
    lanes = cells_ref.shape[2]

    @pl.when(pl.program_id(0) == 0)
    def _():
        total_ref[...] = jnp.zeros_like(total_ref)
        count_ref[...] = jnp.zeros_like(count_ref)

    root, weighted, counts = one_hot(edges_ref, weight_ref, total_ref.shape[1], lanes)
    root_ref[...] = root
    weighted_ref[...] = weighted
    count_ref[...] += counts
    accumulate(weighted, cells_ref, begin, zones, pitch, total_ref, wide_ref)

    @pl.when(pl.program_id(0) == pl.num_programs(0) - 1)
    def _():
        for square in range(8):
            for shift in range(plan.line):
                at = rows_for(plan, square, shift, line_ref)
                out_refs[shift][square, HEAD:, :] = columns_of(total_ref, at, zones, lanes)
                out_refs[shift][square, 0:HEAD, :] = head_rows(*halves_of(count_ref[at, :]))


def first_kernel(plan, begin, zones, pitch, line_ref, weighted_ref, cells_ref, out_ref, total_ref, wide_ref):
    @pl.when(pl.program_id(0) == 0)
    def _():
        total_ref[...] = jnp.zeros_like(total_ref)

    accumulate(weighted_ref[...], cells_ref, begin, zones, pitch, total_ref, wide_ref)

    @pl.when(pl.program_id(0) == pl.num_programs(0) - 1)
    def _():
        for square in range(8):
            for shift in range(plan.line):
                at = rows_for(plan, square, shift, line_ref)
                out_ref[square, shift] = columns_of(total_ref, at, zones, cells_ref.shape[2])


def fixed(shape):
    return pl.BlockSpec(shape, lambda i: (0,) * len(shape))


def half_sums(kernel, plan, part, line, cells, operands, specs, outs, out_specs, counted):
    anchors, zones, lanes = cells.shape
    edges = plan.edges
    half = zones // 2
    rows = min(512, anchors)
    pitch = -(-half // 8) * 8 + 8
    if half % 16 == 0:
        block, begin = pl.BlockSpec((rows, half, lanes), lambda i: (i, part, 0)), 0
    else:
        block, begin = pl.BlockSpec((rows, zones, lanes), lambda i: (i, 0, 0)), part * half
    counts = [pltpu.VMEM((edges, lanes), F32)] if counted else []
    return pl.pallas_call(
        functools.partial(kernel, plan, begin, half, pitch),
        grid=(anchors // rows,),
        in_specs=[pl.BlockSpec(memory_space=pltpu.SMEM)] + specs + [block],
        out_specs=out_specs,
        out_shape=outs,
        scratch_shapes=[pltpu.VMEM((half // 2, edges, 2 * lanes), F32)] + counts + [pltpu.VMEM((rows * pitch, lanes), F32)],
        compiler_params=pltpu.CompilerParams(vmem_limit_bytes=40 * 1024 * 1024),
        cost_estimate=pl.CostEstimate(
            flops=4 * anchors * edges * zones * lanes, bytes_accessed=2 * anchors * zones * lanes, transcendentals=0
        ),
    )(line[None], *operands, cells)


def second_sums(line, cells, edges_t, edge_weight, plan):
    anchors, _, lanes = cells.shape
    rows = min(512, anchors)
    edges = plan.edges
    shape = (8, plan.second_rows, lanes)
    outs = [jax.ShapeDtypeStruct(shape, BF16)] * plan.line
    outs += [jax.ShapeDtypeStruct((1, anchors), F32), jax.ShapeDtypeStruct((edges, anchors), BF16)]
    out_specs = [fixed(shape)] * plan.line
    out_specs += [pl.BlockSpec((1, rows), lambda i: (0, i)), pl.BlockSpec((edges, rows), lambda i: (0, i))]
    specs = [pl.BlockSpec((edges_t.shape[0], rows), lambda i: (0, i)), fixed((1, edges))]
    operands = (edges_t, edge_weight[None, :])
    *seconds, roots, weighted = half_sums(second_kernel, plan, 1, line, cells, operands, specs, outs, out_specs, True)
    if not plan.relative:
        seconds = jnp.stack(seconds * 2)
        seconds = [lax.dynamic_index_in_dim(seconds, line + k, 0, keepdims=False) for k in range(plan.line)]
    return seconds, roots, weighted


def first_sums(line, cells, weighted, plan):
    rows = min(512, cells.shape[0])
    shape = (8, plan.line, plan.first_rows, cells.shape[2])
    specs = [pl.BlockSpec((plan.edges, rows), lambda i: (0, i))]
    out = jax.ShapeDtypeStruct(shape, BF16)
    first = half_sums(first_kernel, plan, 0, line, cells, (weighted,), specs, out, fixed(shape), False)
    if not plan.relative:
        first = lax.dynamic_slice_in_dim(jnp.concatenate([first, first], axis=1), line, plan.line, 1)
    return first


def add_up(pieces):
    total = pieces[0].astype(F32)
    for piece in pieces[1:]:
        total = total + piece.astype(F32)
    return total


def fold_first_kernel(plan, part_ref, *outs):
    for shift in range(plan.line):
        for quarter in range(4):
            outs[shift][quarter] = add_up([part_ref[quarter, shift], part_ref[4 + quarter, shift]]).astype(BF16)


def fold_second_kernel(plan, *refs):
    parts, out_ref = refs[: plan.line], refs[plan.line]
    for square in range(8):
        for rest in range(plan.rest):
            total = add_up([parts[shift][square] for shift in range(rest, plan.line, plan.rest)])
            half = HEAD // 2
            out_ref[square, rest, 0:HEAD, :] = head_rows(*halves_of(total[0:half] * COUNT_BASE + total[half:HEAD]))
            out_ref[square, rest, HEAD:, :] = total[HEAD:].astype(BF16)


def fold(kernel, plan, parts, shapes):
    whole = pl.BlockSpec(memory_space=pltpu.VMEM)
    size = sum(part.size for part in parts)
    return pl.pallas_call(
        functools.partial(kernel, plan),
        in_specs=[whole] * len(parts),
        out_specs=[whole] * len(shapes),
        out_shape=[jax.ShapeDtypeStruct(shape, BF16) for shape in shapes],
        compiler_params=pltpu.CompilerParams(vmem_limit_bytes=16 * 1024 * 1024),
        cost_estimate=pl.CostEstimate(flops=size, bytes_accessed=size * 4, transcendentals=0),
    )(*parts)


def org_sums(line, cells, edges_t, edge_weight, plan):
    lanes = cells.shape[-1]
    seconds, roots, weighted = second_sums(line, cells, edges_t, edge_weight, plan)
    seconds = [shifted(part, shift) if shift else part for shift, part in enumerate(seconds)]
    first = first_sums(line, cells, weighted, plan)
    first, *seconds[1::2] = lax.optimization_barrier((first, *seconds[1::2]))
    first = lax.all_to_all(first, SQUARE, split_axis=0, concat_axis=0, tiled=True)
    second = fold(fold_second_kernel, plan, seconds, [(8, plan.rest, plan.second_rows, lanes)])[0]
    firsts = fold(fold_first_kernel, plan, [first], [(4, plan.first_rows, lanes)] * plan.line)
    firsts = [shifted(part, shift) if shift else part for shift, part in enumerate(firsts)]
    second = lax.all_to_all(second, SQUARE, split_axis=0, concat_axis=0, tiled=True)
    return firsts, second, roots


def table_kernel(plan, weight_ref, mixing_ref, matrix_ref, *refs):
    firsts = refs[: plan.line]
    second_ref, keep_ref, give_ref, mixed_ref = refs[plan.line :]
    own = plan.own
    lanes = mixing_ref.shape[0]
    half = HEAD // 2
    head = add_up([second_ref[0, 0, 0:HEAD, :], second_ref[4, 0, 0:HEAD, :]])
    counts = head[0:half] * COUNT_BASE + head[half:HEAD]
    scale = weight_ref[...] / counts[0:own]
    rows = plan.first_rows + plan.second_rows - HEAD
    zones = rows // own
    n_dst = 4 * plan.rest
    for k in range(n_dst):
        rest, quarter = k // 4, k % 4
        first = add_up([firsts[shift][quarter] for shift in range(rest, plan.line, plan.rest)])
        second = add_up([second_ref[quarter, rest, HEAD:, :], second_ref[4 + quarter, rest, HEAD:, :]])
        start = k * rows
        for total in (first, second):
            size = total.shape[0]
            totals = (total * jnp.concatenate([scale] * (size // own), axis=0)).astype(BF16)
            mixed = jnp.dot(totals, mixing_ref[...], preferred_element_type=F32)
            mixed_ref[start : start + size, :] = mixed
            start += size
    whole = n_dst * zones
    for e in range(own):
        mixed = mixed_ref[pl.ds(e, whole, stride=own), :] if own > 1 else mixed_ref[...]
        high = mixed.astype(BF16)
        low = (mixed - high.astype(F32)).astype(BF16)
        both = jnp.dot(matrix_ref[...], jnp.concatenate([high, low], axis=1), preferred_element_type=F32)
        result = (both[:, 0:lanes] + both[:, lanes : 2 * lanes]).astype(BF16)
        keep_ref[e] = result[0 : whole // 2]
        give_ref[e] = result[whole // 2 :]


def table_rows(firsts, second, weight_rows, mixing, matrix, plan):
    zones = matrix.shape[0]
    lanes = mixing.shape[0]
    whole = pl.BlockSpec(memory_space=pltpu.VMEM)
    half = jax.ShapeDtypeStruct((plan.own, zones // 2, lanes), BF16)
    return pl.pallas_call(
        functools.partial(table_kernel, plan),
        in_specs=[whole] * (4 + len(firsts)),
        out_specs=[whole] * 2,
        out_shape=[half, half],
        scratch_shapes=[pltpu.VMEM((zones * plan.own, lanes), F32)],
        compiler_params=pltpu.CompilerParams(vmem_limit_bytes=32 * 1024 * 1024),
        cost_estimate=pl.CostEstimate(
            flops=8 * plan.own * zones * lanes * lanes, bytes_accessed=4 * zones * plan.own * lanes, transcendentals=0
        ),
    )(weight_rows, mixing, matrix, *firsts, second)


def spread_kernel(n_pieces, stride, offset, half_ref, places_ref, root_ref, bias_ref, *refs):
    out_ref, table_ref, ring_ref, sems, ring_sems = refs[-5:]
    slots, rows, zones, lanes = ring_ref.shape
    steps = out_ref.shape[0] // rows
    first_zone = pl.multiple_of(half_ref[0] * stride + offset, 16)

    copies = []
    for i, source in enumerate(refs[:n_pieces]):
        size = source.shape[0]
        copies.append(pltpu.make_async_copy(source, table_ref.at[pl.ds(i * size, size)], sems.at[i]))
    for copy in copies:
        copy.start()
    for copy in copies:
        copy.wait()

    bias = bias_ref[...]
    count = places_ref.shape[0]
    tile = 16
    batch = min(8 if zones > tile else 16, rows)
    tiles = zones // tile

    def leaving(step, slot):
        place = out_ref.at[pl.ds(step * rows, rows), pl.ds(first_zone, zones), :]
        return pltpu.make_async_copy(ring_ref.at[slot], place, ring_sems.at[slot])

    def one_step(step, carry):
        slot = lax.rem(step, slots)

        @pl.when(step >= slots)
        def _():
            leaving(step - slots, slot).wait()

        def several(group, inner):
            values = []
            for i in range(batch):
                at = step * rows + group * batch + i
                scale = root_ref[0, at]
                spots = [places_ref[j, at] for j in range(count)]
                for first in range(0, zones, tile):
                    pieces = [table_ref[spot, first : first + tile, :] for spot in spots]
                    pieces = [(a + b).astype(F32) for a, b in zip(pieces[0::2], pieces[1::2])]
                    total = sum(pieces[1:], pieces[0])
                    values.append(jnp.maximum((total * scale + bias).astype(BF16), BF16(0.0)))
            for n, value in enumerate(values):
                start = n % tiles * tile
                ring_ref[slot, group * batch + n // tiles, start : start + tile, :] = value
            return inner

        lax.fori_loop(0, rows // batch, several, 0)
        leaving(step, slot).start()
        return carry

    lax.fori_loop(0, steps, one_step, 0)
    for step in range(steps - slots, steps):
        leaving(step, step % slots).wait()


def spread(half, places, root, bias, pieces, offset, stride, before=None):
    anchors = places.shape[1]
    lanes = bias.shape[1]
    zones = pieces[0].shape[1]
    rows = min(16, anchors // 8)
    slots = min(8, anchors // rows)
    smem = pl.BlockSpec(memory_space=pltpu.SMEM)
    anywhere = pl.BlockSpec(memory_space=pltpu.HBM)
    operands = [half, places, root, bias] + pieces
    specs = [smem, smem, smem, pl.BlockSpec(memory_space=pltpu.VMEM)] + [anywhere] * len(pieces)
    aliases = {}
    if before is not None:
        aliases = {len(operands): 0}
        operands.append(before)
        specs.append(anywhere)
    return pl.pallas_call(
        functools.partial(spread_kernel, len(pieces), stride, offset),
        in_specs=specs,
        out_specs=anywhere,
        out_shape=jax.ShapeDtypeStruct((anchors, 2 * stride, lanes), BF16),
        scratch_shapes=[
            pltpu.VMEM((len(pieces) * pieces[0].shape[0], zones, lanes), BF16),
            pltpu.VMEM((slots, rows, zones, lanes), BF16),
            pltpu.SemaphoreType.DMA((len(pieces),)),
            pltpu.SemaphoreType.DMA((slots,)),
        ],
        input_output_aliases=aliases,
        compiler_params=pltpu.CompilerParams(vmem_limit_bytes=24 * 1024 * 1024),
        cost_estimate=pl.CostEstimate(
            flops=4096 * anchors * zones * lanes, bytes_accessed=4 * anchors * zones * lanes, transcendentals=0
        ),
    )(*operands)


LINE = ("slow", "rest")
SQUARE = ("mid", "near", "core")


def shifted(x, amount):
    size = lax.axis_size(LINE)
    return lax.ppermute(x, LINE, [(i, (i + amount) % size) for i in range(size)])


def crossed(x, turn):
    pairs = []
    for device in range(8):
        core = device % 2
        pairs.append((device, device ^ (2 if core == turn else 4)))
    return lax.ppermute(x, SQUARE, pairs)


def masked(x, mask):
    return lax.ppermute(x, SQUARE, [(device, device ^ mask) for device in range(8)])


def swapped(x):
    return lax.ppermute(x, "core", [(0, 1), (1, 0)])


def gather_table(keep, give):
    size = lax.axis_size(LINE)
    block = jnp.concatenate([keep, swapped(give)], axis=0)
    split = block.shape[1] * 3 // 4
    long, short = block[:, :split], block[:, split:]
    line = [long] + [shifted(long, k) for k in range(1, size)]
    short = jnp.concatenate([short, crossed(short, 0), crossed(short, 1), masked(short, 6)], axis=0)
    long = jnp.concatenate(line, axis=0)
    short, long = lax.optimization_barrier((short, long))
    first = crossed(long, 0)
    second = crossed(long, 1)
    shorts = [short] + [shifted(short, k) for k in range(1, size)]
    first, *shorts[1:-1] = lax.optimization_barrier((first, *shorts[1:-1]))
    both = crossed(first, 1)
    return [long, first, second, both], shorts


def places_of(ids, core, own):
    rest, size = lax.axis_size("rest"), lax.axis_size(LINE)
    owner = ids // own
    slot = jnp.where(owner % 2 == core, 0, own) + ids % own
    near = jnp.bitwise_xor(owner // 2 % 2, lax.axis_index("near"))
    mid = jnp.bitwise_xor(owner // (4 * rest) % 2, lax.axis_index("mid"))
    line = owner // (8 * rest) * rest + owner // 4 % rest
    line = lax.rem(lax.axis_index(LINE) - line + size, size)
    square = jnp.where(core == 0, 2 * mid + near, 2 * near + mid)
    return (square * size + line) * (2 * own) + slot, (line * 4 + square) * (2 * own) + slot


def relative_columns(matrix):
    zones, rest = matrix.shape[0], lax.axis_size("rest")
    if rest == 1:
        return matrix
    back = jnp.flip(matrix.reshape(zones, rest, -1), 1)
    back = jnp.concatenate([back, back], axis=1)
    return lax.dynamic_slice_in_dim(back, rest - 1 - lax.axis_index("rest"), rest, 1).reshape(zones, zones)


def shards(od_cells, anchor_edges, edge_weight, mixing, dst_edges, dst_weight, out_bias):
    n_org = lax.axis_size("slow") * lax.axis_size("mid")
    n_dst = lax.axis_size("rest") * lax.axis_size("near") * lax.axis_size("core")
    own = edge_weight.shape[0] // (n_org * n_dst)
    everyone = ("slow", "mid", "rest", "near", "core")
    core = lax.axis_index("core")
    edges_t = anchor_edges.T
    plan = Plan(od_cells.shape[1], edge_weight.shape[0], own, lax.axis_size("rest"), lax.axis_size(LINE))
    firsts, second, roots = org_sums(lax.axis_index(LINE), od_cells, edges_t, edge_weight, plan)
    own_weight = lax.dynamic_slice_in_dim(edge_weight, lax.axis_index(everyone) * own, own, 0)
    weight_rows = jnp.broadcast_to(own_weight[:, None], (own, mixing.shape[0]))
    matrix = relative_columns(dest_operator(dst_edges, dst_weight))
    half = matrix.shape[0] // 2
    matrix = jnp.where(core == 0, matrix, jnp.concatenate([matrix[half:], matrix[:half]], axis=0))
    keep, give = table_rows(firsts, second, weight_rows, mixing, matrix, plan)
    longs, shorts = gather_table(keep, give)
    rows = anchor_edges.shape[0] // n_dst
    start = lax.axis_index(("rest", "near", "core")) * rows
    ids = lax.dynamic_slice_in_dim(edges_t, start, rows, 1)
    own_root = lax.dynamic_slice_in_dim(roots, start, rows, 1)
    bias = out_bias[None, :]
    other = 1 - core
    long_places, short_places = places_of(ids, core, own)
    far_long_places, far_short_places = places_of(ids, other, own)
    split = longs[0].shape[1]
    here, there = core[None], other[None]
    result = spread(here, short_places, own_root, bias, shorts, split, half)
    far = [swapped(x) for x in shorts]
    result = spread(there, far_short_places, own_root, bias, far, split, half, result)
    result = spread(here, long_places, own_root, bias, longs, 0, half, result)
    far = [swapped(x) for x in longs]
    return spread(there, far_long_places, own_root, bias, far, 0, half, result)


def solution(mesh):
    n_org, n_dst = mesh.devices.shape
    fine = Mesh(mesh.devices.reshape(n_org // 2, 2, n_dst // 4, 2, 2), ("slow", "mid", "rest", "near", "core"))
    org, dst = ("slow", "mid"), ("rest", "near", "core")
    in_specs = (P(org, dst, None), P(org, None), P(), P(), P(), P(), P())
    out_specs = P(org + dst, None, None)
    return jax.shard_map(shards, mesh=fine, in_specs=in_specs, out_specs=out_specs, check_vma=False)
```

```python
import functools

import jax
import jax.numpy as jnp
from jax import lax
from jax.experimental import pallas as pl
from jax.experimental.pallas import tpu as pltpu
from jax.sharding import Mesh, PartitionSpec as P

BF16 = jnp.bfloat16
F32 = jnp.float32
COUNT_BASE = 256.0
HEAD = 16


def corridor_table(edge_ids, edge_count):
    columns = jnp.arange(edge_count, dtype=jnp.int32)
    return jnp.sum((edge_ids[:, :, None] == columns[None, None, :]).astype(F32), axis=1)


def dest_operator(dst_edges, dst_weight):
    dst_member = corridor_table(dst_edges, dst_weight.shape[0])
    dst_degree = jnp.sum(dst_member * dst_weight[None, :], axis=1)
    edge_sizes = jnp.sum(dst_member, axis=0)
    left_factor = dst_member * lax.rsqrt(dst_degree)[:, None]
    right_factor = left_factor * (dst_weight / edge_sizes)[None, :]
    result = jnp.dot(right_factor, left_factor.T, precision=lax.Precision.HIGHEST)
    return result.astype(BF16)


class Plan:
    def __init__(self, zones, edges, own, rest, line):
        self.edges = edges
        self.own = own
        self.rest = rest
        self.line = line
        self.cut = zones // 2
        self.first_rows = self.cut * own
        self.second_rows = HEAD + (zones - self.cut) * own

        self.relative = own % 8 == 0

    def device(self, square, line):
        core, near, mid = square % 2, square // 2 % 2, square // 4
        if isinstance(line, int):
            slow, rest = line // self.rest, line % self.rest
        else:
            slow, rest = lax.div(line, self.rest), lax.rem(line, self.rest)
        return (((slow * 2 + mid) * self.rest + rest) * 2 + near) * 2 + core


def halves_of(counts):
    high = jnp.floor(counts * (1.0 / COUNT_BASE))
    return high, counts - high * COUNT_BASE


def head_rows(high, low):
    parts = [high, low]
    if high.shape[0] < HEAD // 2:
        pad = jnp.zeros((HEAD // 2 - high.shape[0], high.shape[1]), F32)
        parts = [high, pad, low, pad]
    return jnp.concatenate(parts, axis=0).astype(BF16)


def one_hot(edges_ref, weight_ref, edges, lanes):
    ids = edges_ref[...]
    rows = ids.shape[1]
    columns = lax.broadcasted_iota(jnp.int32, (edges, rows), 0)
    member = columns == ids[0:1, :]
    for j in range(1, ids.shape[0]):
        member = jnp.logical_or(member, columns == ids[j : j + 1, :])
    upright = jnp.transpose(jnp.broadcast_to(weight_ref[...], (lanes, edges)))
    upright = jnp.concatenate([upright] * (rows // lanes), axis=1)
    root = lax.rsqrt(jnp.sum(jnp.where(member, upright, 0.0), axis=0, keepdims=True))
    rounded = root.astype(BF16).astype(F32)
    weighted = jnp.where(member, rounded, 0.0).astype(BF16)
    hot = jnp.where(member, 1.0, 0.0).astype(BF16)
    return root, weighted, jnp.dot(hot, jnp.ones((rows, lanes), BF16), preferred_element_type=F32)


def accumulate(weighted, cells_ref, begin, zones, pitch, total_ref, wide_ref):
    rows, _, lanes = cells_ref.shape
    part = 32

    def widen(i, carry):
        first = i * part
        piece = cells_ref[pl.ds(first, part), begin : begin + zones, :].astype(F32)
        for j in range(part):
            wide_ref[pl.ds(pl.multiple_of((first + j) * pitch, 8), zones), :] = piece[j]
        return carry

    lax.fori_loop(0, rows // part, widen, 0)
    for pair in range(zones // 2):
        left = wide_ref[pl.ds(2 * pair, rows, stride=pitch), :].astype(BF16)
        right = wide_ref[pl.ds(2 * pair + 1, rows, stride=pitch), :].astype(BF16)
        both = jnp.concatenate([left, right], axis=1)
        total_ref[pair] += jnp.dot(weighted, both, preferred_element_type=F32)


def columns_of(total_ref, at, zones, lanes):
    data = []
    for d in range(zones):
        data.append(total_ref[d // 2, at, (d % 2) * lanes : (d % 2 + 1) * lanes])
    return jnp.concatenate(data, axis=0).astype(BF16)


def rows_for(plan, square, shift, line_ref):
    own = plan.own
    if plan.relative:
        device = plan.device(square, lax.rem(line_ref[0] + shift, plan.line))
        return pl.ds(pl.multiple_of(device * own, own), own)
    device = plan.device(square, shift)
    return slice(device * own, (device + 1) * own)


def second_kernel(plan, begin, zones, pitch, line_ref, edges_ref, weight_ref, cells_ref, *refs):
    out_refs = refs[: plan.line]
    root_ref, weighted_ref, total_ref, count_ref, wide_ref = refs[plan.line :]
    lanes = cells_ref.shape[2]

    @pl.when(pl.program_id(0) == 0)
    def _():
        total_ref[...] = jnp.zeros_like(total_ref)
        count_ref[...] = jnp.zeros_like(count_ref)

    root, weighted, counts = one_hot(edges_ref, weight_ref, total_ref.shape[1], lanes)
    root_ref[...] = root
    weighted_ref[...] = weighted
    count_ref[...] += counts
    accumulate(weighted, cells_ref, begin, zones, pitch, total_ref, wide_ref)

    @pl.when(pl.program_id(0) == pl.num_programs(0) - 1)
    def _():
        for square in range(8):
            for shift in range(plan.line):
                at = rows_for(plan, square, shift, line_ref)
                out_refs[shift][square, HEAD:, :] = columns_of(total_ref, at, zones, lanes)
                out_refs[shift][square, 0:HEAD, :] = head_rows(*halves_of(count_ref[at, :]))


def first_kernel(plan, begin, zones, pitch, line_ref, weighted_ref, cells_ref, out_ref, total_ref, wide_ref):
    @pl.when(pl.program_id(0) == 0)
    def _():
        total_ref[...] = jnp.zeros_like(total_ref)

    accumulate(weighted_ref[...], cells_ref, begin, zones, pitch, total_ref, wide_ref)

    @pl.when(pl.program_id(0) == pl.num_programs(0) - 1)
    def _():
        for square in range(8):
            for shift in range(plan.line):
                at = rows_for(plan, square, shift, line_ref)
                out_ref[square, shift] = columns_of(total_ref, at, zones, cells_ref.shape[2])


def fixed(shape):
    return pl.BlockSpec(shape, lambda i: (0,) * len(shape))


def half_sums(kernel, plan, part, line, cells, operands, specs, outs, out_specs, counted):
    anchors, zones, lanes = cells.shape
    edges = plan.edges
    half = zones // 2
    rows = min(512, anchors)
    pitch = -(-half // 8) * 8 + 8
    if half % 16 == 0:
        block, begin = pl.BlockSpec((rows, half, lanes), lambda i: (i, part, 0)), 0
    else:
        block, begin = pl.BlockSpec((rows, zones, lanes), lambda i: (i, 0, 0)), part * half
    counts = [pltpu.VMEM((edges, lanes), F32)] if counted else []
    return pl.pallas_call(
        functools.partial(kernel, plan, begin, half, pitch),
        grid=(anchors // rows,),
        in_specs=[pl.BlockSpec(memory_space=pltpu.SMEM)] + specs + [block],
        out_specs=out_specs,
        out_shape=outs,
        scratch_shapes=[pltpu.VMEM((half // 2, edges, 2 * lanes), F32)] + counts + [pltpu.VMEM((rows * pitch, lanes), F32)],
        compiler_params=pltpu.CompilerParams(vmem_limit_bytes=40 * 1024 * 1024),
        cost_estimate=pl.CostEstimate(
            flops=4 * anchors * edges * zones * lanes, bytes_accessed=2 * anchors * zones * lanes, transcendentals=0
        ),
    )(line[None], *operands, cells)


def second_sums(line, cells, edges_t, edge_weight, plan):
    anchors, _, lanes = cells.shape
    rows = min(512, anchors)
    edges = plan.edges
    shape = (8, plan.second_rows, lanes)
    outs = [jax.ShapeDtypeStruct(shape, BF16)] * plan.line
    outs += [jax.ShapeDtypeStruct((1, anchors), F32), jax.ShapeDtypeStruct((edges, anchors), BF16)]
    out_specs = [fixed(shape)] * plan.line
    out_specs += [pl.BlockSpec((1, rows), lambda i: (0, i)), pl.BlockSpec((edges, rows), lambda i: (0, i))]
    specs = [pl.BlockSpec((edges_t.shape[0], rows), lambda i: (0, i)), fixed((1, edges))]
    operands = (edges_t, edge_weight[None, :])
    *seconds, roots, weighted = half_sums(second_kernel, plan, 1, line, cells, operands, specs, outs, out_specs, True)
    if not plan.relative:
        seconds = jnp.stack(seconds * 2)
        seconds = [lax.dynamic_index_in_dim(seconds, line + k, 0, keepdims=False) for k in range(plan.line)]
    return seconds, roots, weighted


def first_sums(line, cells, weighted, plan):
    rows = min(512, cells.shape[0])
    shape = (8, plan.line, plan.first_rows, cells.shape[2])
    specs = [pl.BlockSpec((plan.edges, rows), lambda i: (0, i))]
    out = jax.ShapeDtypeStruct(shape, BF16)
    first = half_sums(first_kernel, plan, 0, line, cells, (weighted,), specs, out, fixed(shape), False)
    if not plan.relative:
        first = lax.dynamic_slice_in_dim(jnp.concatenate([first, first], axis=1), line, plan.line, 1)
    return first


def add_up(pieces):
    total = pieces[0].astype(F32)
    for piece in pieces[1:]:
        total = total + piece.astype(F32)
    return total


def fold_first_kernel(plan, part_ref, *outs):
    for shift in range(plan.line):
        for quarter in range(4):
            outs[shift][quarter] = add_up([part_ref[quarter, shift], part_ref[4 + quarter, shift]]).astype(BF16)


def fold_second_kernel(plan, *refs):
    parts, out_ref = refs[: plan.line], refs[plan.line]
    for square in range(8):
        for rest in range(plan.rest):
            total = add_up([parts[shift][square] for shift in range(rest, plan.line, plan.rest)])
            half = HEAD // 2
            out_ref[square, rest, 0:HEAD, :] = head_rows(*halves_of(total[0:half] * COUNT_BASE + total[half:HEAD]))
            out_ref[square, rest, HEAD:, :] = total[HEAD:].astype(BF16)


def fold(kernel, plan, parts, shapes):
    whole = pl.BlockSpec(memory_space=pltpu.VMEM)
    size = sum(part.size for part in parts)
    return pl.pallas_call(
        functools.partial(kernel, plan),
        in_specs=[whole] * len(parts),
        out_specs=[whole] * len(shapes),
        out_shape=[jax.ShapeDtypeStruct(shape, BF16) for shape in shapes],
        compiler_params=pltpu.CompilerParams(vmem_limit_bytes=16 * 1024 * 1024),
        cost_estimate=pl.CostEstimate(flops=size, bytes_accessed=size * 4, transcendentals=0),
    )(*parts)


def org_sums(line, cells, edges_t, edge_weight, plan):
    lanes = cells.shape[-1]
    seconds, roots, weighted = second_sums(line, cells, edges_t, edge_weight, plan)
    seconds = [shifted(part, shift) if shift else part for shift, part in enumerate(seconds)]
    first = first_sums(line, cells, weighted, plan)
    first, seconds[1] = lax.optimization_barrier((first, seconds[1]))
    first = lax.all_to_all(first, SQUARE, split_axis=0, concat_axis=0, tiled=True)
    firsts = fold(fold_first_kernel, plan, [first], [(4, plan.first_rows, lanes)] * plan.line)
    firsts = [shifted(part, shift) if shift else part for shift, part in enumerate(firsts)]
    firsts[1], seconds[2] = lax.optimization_barrier((firsts[1], seconds[2]))
    second = fold(fold_second_kernel, plan, seconds, [(8, plan.rest, plan.second_rows, lanes)])[0]
    second = lax.all_to_all(second, SQUARE, split_axis=0, concat_axis=0, tiled=True)
    return firsts, second, roots


def table_kernel(plan, weight_ref, mixing_ref, matrix_ref, *refs):
    firsts = refs[: plan.line]
    second_ref, keep_ref, give_ref, mixed_ref = refs[plan.line :]
    own = plan.own
    lanes = mixing_ref.shape[0]
    half = HEAD // 2
    head = add_up([second_ref[0, 0, 0:HEAD, :], second_ref[4, 0, 0:HEAD, :]])
    counts = head[0:half] * COUNT_BASE + head[half:HEAD]
    scale = weight_ref[...] / counts[0:own]
    rows = plan.first_rows + plan.second_rows - HEAD
    zones = rows // own
    n_dst = 4 * plan.rest
    for k in range(n_dst):
        rest, quarter = k // 4, k % 4
        first = add_up([firsts[shift][quarter] for shift in range(rest, plan.line, plan.rest)])
        second = add_up([second_ref[quarter, rest, HEAD:, :], second_ref[4 + quarter, rest, HEAD:, :]])
        start = k * rows
        for total in (first, second):
            size = total.shape[0]
            totals = (total * jnp.concatenate([scale] * (size // own), axis=0)).astype(BF16)
            mixed = jnp.dot(totals, mixing_ref[...], preferred_element_type=F32)
            mixed_ref[start : start + size, :] = mixed
            start += size
    whole = n_dst * zones
    for e in range(own):
        mixed = mixed_ref[pl.ds(e, whole, stride=own), :] if own > 1 else mixed_ref[...]
        high = mixed.astype(BF16)
        low = (mixed - high.astype(F32)).astype(BF16)
        both = jnp.dot(matrix_ref[...], jnp.concatenate([high, low], axis=1), preferred_element_type=F32)
        result = (both[:, 0:lanes] + both[:, lanes : 2 * lanes]).astype(BF16)
        keep_ref[e] = result[0 : whole // 2]
        give_ref[e] = result[whole // 2 :]


def table_rows(firsts, second, weight_rows, mixing, matrix, plan):
    zones = matrix.shape[0]
    lanes = mixing.shape[0]
    whole = pl.BlockSpec(memory_space=pltpu.VMEM)
    half = jax.ShapeDtypeStruct((plan.own, zones // 2, lanes), BF16)
    return pl.pallas_call(
        functools.partial(table_kernel, plan),
        in_specs=[whole] * (4 + len(firsts)),
        out_specs=[whole] * 2,
        out_shape=[half, half],
        scratch_shapes=[pltpu.VMEM((zones * plan.own, lanes), F32)],
        compiler_params=pltpu.CompilerParams(vmem_limit_bytes=32 * 1024 * 1024),
        cost_estimate=pl.CostEstimate(
            flops=8 * plan.own * zones * lanes * lanes, bytes_accessed=4 * zones * plan.own * lanes, transcendentals=0
        ),
    )(weight_rows, mixing, matrix, *firsts, second)


def spread_kernel(n_pieces, stride, offset, half_ref, places_ref, root_ref, bias_ref, *refs):
    out_ref, table_ref, ring_ref, sems, ring_sems = refs[-5:]
    slots, rows, zones, lanes = ring_ref.shape
    steps = out_ref.shape[0] // rows
    first_zone = pl.multiple_of(half_ref[0] * stride + offset, 16)

    copies = []
    for i, source in enumerate(refs[:n_pieces]):
        size = source.shape[0]
        copies.append(pltpu.make_async_copy(source, table_ref.at[pl.ds(i * size, size), :], sems.at[i]))
    for copy in copies:
        copy.start()
    for copy in copies:
        copy.wait()

    bias = bias_ref[...]
    anchors = root_ref.shape[0]
    count = places_ref.shape[0] // anchors
    tile = 16
    batch = min(8 if zones > tile else 16, rows)
    tiles = zones // tile

    def leaving(step, slot):
        place = out_ref.at[pl.ds(step * rows, rows), pl.ds(first_zone, zones), :]
        return pltpu.make_async_copy(ring_ref.at[slot], place, ring_sems.at[slot])

    def one_step(step, carry):
        slot = lax.rem(step, slots)

        @pl.when(step >= slots)
        def _():
            leaving(step - slots, slot).wait()

        def several(group, inner):
            values = []
            for i in range(batch):
                at = step * rows + group * batch + i
                scale = root_ref[at]
                spots = [pl.multiple_of(places_ref[j * anchors + at], tile) for j in range(count)]
                for first in range(0, zones, tile):
                    pieces = [table_ref[pl.ds(spot + first, tile), :] for spot in spots]
                    pieces = [(a + b).astype(F32) for a, b in zip(pieces[0::2], pieces[1::2])]
                    total = sum(pieces[1:], pieces[0])
                    values.append(jnp.maximum((total * scale + bias).astype(BF16), BF16(0.0)))
            for n, value in enumerate(values):
                start = n % tiles * tile
                ring_ref[slot, group * batch + n // tiles, start : start + tile, :] = value
            return inner

        lax.fori_loop(0, rows // batch, several, 0)
        leaving(step, slot).start()
        return carry

    lax.fori_loop(0, steps, one_step, 0)
    for step in range(steps - slots, steps):
        leaving(step, step % slots).wait()


def spread(half, places, root, bias, pieces, offset, stride, before=None):
    anchors = places.shape[1]
    lanes = bias.shape[1]
    zones = pieces[0].shape[1]
    edges = len(pieces) * pieces[0].shape[0]
    pieces = [piece.reshape(-1, lanes) for piece in pieces]
    rows = min(16, anchors // 8)
    slots = min(8, anchors // rows)
    smem = pl.BlockSpec(memory_space=pltpu.SMEM)
    anywhere = pl.BlockSpec(memory_space=pltpu.HBM)
    operands = [half, (places * zones).reshape(-1), root.reshape(-1), bias] + pieces
    specs = [smem, smem, smem, pl.BlockSpec(memory_space=pltpu.VMEM)] + [anywhere] * len(pieces)
    aliases = {}
    if before is not None:
        aliases = {len(operands): 0}
        operands.append(before)
        specs.append(anywhere)
    return pl.pallas_call(
        functools.partial(spread_kernel, len(pieces), stride, offset),
        in_specs=specs,
        out_specs=anywhere,
        out_shape=jax.ShapeDtypeStruct((anchors, 2 * stride, lanes), BF16),
        scratch_shapes=[
            pltpu.VMEM((edges * zones, lanes), BF16),
            pltpu.VMEM((slots, rows, zones, lanes), BF16),
            pltpu.SemaphoreType.DMA((len(pieces),)),
            pltpu.SemaphoreType.DMA((slots,)),
        ],
        input_output_aliases=aliases,
        compiler_params=pltpu.CompilerParams(vmem_limit_bytes=24 * 1024 * 1024),
        cost_estimate=pl.CostEstimate(
            flops=4096 * anchors * zones * lanes, bytes_accessed=4 * anchors * zones * lanes, transcendentals=0
        ),
    )(*operands)


LINE = ("slow", "rest")
SQUARE = ("mid", "near", "core")


def shifted(x, amount):
    size = lax.axis_size(LINE)
    return lax.ppermute(x, LINE, [(i, (i + amount) % size) for i in range(size)])


def crossed(x, turn):
    pairs = []
    for device in range(8):
        core = device % 2
        pairs.append((device, device ^ (2 if core == turn else 4)))
    return lax.ppermute(x, SQUARE, pairs)


def masked(x, mask):
    return lax.ppermute(x, SQUARE, [(device, device ^ mask) for device in range(8)])


def swapped(x):
    return lax.ppermute(x, "core", [(0, 1), (1, 0)])


def gather_table(keep, give):
    size = lax.axis_size(LINE)
    block = jnp.concatenate([keep, swapped(give)], axis=0)
    split = block.shape[1] * 3 // 4
    long, short = block[:, :split], block[:, split:]
    line = [long] + [shifted(long, k) for k in range(1, size)]
    short = jnp.concatenate([short, crossed(short, 0), crossed(short, 1), masked(short, 6)], axis=0)
    long = jnp.concatenate(line, axis=0)
    short, long = lax.optimization_barrier((short, long))
    first = crossed(long, 0)
    second = crossed(long, 1)
    shorts = [short] + [shifted(short, k) for k in range(1, size)]
    first, *shorts[1:-1] = lax.optimization_barrier((first, *shorts[1:-1]))
    both = crossed(first, 1)
    return [long, first, second, both], shorts


def places_of(ids, core, own):
    rest, size = lax.axis_size("rest"), lax.axis_size(LINE)
    owner = ids // own
    slot = jnp.where(owner % 2 == core, 0, own) + ids % own
    near = jnp.bitwise_xor(owner // 2 % 2, lax.axis_index("near"))
    mid = jnp.bitwise_xor(owner // (4 * rest) % 2, lax.axis_index("mid"))
    line = owner // (8 * rest) * rest + owner // 4 % rest
    line = lax.rem(lax.axis_index(LINE) - line + size, size)
    square = jnp.where(core == 0, 2 * mid + near, 2 * near + mid)
    return (square * size + line) * (2 * own) + slot, (line * 4 + square) * (2 * own) + slot


def relative_columns(matrix):
    zones, rest = matrix.shape[0], lax.axis_size("rest")
    if rest == 1:
        return matrix
    back = jnp.flip(matrix.reshape(zones, rest, -1), 1)
    back = jnp.concatenate([back, back], axis=1)
    return lax.dynamic_slice_in_dim(back, rest - 1 - lax.axis_index("rest"), rest, 1).reshape(zones, zones)


def shards(od_cells, anchor_edges, edge_weight, mixing, dst_edges, dst_weight, out_bias):
    n_org = lax.axis_size("slow") * lax.axis_size("mid")
    n_dst = lax.axis_size("rest") * lax.axis_size("near") * lax.axis_size("core")
    own = edge_weight.shape[0] // (n_org * n_dst)
    everyone = ("slow", "mid", "rest", "near", "core")
    core = lax.axis_index("core")
    edges_t = anchor_edges.T
    plan = Plan(od_cells.shape[1], edge_weight.shape[0], own, lax.axis_size("rest"), lax.axis_size(LINE))
    firsts, second, roots = org_sums(lax.axis_index(LINE), od_cells, edges_t, edge_weight, plan)
    own_weight = lax.dynamic_slice_in_dim(edge_weight, lax.axis_index(everyone) * own, own, 0)
    weight_rows = jnp.broadcast_to(own_weight[:, None], (own, mixing.shape[0]))
    matrix = relative_columns(dest_operator(dst_edges, dst_weight))
    half = matrix.shape[0] // 2
    matrix = jnp.where(core == 0, matrix, jnp.concatenate([matrix[half:], matrix[:half]], axis=0))
    keep, give = table_rows(firsts, second, weight_rows, mixing, matrix, plan)
    longs, shorts = gather_table(keep, give)
    rows = anchor_edges.shape[0] // n_dst
    start = lax.axis_index(("rest", "near", "core")) * rows
    ids = lax.dynamic_slice_in_dim(edges_t, start, rows, 1)
    own_root = lax.dynamic_slice_in_dim(roots, start, rows, 1)
    bias = out_bias[None, :]
    other = 1 - core
    long_places, short_places = places_of(ids, core, own)
    far_long_places, far_short_places = places_of(ids, other, own)
    split = longs[0].shape[1]
    here, there = core[None], other[None]
    result = spread(here, short_places, own_root, bias, shorts, split, half)
    far = [swapped(x) for x in shorts]
    result = spread(there, far_short_places, own_root, bias, far, split, half, result)
    result = spread(here, long_places, own_root, bias, longs, 0, half, result)
    far = [swapped(x) for x in longs]
    return spread(there, far_long_places, own_root, bias, far, 0, half, result)


def solution(mesh):
    n_org, n_dst = mesh.devices.shape
    fine = Mesh(mesh.devices.reshape(n_org // 2, 2, n_dst // 4, 2, 2), ("slow", "mid", "rest", "near", "core"))
    org, dst = ("slow", "mid"), ("rest", "near", "core")
    in_specs = (P(org, dst, None), P(org, None), P(), P(), P(), P(), P())
    out_specs = P(org + dst, None, None)
    return jax.shard_map(shards, mesh=fine, in_specs=in_specs, out_specs=out_specs, check_vma=False)
```

```python
import functools

import jax
import jax.numpy as jnp
from jax import lax
from jax.experimental import pallas as pl
from jax.experimental.pallas import tpu as pltpu
from jax.sharding import Mesh, PartitionSpec as P

BF16 = jnp.bfloat16
F32 = jnp.float32
COUNT_BASE = 256.0
HEAD = 16


def corridor_table(edge_ids, edge_count):
    columns = jnp.arange(edge_count, dtype=jnp.int32)
    return jnp.sum((edge_ids[:, :, None] == columns[None, None, :]).astype(F32), axis=1)


def dest_operator(dst_edges, dst_weight):
    dst_member = corridor_table(dst_edges, dst_weight.shape[0])
    dst_degree = jnp.sum(dst_member * dst_weight[None, :], axis=1)
    edge_sizes = jnp.sum(dst_member, axis=0)
    left_factor = dst_member * lax.rsqrt(dst_degree)[:, None]
    right_factor = left_factor * (dst_weight / edge_sizes)[None, :]
    result = jnp.dot(right_factor, left_factor.T, precision=lax.Precision.HIGHEST)
    return result.astype(BF16)


class Plan:
    def __init__(self, zones, edges, own, rest, line):
        self.edges = edges
        self.own = own
        self.rest = rest
        self.line = line
        self.cut = zones // 2
        self.first_rows = self.cut * own
        self.second_rows = HEAD + (zones - self.cut) * own

        self.relative = own % 8 == 0

    def device(self, square, line):
        core, near, mid = square % 2, square // 2 % 2, square // 4
        if isinstance(line, int):
            slow, rest = line // self.rest, line % self.rest
        else:
            slow, rest = lax.div(line, self.rest), lax.rem(line, self.rest)
        return (((slow * 2 + mid) * self.rest + rest) * 2 + near) * 2 + core


def halves_of(counts):
    high = jnp.floor(counts * (1.0 / COUNT_BASE))
    return high, counts - high * COUNT_BASE


def head_rows(high, low):
    parts = [high, low]
    if high.shape[0] < HEAD // 2:
        pad = jnp.zeros((HEAD // 2 - high.shape[0], high.shape[1]), F32)
        parts = [high, pad, low, pad]
    return jnp.concatenate(parts, axis=0).astype(BF16)


def one_hot(edges_ref, weight_ref, edges, lanes):
    ids = edges_ref[...]
    rows = ids.shape[1]
    columns = lax.broadcasted_iota(jnp.int32, (edges, rows), 0)
    member = columns == ids[0:1, :]
    for j in range(1, ids.shape[0]):
        member = jnp.logical_or(member, columns == ids[j : j + 1, :])
    upright = jnp.transpose(jnp.broadcast_to(weight_ref[...], (lanes, edges)))
    upright = jnp.concatenate([upright] * (rows // lanes), axis=1)
    root = lax.rsqrt(jnp.sum(jnp.where(member, upright, 0.0), axis=0, keepdims=True))
    rounded = root.astype(BF16).astype(F32)
    weighted = jnp.where(member, rounded, 0.0).astype(BF16)
    hot = jnp.where(member, 1.0, 0.0).astype(BF16)
    return root, weighted, jnp.dot(hot, jnp.ones((rows, lanes), BF16), preferred_element_type=F32)


def accumulate(weighted, cells_ref, begin, zones, pitch, total_ref, wide_ref):
    rows, _, lanes = cells_ref.shape
    part = 32

    def widen(i, carry):
        first = i * part
        piece = cells_ref[pl.ds(first, part), begin : begin + zones, :].astype(F32)
        for j in range(part):
            wide_ref[pl.ds(pl.multiple_of((first + j) * pitch, 8), zones), :] = piece[j]
        return carry

    lax.fori_loop(0, rows // part, widen, 0)
    for pair in range(zones // 2):
        left = wide_ref[pl.ds(2 * pair, rows, stride=pitch), :].astype(BF16)
        right = wide_ref[pl.ds(2 * pair + 1, rows, stride=pitch), :].astype(BF16)
        both = jnp.concatenate([left, right], axis=1)
        total_ref[pair] += jnp.dot(weighted, both, preferred_element_type=F32)


def columns_of(total_ref, at, zones, lanes):
    data = []
    for d in range(zones):
        data.append(total_ref[d // 2, at, (d % 2) * lanes : (d % 2 + 1) * lanes])
    return jnp.concatenate(data, axis=0).astype(BF16)


def rows_for(plan, square, shift, line_ref):
    own = plan.own
    if plan.relative:
        device = plan.device(square, lax.rem(line_ref[0] + shift, plan.line))
        return pl.ds(pl.multiple_of(device * own, own), own)
    device = plan.device(square, shift)
    return slice(device * own, (device + 1) * own)


def second_kernel(plan, begin, zones, pitch, line_ref, edges_ref, weight_ref, cells_ref, *refs):
    out_refs = refs[: plan.line]
    root_ref, weighted_ref, total_ref, count_ref, wide_ref = refs[plan.line :]
    lanes = cells_ref.shape[2]

    @pl.when(pl.program_id(0) == 0)
    def _():
        total_ref[...] = jnp.zeros_like(total_ref)
        count_ref[...] = jnp.zeros_like(count_ref)

    root, weighted, counts = one_hot(edges_ref, weight_ref, total_ref.shape[1], lanes)
    root_ref[...] = root
    weighted_ref[...] = weighted
    count_ref[...] += counts
    accumulate(weighted, cells_ref, begin, zones, pitch, total_ref, wide_ref)

    @pl.when(pl.program_id(0) == pl.num_programs(0) - 1)
    def _():
        for square in range(8):
            for shift in range(plan.line):
                at = rows_for(plan, square, shift, line_ref)
                out_refs[shift][square, HEAD:, :] = columns_of(total_ref, at, zones, lanes)
                out_refs[shift][square, 0:HEAD, :] = head_rows(*halves_of(count_ref[at, :]))


def first_kernel(plan, begin, zones, pitch, line_ref, weighted_ref, cells_ref, out_ref, total_ref, wide_ref):
    @pl.when(pl.program_id(0) == 0)
    def _():
        total_ref[...] = jnp.zeros_like(total_ref)

    accumulate(weighted_ref[...], cells_ref, begin, zones, pitch, total_ref, wide_ref)

    @pl.when(pl.program_id(0) == pl.num_programs(0) - 1)
    def _():
        for square in range(8):
            for shift in range(plan.line):
                at = rows_for(plan, square, shift, line_ref)
                out_ref[square, shift] = columns_of(total_ref, at, zones, cells_ref.shape[2])


def fixed(shape):
    return pl.BlockSpec(shape, lambda i: (0,) * len(shape))


def half_sums(kernel, plan, part, line, cells, operands, specs, outs, out_specs, counted):
    anchors, zones, lanes = cells.shape
    edges = plan.edges
    half = zones // 2
    rows = min(512, anchors)
    pitch = -(-half // 8) * 8 + 8
    if half % 16 == 0:
        block, begin = pl.BlockSpec((rows, half, lanes), lambda i: (i, part, 0)), 0
    else:
        block, begin = pl.BlockSpec((rows, zones, lanes), lambda i: (i, 0, 0)), part * half
    counts = [pltpu.VMEM((edges, lanes), F32)] if counted else []
    return pl.pallas_call(
        functools.partial(kernel, plan, begin, half, pitch),
        grid=(anchors // rows,),
        in_specs=[pl.BlockSpec(memory_space=pltpu.SMEM)] + specs + [block],
        out_specs=out_specs,
        out_shape=outs,
        scratch_shapes=[pltpu.VMEM((half // 2, edges, 2 * lanes), F32)] + counts + [pltpu.VMEM((rows * pitch, lanes), F32)],
        compiler_params=pltpu.CompilerParams(vmem_limit_bytes=40 * 1024 * 1024),
        cost_estimate=pl.CostEstimate(
            flops=4 * anchors * edges * zones * lanes, bytes_accessed=2 * anchors * zones * lanes, transcendentals=0
        ),
    )(line[None], *operands, cells)


def second_sums(line, cells, edges_t, edge_weight, plan):
    anchors, _, lanes = cells.shape
    rows = min(512, anchors)
    edges = plan.edges
    shape = (8, plan.second_rows, lanes)
    outs = [jax.ShapeDtypeStruct(shape, BF16)] * plan.line
    outs += [jax.ShapeDtypeStruct((1, anchors), F32), jax.ShapeDtypeStruct((edges, anchors), BF16)]
    out_specs = [fixed(shape)] * plan.line
    out_specs += [pl.BlockSpec((1, rows), lambda i: (0, i)), pl.BlockSpec((edges, rows), lambda i: (0, i))]
    specs = [pl.BlockSpec((edges_t.shape[0], rows), lambda i: (0, i)), fixed((1, edges))]
    operands = (edges_t, edge_weight[None, :])
    *seconds, roots, weighted = half_sums(second_kernel, plan, 1, line, cells, operands, specs, outs, out_specs, True)
    if not plan.relative:
        seconds = jnp.stack(seconds * 2)
        seconds = [lax.dynamic_index_in_dim(seconds, line + k, 0, keepdims=False) for k in range(plan.line)]
    return seconds, roots, weighted


def first_sums(line, cells, weighted, plan):
    rows = min(512, cells.shape[0])
    shape = (8, plan.line, plan.first_rows, cells.shape[2])
    specs = [pl.BlockSpec((plan.edges, rows), lambda i: (0, i))]
    out = jax.ShapeDtypeStruct(shape, BF16)
    first = half_sums(first_kernel, plan, 0, line, cells, (weighted,), specs, out, fixed(shape), False)
    if not plan.relative:
        first = lax.dynamic_slice_in_dim(jnp.concatenate([first, first], axis=1), line, plan.line, 1)
    return first


def add_up(pieces):
    total = pieces[0].astype(F32)
    for piece in pieces[1:]:
        total = total + piece.astype(F32)
    return total


def fold_first_kernel(plan, part_ref, *outs):
    for shift in range(plan.line):
        for quarter in range(4):
            outs[shift][quarter] = add_up([part_ref[quarter, shift], part_ref[4 + quarter, shift]]).astype(BF16)


def fold_second_kernel(plan, *refs):
    parts, out_ref = refs[: plan.line], refs[plan.line]
    for square in range(8):
        for rest in range(plan.rest):
            total = add_up([parts[shift][square] for shift in range(rest, plan.line, plan.rest)])
            half = HEAD // 2
            out_ref[square, rest, 0:HEAD, :] = head_rows(*halves_of(total[0:half] * COUNT_BASE + total[half:HEAD]))
            out_ref[square, rest, HEAD:, :] = total[HEAD:].astype(BF16)


def fold(kernel, plan, parts, shapes):
    whole = pl.BlockSpec(memory_space=pltpu.VMEM)
    size = sum(part.size for part in parts)
    return pl.pallas_call(
        functools.partial(kernel, plan),
        in_specs=[whole] * len(parts),
        out_specs=[whole] * len(shapes),
        out_shape=[jax.ShapeDtypeStruct(shape, BF16) for shape in shapes],
        compiler_params=pltpu.CompilerParams(vmem_limit_bytes=16 * 1024 * 1024),
        cost_estimate=pl.CostEstimate(flops=size, bytes_accessed=size * 4, transcendentals=0),
    )(*parts)


def org_sums(line, cells, edges_t, edge_weight, plan):
    lanes = cells.shape[-1]
    seconds, roots, weighted = second_sums(line, cells, edges_t, edge_weight, plan)
    seconds = [shifted(part, shift) if shift else part for shift, part in enumerate(seconds)]
    first = first_sums(line, cells, weighted, plan)
    first, *seconds[1::2] = lax.optimization_barrier((first, *seconds[1::2]))
    first = lax.all_to_all(first, SQUARE, split_axis=0, concat_axis=0, tiled=True)
    second = fold(fold_second_kernel, plan, seconds, [(8, plan.rest, plan.second_rows, lanes)])[0]
    firsts = fold(fold_first_kernel, plan, [first], [(4, plan.first_rows, lanes)] * plan.line)
    firsts = [shifted(part, shift) if shift else part for shift, part in enumerate(firsts)]
    second = lax.all_to_all(second, SQUARE, split_axis=0, concat_axis=0, tiled=True)
    return firsts, second, roots


def table_kernel(plan, weight_ref, mixing_ref, matrix_ref, *refs):
    firsts = refs[: plan.line]
    second_ref, keep_ref, give_ref, mixed_ref = refs[plan.line :]
    own = plan.own
    lanes = mixing_ref.shape[0]
    half = HEAD // 2
    head = add_up([second_ref[0, 0, 0:HEAD, :], second_ref[4, 0, 0:HEAD, :]])
    counts = head[0:half] * COUNT_BASE + head[half:HEAD]
    scale = weight_ref[...] / counts[0:own]
    rows = plan.first_rows + plan.second_rows - HEAD
    zones = rows // own
    n_dst = 4 * plan.rest
    for k in range(n_dst):
        rest, quarter = k // 4, k % 4
        first = add_up([firsts[shift][quarter] for shift in range(rest, plan.line, plan.rest)])
        second = add_up([second_ref[quarter, rest, HEAD:, :], second_ref[4 + quarter, rest, HEAD:, :]])
        start = k * rows
        for total in (first, second):
            size = total.shape[0]
            totals = (total * jnp.concatenate([scale] * (size // own), axis=0)).astype(BF16)
            mixed = jnp.dot(totals, mixing_ref[...], preferred_element_type=F32)
            mixed_ref[start : start + size, :] = mixed
            start += size
    whole = n_dst * zones
    for e in range(own):
        mixed = mixed_ref[pl.ds(e, whole, stride=own), :] if own > 1 else mixed_ref[...]
        high = mixed.astype(BF16)
        low = (mixed - high.astype(F32)).astype(BF16)
        both = jnp.dot(matrix_ref[...], jnp.concatenate([high, low], axis=1), preferred_element_type=F32)
        result = (both[:, 0:lanes] + both[:, lanes : 2 * lanes]).astype(BF16)
        keep_ref[e] = result[0 : whole // 2]
        give_ref[e] = result[whole // 2 :]


def table_rows(firsts, second, weight_rows, mixing, matrix, plan):
    zones = matrix.shape[0]
    lanes = mixing.shape[0]
    whole = pl.BlockSpec(memory_space=pltpu.VMEM)
    half = jax.ShapeDtypeStruct((plan.own, zones // 2, lanes), BF16)
    return pl.pallas_call(
        functools.partial(table_kernel, plan),
        in_specs=[whole] * (4 + len(firsts)),
        out_specs=[whole] * 2,
        out_shape=[half, half],
        scratch_shapes=[pltpu.VMEM((zones * plan.own, lanes), F32)],
        compiler_params=pltpu.CompilerParams(vmem_limit_bytes=32 * 1024 * 1024),
        cost_estimate=pl.CostEstimate(
            flops=8 * plan.own * zones * lanes * lanes, bytes_accessed=4 * zones * plan.own * lanes, transcendentals=0
        ),
    )(weight_rows, mixing, matrix, *firsts, second)


def spread_kernel(n_long, n_short, core_ref, places_ref, root_ref, bias_ref, *refs):
    pieces = refs[: 2 * (n_long + n_short)]
    out_ref, table_ref, ring_ref, sems, ring_sems = refs[-5:]
    slots, rows, zones, lanes = ring_ref.shape
    steps = out_ref.shape[0] // rows
    half = zones // 2
    copies = []

    def bring(source, first, start):
        size, height = source.shape[0], source.shape[1]
        place = table_ref.at[pl.ds(first, size), pl.ds(pl.multiple_of(start, 16), height), :]
        copies.append(pltpu.make_async_copy(source, place, sems.at[len(copies)]))

    for side in range(2):
        core = core_ref[0] if side == 0 else 1 - core_ref[0]
        longs = pieces[side * (n_long + n_short) :][:n_long]
        shorts = pieces[side * (n_long + n_short) + n_long :][:n_short]
        split = longs[0].shape[1]
        size = shorts[0].shape[0] // n_long
        for turn, source in enumerate(longs):
            square = turn if turn in (0, 3) else turn + core * (3 - 2 * turn)
            bring(source, square * (n_short * size), core * half)
        for shift, source in enumerate(shorts):
            for square in range(n_long):
                bring(source.at[pl.ds(square * size, size)], (square * n_short + shift) * size, core * half + split)
    for copy in copies:
        copy.start()
    for copy in copies:
        copy.wait()

    bias = bias_ref[...]
    count = places_ref.shape[0]
    tile = 16
    batch = min(4, rows)
    tiles = zones // tile

    def leaving(step, slot):
        return pltpu.make_async_copy(ring_ref.at[slot], out_ref.at[pl.ds(step * rows, rows)], ring_sems.at[slot])

    def one_step(step, carry):
        slot = lax.rem(step, slots)

        @pl.when(step >= slots)
        def _():
            leaving(step - slots, slot).wait()

        def several(group, inner):
            values = []
            for i in range(batch):
                at = step * rows + group * batch + i
                scale = root_ref[0, at]
                spots = [places_ref[j, at] for j in range(count)]
                for first in range(0, zones, tile):
                    parts = [table_ref[spot, first : first + tile, :] for spot in spots]
                    parts = [(a + b).astype(F32) for a, b in zip(parts[0::2], parts[1::2])]
                    total = sum(parts[1:], parts[0])
                    values.append(jnp.maximum((total * scale + bias).astype(BF16), BF16(0.0)))
            for n, value in enumerate(values):
                start = n % tiles * tile
                ring_ref[slot, group * batch + n // tiles, start : start + tile, :] = value
            return inner

        lax.fori_loop(0, rows // batch, several, 0)
        leaving(step, slot).start()
        return carry

    lax.fori_loop(0, steps, one_step, 0)
    for step in range(steps - slots, steps):
        leaving(step, step % slots).wait()


def spread(core, places, root, bias, near, far):
    anchors = places.shape[1]
    lanes = bias.shape[1]
    longs, shorts = near
    zones = 2 * (longs[0].shape[1] + shorts[0].shape[1])
    edges = len(longs) * longs[0].shape[0]
    rows = min(16, anchors // 8)
    slots = min(8, anchors // rows)
    smem = pl.BlockSpec(memory_space=pltpu.SMEM)
    anywhere = pl.BlockSpec(memory_space=pltpu.HBM)
    pieces = longs + shorts + far[0] + far[1]
    return pl.pallas_call(
        functools.partial(spread_kernel, len(longs), len(shorts)),
        in_specs=[smem, smem, smem, pl.BlockSpec(memory_space=pltpu.VMEM)] + [anywhere] * len(pieces),
        out_specs=anywhere,
        out_shape=jax.ShapeDtypeStruct((anchors, zones, lanes), BF16),
        scratch_shapes=[
            pltpu.VMEM((edges, zones, lanes), BF16),
            pltpu.VMEM((slots, rows, zones, lanes), BF16),
            pltpu.SemaphoreType.DMA((2 * len(longs) * (1 + len(shorts)),)),
            pltpu.SemaphoreType.DMA((slots,)),
        ],
        compiler_params=pltpu.CompilerParams(vmem_limit_bytes=32 * 1024 * 1024),
        cost_estimate=pl.CostEstimate(
            flops=4096 * anchors * zones * lanes, bytes_accessed=4 * anchors * zones * lanes, transcendentals=0
        ),
    )(core, places, root, bias, *pieces)


LINE = ("slow", "rest")
SQUARE = ("mid", "near", "core")


def shifted(x, amount):
    size = lax.axis_size(LINE)
    return lax.ppermute(x, LINE, [(i, (i + amount) % size) for i in range(size)])


def crossed(x, turn):
    pairs = []
    for device in range(8):
        core = device % 2
        pairs.append((device, device ^ (2 if core == turn else 4)))
    return lax.ppermute(x, SQUARE, pairs)


def masked(x, mask):
    return lax.ppermute(x, SQUARE, [(device, device ^ mask) for device in range(8)])


def swapped(x):
    return lax.ppermute(x, "core", [(0, 1), (1, 0)])


def gather_table(keep, give, core):
    size = lax.axis_size(LINE)
    got = swapped(give)
    block = jnp.concatenate([jnp.where(core == 0, keep, got), jnp.where(core == 0, got, keep)], axis=0)
    split = block.shape[1] * 3 // 4
    long, short = block[:, :split], block[:, split:]
    line = [long] + [shifted(long, k) for k in range(1, size)]
    short = jnp.concatenate([short, masked(short, 2), masked(short, 4), masked(short, 6)], axis=0)
    long = jnp.concatenate(line, axis=0)
    short, long = lax.optimization_barrier((short, long))
    first = crossed(long, 0)
    second = crossed(long, 1)
    shorts = [short] + [shifted(short, k) for k in range(1, size)]
    far_long, far_short = swapped(long), swapped(short)
    first, far_long, far_short, *shorts[1:-1] = lax.optimization_barrier((first, far_long, far_short, *shorts[1:-1]))
    both = crossed(first, 1)
    far_first, far_second = swapped(first), swapped(second)
    far_shorts = [far_short] + [swapped(x) for x in shorts[1:]]
    both, far_first, far_second, *far_shorts = lax.optimization_barrier((both, far_first, far_second, *far_shorts))
    return ([long, first, second, both], shorts), ([far_long, far_first, far_second, swapped(both)], far_shorts)


def places_of(ids, own):
    rest, size = lax.axis_size("rest"), lax.axis_size(LINE)
    owner = ids // own
    near = jnp.bitwise_xor(owner // 2 % 2, lax.axis_index("near"))
    mid = jnp.bitwise_xor(owner // (4 * rest) % 2, lax.axis_index("mid"))
    line = owner // (8 * rest) * rest + owner // 4 % rest
    line = lax.rem(lax.axis_index(LINE) - line + size, size)
    return ((2 * mid + near) * size + line) * (2 * own) + owner % 2 * own + ids % own


def relative_columns(matrix):
    zones, rest = matrix.shape[0], lax.axis_size("rest")
    if rest == 1:
        return matrix
    back = jnp.flip(matrix.reshape(zones, rest, -1), 1)
    back = jnp.concatenate([back, back], axis=1)
    return lax.dynamic_slice_in_dim(back, rest - 1 - lax.axis_index("rest"), rest, 1).reshape(zones, zones)


def shards(od_cells, anchor_edges, edge_weight, mixing, dst_edges, dst_weight, out_bias):
    n_org = lax.axis_size("slow") * lax.axis_size("mid")
    n_dst = lax.axis_size("rest") * lax.axis_size("near") * lax.axis_size("core")
    own = edge_weight.shape[0] // (n_org * n_dst)
    everyone = ("slow", "mid", "rest", "near", "core")
    core = lax.axis_index("core")
    edges_t = anchor_edges.T
    plan = Plan(od_cells.shape[1], edge_weight.shape[0], own, lax.axis_size("rest"), lax.axis_size(LINE))
    firsts, second, roots = org_sums(lax.axis_index(LINE), od_cells, edges_t, edge_weight, plan)
    own_weight = lax.dynamic_slice_in_dim(edge_weight, lax.axis_index(everyone) * own, own, 0)
    weight_rows = jnp.broadcast_to(own_weight[:, None], (own, mixing.shape[0]))
    matrix = relative_columns(dest_operator(dst_edges, dst_weight))
    half = matrix.shape[0] // 2
    matrix = jnp.where(core == 0, matrix, jnp.concatenate([matrix[half:], matrix[:half]], axis=0))
    keep, give = table_rows(firsts, second, weight_rows, mixing, matrix, plan)
    near, far = gather_table(keep, give, core)
    rows = anchor_edges.shape[0] // n_dst
    start = lax.axis_index(("rest", "near", "core")) * rows
    ids = lax.dynamic_slice_in_dim(edges_t, start, rows, 1)
    own_root = lax.dynamic_slice_in_dim(roots, start, rows, 1)
    return spread(core[None], places_of(ids, own), own_root, out_bias[None, :], near, far)


def solution(mesh):
    n_org, n_dst = mesh.devices.shape
    fine = Mesh(mesh.devices.reshape(n_org // 2, 2, n_dst // 4, 2, 2), ("slow", "mid", "rest", "near", "core"))
    org, dst = ("slow", "mid"), ("rest", "near", "core")
    in_specs = (P(org, dst, None), P(org, None), P(), P(), P(), P(), P())
    out_specs = P(org + dst, None, None)
    return jax.shard_map(shards, mesh=fine, in_specs=in_specs, out_specs=out_specs, check_vma=False)
```

```python
import functools

import jax
import jax.numpy as jnp
from jax import lax
from jax.experimental import pallas as pl
from jax.experimental.pallas import tpu as pltpu
from jax.sharding import Mesh, PartitionSpec as P

BF16 = jnp.bfloat16
F32 = jnp.float32
COUNT_BASE = 256.0
HEAD = 16
TILE = 16


def corridor_table(edge_ids, edge_count):
    columns = jnp.arange(edge_count, dtype=jnp.int32)
    return jnp.sum((edge_ids[:, :, None] == columns[None, None, :]).astype(F32), axis=1)


def dest_operator(dst_edges, dst_weight):
    dst_member = corridor_table(dst_edges, dst_weight.shape[0])
    dst_degree = jnp.sum(dst_member * dst_weight[None, :], axis=1)
    edge_sizes = jnp.sum(dst_member, axis=0)
    left_factor = dst_member * lax.rsqrt(dst_degree)[:, None]
    right_factor = left_factor * (dst_weight / edge_sizes)[None, :]
    result = jnp.dot(right_factor, left_factor.T, precision=lax.Precision.HIGHEST)
    return result.astype(BF16)


class Plan:
    def __init__(self, zones, edges, own, rest, line):
        self.edges = edges
        self.own = own
        self.rest = rest
        self.line = line
        self.cut = zones // 2
        self.first_rows = self.cut * own
        self.second_rows = HEAD + (zones - self.cut) * own

        self.relative = own % 8 == 0

    def device(self, square, line):
        core, near, mid = square % 2, square // 2 % 2, square // 4
        if isinstance(line, int):
            slow, rest = line // self.rest, line % self.rest
        else:
            slow, rest = lax.div(line, self.rest), lax.rem(line, self.rest)
        return (((slow * 2 + mid) * self.rest + rest) * 2 + near) * 2 + core


def halves_of(counts):
    high = jnp.floor(counts * (1.0 / COUNT_BASE))
    return high, counts - high * COUNT_BASE


def head_rows(high, low):
    parts = [high, low]
    if high.shape[0] < HEAD // 2:
        pad = jnp.zeros((HEAD // 2 - high.shape[0], high.shape[1]), F32)
        parts = [high, pad, low, pad]
    return jnp.concatenate(parts, axis=0).astype(BF16)


def one_hot(edges_ref, weight_ref, edges, lanes):
    ids = edges_ref[...]
    rows = ids.shape[1]
    columns = lax.broadcasted_iota(jnp.int32, (edges, rows), 0)
    member = columns == ids[0:1, :]
    for j in range(1, ids.shape[0]):
        member = jnp.logical_or(member, columns == ids[j : j + 1, :])
    upright = jnp.transpose(jnp.broadcast_to(weight_ref[...], (lanes, edges)))
    upright = jnp.concatenate([upright] * (rows // lanes), axis=1)
    root = lax.rsqrt(jnp.sum(jnp.where(member, upright, 0.0), axis=0, keepdims=True))
    rounded = root.astype(BF16).astype(F32)
    weighted = jnp.where(member, rounded, 0.0).astype(BF16)
    hot = jnp.where(member, 1.0, 0.0).astype(BF16)
    return root, weighted, jnp.dot(hot, jnp.ones((rows, lanes), BF16), preferred_element_type=F32)


def turn_rows(cells_ref, turned_ref):
    rows, zones, lanes = cells_ref.shape
    size = TILE * zones
    target = lax.broadcasted_iota(jnp.int32, (size, size), 0)
    source = lax.broadcasted_iota(jnp.int32, (size, size), 1)
    wanted = jnp.bitwise_and(target, TILE - 1) * zones + lax.shift_right_logical(target, 4)
    turn = jnp.where(source == wanted, 1.0, 0.0).astype(BF16)

    def block(i, carry):
        first = i * 2 * TILE
        left = cells_ref[pl.ds(first, TILE)].reshape(size, lanes)
        right = cells_ref[pl.ds(first + TILE, TILE)].reshape(size, lanes)
        both = jnp.dot(turn, jnp.concatenate([left, right], axis=1), preferred_element_type=F32).astype(BF16)
        for d in range(zones):
            at = slice(d % 2 * lanes, (d % 2 + 1) * lanes)
            piece = both[d * TILE : (d + 1) * TILE]
            turned_ref[d // 2, pl.ds(pl.multiple_of(first, TILE), TILE), at] = piece[:, :lanes]
            turned_ref[d // 2, pl.ds(pl.multiple_of(first + TILE, TILE), TILE), at] = piece[:, lanes:]
        return carry

    lax.fori_loop(0, rows // (2 * TILE), block, 0, unroll=4)


def accumulate(weighted, cells_ref, begin, zones, pitch, total_ref, wide_ref):
    rows, _, lanes = cells_ref.shape
    if zones == TILE:
        turn_rows(cells_ref, wide_ref)
        for pair in range(zones // 2):
            total_ref[pair] += jnp.dot(weighted, wide_ref[pair], preferred_element_type=F32)
        return
    part = 32

    def widen(i, carry):
        first = i * part
        piece = cells_ref[pl.ds(first, part), begin : begin + zones, :].astype(F32)
        for j in range(part):
            wide_ref[pl.ds(pl.multiple_of((first + j) * pitch, 8), zones), :] = piece[j]
        return carry

    lax.fori_loop(0, rows // part, widen, 0)
    for pair in range(zones // 2):
        left = wide_ref[pl.ds(2 * pair, rows, stride=pitch), :].astype(BF16)
        right = wide_ref[pl.ds(2 * pair + 1, rows, stride=pitch), :].astype(BF16)
        both = jnp.concatenate([left, right], axis=1)
        total_ref[pair] += jnp.dot(weighted, both, preferred_element_type=F32)


def columns_of(total_ref, at, zones, lanes):
    data = []
    for d in range(zones):
        data.append(total_ref[d // 2, at, (d % 2) * lanes : (d % 2 + 1) * lanes])
    return jnp.concatenate(data, axis=0).astype(BF16)


def rows_for(plan, square, shift, line_ref):
    own = plan.own
    if plan.relative:
        device = plan.device(square, lax.rem(line_ref[0] + shift, plan.line))
        return pl.ds(pl.multiple_of(device * own, own), own)
    device = plan.device(square, shift)
    return slice(device * own, (device + 1) * own)


def second_kernel(plan, begin, zones, pitch, line_ref, edges_ref, weight_ref, cells_ref, *refs):
    out_ref, root_ref, weighted_ref, total_ref, count_ref, wide_ref = refs
    lanes = cells_ref.shape[2]

    @pl.when(pl.program_id(0) == 0)
    def _():
        total_ref[...] = jnp.zeros_like(total_ref)
        count_ref[...] = jnp.zeros_like(count_ref)

    root, weighted, counts = one_hot(edges_ref, weight_ref, total_ref.shape[1], lanes)
    root_ref[...] = root
    weighted_ref[...] = weighted
    count_ref[...] += counts
    accumulate(weighted, cells_ref, begin, zones, pitch, total_ref, wide_ref)

    @pl.when(pl.program_id(0) == pl.num_programs(0) - 1)
    def _():
        for square in range(8):
            for shift in range(plan.line):
                at = rows_for(plan, square, shift, line_ref)
                out_ref[square, shift, HEAD:, :] = columns_of(total_ref, at, zones, lanes)
                out_ref[square, shift, 0:HEAD, :] = head_rows(*halves_of(count_ref[at, :]))


def first_kernel(plan, begin, zones, pitch, line_ref, weighted_ref, cells_ref, out_ref, total_ref, wide_ref):
    @pl.when(pl.program_id(0) == 0)
    def _():
        total_ref[...] = jnp.zeros_like(total_ref)

    accumulate(weighted_ref[...], cells_ref, begin, zones, pitch, total_ref, wide_ref)

    @pl.when(pl.program_id(0) == pl.num_programs(0) - 1)
    def _():
        for square in range(8):
            for shift in range(plan.line):
                at = rows_for(plan, square, shift, line_ref)
                out_ref[square, shift] = columns_of(total_ref, at, zones, cells_ref.shape[2])


def fixed(shape):
    return pl.BlockSpec(shape, lambda i: (0,) * len(shape))


def half_sums(kernel, plan, part, line, cells, operands, specs, outs, out_specs, counted):
    anchors, zones, lanes = cells.shape
    edges = plan.edges
    half = zones // 2
    rows = min(512, anchors)
    pitch = -(-half // 8) * 8 + 8
    if half % 16 == 0:
        block, begin = pl.BlockSpec((rows, half, lanes), lambda i: (i, part, 0)), 0
    else:
        block, begin = pl.BlockSpec((rows, zones, lanes), lambda i: (i, 0, 0)), part * half
    counts = [pltpu.VMEM((edges, lanes), F32)] if counted else []
    wide = pltpu.VMEM((rows * pitch, lanes), F32)
    if half == TILE:
        wide = pltpu.VMEM((half // 2, rows, 2 * lanes), BF16)
    return pl.pallas_call(
        functools.partial(kernel, plan, begin, half, pitch),
        grid=(anchors // rows,),
        in_specs=[pl.BlockSpec(memory_space=pltpu.SMEM)] + specs + [block],
        out_specs=out_specs,
        out_shape=outs,
        scratch_shapes=[pltpu.VMEM((half // 2, edges, 2 * lanes), F32)] + counts + [wide],
        compiler_params=pltpu.CompilerParams(vmem_limit_bytes=40 * 1024 * 1024),
        cost_estimate=pl.CostEstimate(
            flops=4 * anchors * edges * zones * lanes, bytes_accessed=2 * anchors * zones * lanes, transcendentals=0
        ),
    )(line[None], *operands, cells)


def second_sums(line, cells, edges_t, edge_weight, plan):
    anchors, _, lanes = cells.shape
    rows = min(512, anchors)
    edges = plan.edges
    shape = (8, plan.line, plan.second_rows, lanes)
    outs = [jax.ShapeDtypeStruct(shape, BF16)]
    outs += [jax.ShapeDtypeStruct((1, anchors), F32), jax.ShapeDtypeStruct((edges, anchors), BF16)]
    out_specs = [fixed(shape)]
    out_specs += [pl.BlockSpec((1, rows), lambda i: (0, i)), pl.BlockSpec((edges, rows), lambda i: (0, i))]
    specs = [pl.BlockSpec((edges_t.shape[0], rows), lambda i: (0, i)), fixed((1, edges))]
    operands = (edges_t, edge_weight[None, :])
    second, roots, weighted = half_sums(second_kernel, plan, 1, line, cells, operands, specs, outs, out_specs, True)
    return rolled(second, line, plan), roots, weighted


def rolled(parts, line, plan):
    if plan.relative:
        return parts
    return lax.dynamic_slice_in_dim(jnp.concatenate([parts, parts], axis=1), line, plan.line, 1)


def first_sums(line, cells, weighted, plan):
    rows = min(512, cells.shape[0])
    shape = (8, plan.line, plan.first_rows, cells.shape[2])
    specs = [pl.BlockSpec((plan.edges, rows), lambda i: (0, i))]
    out = jax.ShapeDtypeStruct(shape, BF16)
    return rolled(half_sums(first_kernel, plan, 0, line, cells, (weighted,), specs, out, fixed(shape), False), line, plan)


def add_up(pieces):
    total = pieces[0].astype(F32)
    for piece in pieces[1:]:
        total = total + piece.astype(F32)
    return total


def fold_kernel(plan, counted, part_ref, *outs):
    half = HEAD // 2
    for shift in range(plan.line):
        for quarter in range(4):
            total = add_up([part_ref[quarter, shift], part_ref[4 + quarter, shift]])
            if counted:
                outs[shift][quarter, 0:HEAD, :] = head_rows(*halves_of(total[0:half] * COUNT_BASE + total[half:HEAD]))
                outs[shift][quarter, HEAD:, :] = total[HEAD:].astype(BF16)
            else:
                outs[shift][quarter] = total.astype(BF16)


def fold(plan, counted, part):
    whole = pl.BlockSpec(memory_space=pltpu.VMEM)
    return pl.pallas_call(
        functools.partial(fold_kernel, plan, counted),
        in_specs=[whole],
        out_specs=[whole] * plan.line,
        out_shape=[jax.ShapeDtypeStruct((4,) + part.shape[2:], BF16)] * plan.line,
        compiler_params=pltpu.CompilerParams(vmem_limit_bytes=16 * 1024 * 1024),
        cost_estimate=pl.CostEstimate(flops=part.size, bytes_accessed=part.size * 4, transcendentals=0),
    )(part)


def along_line(parts):
    return [shifted(part, shift) if shift else part for shift, part in enumerate(parts)]


def org_sums(line, cells, edges_t, edge_weight, plan):
    second, roots, weighted = second_sums(line, cells, edges_t, edge_weight, plan)
    second = lax.all_to_all(second, SQUARE, split_axis=0, concat_axis=0, tiled=True)
    first = first_sums(line, cells, weighted, plan)
    first, second = lax.optimization_barrier((first, second))
    first = lax.all_to_all(first, SQUARE, split_axis=0, concat_axis=0, tiled=True)
    seconds = along_line(fold(plan, True, second))
    first, *seconds = lax.optimization_barrier((first, *seconds))
    firsts = along_line(fold(plan, False, first))
    return firsts, seconds, roots


def table_kernel(plan, weight_ref, mixing_ref, matrix_ref, *refs):
    firsts, seconds = refs[: plan.line], refs[plan.line : 2 * plan.line]
    keep_ref, give_ref, mixed_ref = refs[2 * plan.line :]
    own = plan.own
    lanes = mixing_ref.shape[0]
    half = HEAD // 2
    head = add_up([seconds[shift][0, 0:HEAD, :] for shift in range(0, plan.line, plan.rest)])
    counts = head[0:half] * COUNT_BASE + head[half:HEAD]
    scale = weight_ref[...] / counts[0:own]
    rows = plan.first_rows + plan.second_rows - HEAD
    zones = rows // own
    n_dst = 4 * plan.rest
    for k in range(n_dst):
        rest, quarter = k // 4, k % 4
        first = add_up([firsts[shift][quarter] for shift in range(rest, plan.line, plan.rest)])
        second = add_up([seconds[shift][quarter, HEAD:, :] for shift in range(rest, plan.line, plan.rest)])
        start = k * rows
        for total in (first, second):
            size = total.shape[0]
            totals = (total * jnp.concatenate([scale] * (size // own), axis=0)).astype(BF16)
            mixed = jnp.dot(totals, mixing_ref[...], preferred_element_type=F32)
            mixed_ref[start : start + size, :] = mixed
            start += size
    whole = n_dst * zones
    for e in range(own):
        mixed = mixed_ref[pl.ds(e, whole, stride=own), :] if own > 1 else mixed_ref[...]
        high = mixed.astype(BF16)
        low = (mixed - high.astype(F32)).astype(BF16)
        both = jnp.dot(matrix_ref[...], jnp.concatenate([high, low], axis=1), preferred_element_type=F32)
        result = (both[:, 0:lanes] + both[:, lanes : 2 * lanes]).astype(BF16)
        keep_ref[e] = result[0 : whole // 2]
        give_ref[e] = result[whole // 2 :]


def table_rows(firsts, seconds, weight_rows, mixing, matrix, plan):
    zones = matrix.shape[0]
    lanes = mixing.shape[0]
    whole = pl.BlockSpec(memory_space=pltpu.VMEM)
    half = jax.ShapeDtypeStruct((plan.own, zones // 2, lanes), BF16)
    return pl.pallas_call(
        functools.partial(table_kernel, plan),
        in_specs=[whole] * (3 + len(firsts) + len(seconds)),
        out_specs=[whole] * 2,
        out_shape=[half, half],
        scratch_shapes=[pltpu.VMEM((zones * plan.own, lanes), F32)],
        compiler_params=pltpu.CompilerParams(vmem_limit_bytes=32 * 1024 * 1024),
        cost_estimate=pl.CostEstimate(
            flops=8 * plan.own * zones * lanes * lanes, bytes_accessed=4 * zones * plan.own * lanes, transcendentals=0
        ),
    )(weight_rows, mixing, matrix, *firsts, *seconds)


def spread_kernel(n_long, n_short, half_ref, places_ref, root_ref, bias_ref, *refs):
    longs = refs[:n_long]
    shorts = refs[n_long : n_long + n_short]
    out_ref, table_ref, ring_ref, sems, ring_sems = refs[-5:]
    slots, rows, zones, lanes = ring_ref.shape
    steps = out_ref.shape[0] // rows
    half = half_ref[0]

    copies = []

    def bring(source, first, start):
        place = table_ref.at[pl.ds(first, source.shape[0]), pl.ds(start, source.shape[1]), :]
        copies.append(pltpu.make_async_copy(source, place, sems.at[len(copies)]))

    split = longs[0].shape[1]
    size = shorts[0].shape[0] // n_long
    for square, source in enumerate(longs):
        bring(source, square * n_short * size, 0)
    for shift, source in enumerate(shorts):
        for square in range(n_long):
            bring(source.at[pl.ds(square * size, size)], (square * n_short + shift) * size, split)
    for copy in copies:
        copy.start()
    for copy in copies:
        copy.wait()

    bias = bias_ref[...]
    count = places_ref.shape[0]
    tile = 16
    batch = min(8, rows)
    tiles = zones // tile

    def leaving(step, slot):
        place = out_ref.at[pl.ds(step * rows, rows), pl.ds(pl.multiple_of(half * zones, zones), zones), :]
        return pltpu.make_async_copy(ring_ref.at[slot], place, ring_sems.at[slot])

    def one_step(step, carry):
        slot = lax.rem(step, slots)

        @pl.when(step >= slots)
        def _():
            leaving(step - slots, slot).wait()

        def several(group, inner):
            values = []
            for i in range(batch):
                at = step * rows + group * batch + i
                scale = root_ref[0, at]
                spots = [places_ref[j, at] for j in range(count)]
                for first in range(0, zones, tile):
                    pieces = [table_ref[spot, first : first + tile, :] for spot in spots]
                    pieces = [(a + b).astype(F32) for a, b in zip(pieces[0::2], pieces[1::2])]
                    total = sum(pieces[1:], pieces[0])
                    values.append(jnp.maximum((total * scale + bias).astype(BF16), BF16(0.0)))
            for n, value in enumerate(values):
                start = n % tiles * tile
                ring_ref[slot, group * batch + n // tiles, start : start + tile, :] = value
            return inner

        lax.fori_loop(0, rows // batch, several, 0)
        leaving(step, slot).start()
        return carry

    lax.fori_loop(0, steps, one_step, 0)
    for step in range(steps - slots, steps):
        leaving(step, step % slots).wait()


def spread(half, places, root, bias, longs, shorts, before=None):
    anchors = places.shape[1]
    lanes = bias.shape[1]
    zones = longs[0].shape[1] + shorts[0].shape[1]
    rows = min(16, anchors // 8)
    slots = min(8, anchors // rows)
    smem = pl.BlockSpec(memory_space=pltpu.SMEM)
    anywhere = pl.BlockSpec(memory_space=pltpu.HBM)
    pieces = longs + shorts
    operands = [half, places, root, bias] + pieces
    specs = [smem, smem, smem, pl.BlockSpec(memory_space=pltpu.VMEM)] + [anywhere] * len(pieces)
    aliases = {}
    if before is not None:
        aliases = {len(operands): 0}
        operands.append(before)
        specs.append(anywhere)
    return pl.pallas_call(
        functools.partial(spread_kernel, len(longs), len(shorts)),
        in_specs=specs,
        out_specs=anywhere,
        out_shape=jax.ShapeDtypeStruct((anchors, 2 * zones, lanes), BF16),
        scratch_shapes=[
            pltpu.VMEM((len(longs) * longs[0].shape[0], zones, lanes), BF16),
            pltpu.VMEM((slots, rows, zones, lanes), BF16),
            pltpu.SemaphoreType.DMA((len(longs) * (1 + len(shorts)),)),
            pltpu.SemaphoreType.DMA((slots,)),
        ],
        input_output_aliases=aliases,
        compiler_params=pltpu.CompilerParams(vmem_limit_bytes=24 * 1024 * 1024),
        cost_estimate=pl.CostEstimate(
            flops=4096 * anchors * zones * lanes, bytes_accessed=4 * anchors * zones * lanes, transcendentals=0
        ),
    )(*operands)


LINE = ("slow", "rest")
SQUARE = ("mid", "near", "core")


def shifted(x, amount):
    size = lax.axis_size(LINE)
    return lax.ppermute(x, LINE, [(i, (i + amount) % size) for i in range(size)])


def crossed(x, turn):
    pairs = []
    for device in range(8):
        core = device % 2
        pairs.append((device, device ^ (2 if core == turn else 4)))
    return lax.ppermute(x, SQUARE, pairs)


def masked(x, mask):
    return lax.ppermute(x, SQUARE, [(device, device ^ mask) for device in range(8)])


def swapped(x):
    return lax.ppermute(x, "core", [(0, 1), (1, 0)])


def gather_table(keep, give):
    size = lax.axis_size(LINE)
    block = jnp.concatenate([keep, swapped(give)], axis=0)
    split = block.shape[1] * 3 // 4
    long, short = block[:, :split], block[:, split:]
    line = [long] + [shifted(long, k) for k in range(1, size)]
    short = jnp.concatenate([short, crossed(short, 0), crossed(short, 1), masked(short, 6)], axis=0)
    long = jnp.concatenate(line, axis=0)
    short, long = lax.optimization_barrier((short, long))
    first = crossed(long, 0)
    second = crossed(long, 1)
    shorts = [short] + [shifted(short, k) for k in range(1, size)]
    first, *shorts[1:-1] = lax.optimization_barrier((first, *shorts[1:-1]))
    both = crossed(first, 1)
    return [long, first, second, both], shorts


def places_of(ids, core, own):
    rest, size = lax.axis_size("rest"), lax.axis_size(LINE)
    owner = ids // own
    slot = jnp.where(owner % 2 == core, 0, own) + ids % own
    near = jnp.bitwise_xor(owner // 2 % 2, lax.axis_index("near"))
    mid = jnp.bitwise_xor(owner // (4 * rest) % 2, lax.axis_index("mid"))
    line = owner // (8 * rest) * rest + owner // 4 % rest
    line = lax.rem(lax.axis_index(LINE) - line + size, size)
    square = jnp.where(core == 0, 2 * mid + near, 2 * near + mid)
    return (square * size + line) * (2 * own) + slot


def relative_columns(matrix):
    zones, rest = matrix.shape[0], lax.axis_size("rest")
    if rest == 1:
        return matrix
    back = jnp.flip(matrix.reshape(zones, rest, -1), 1)
    back = jnp.concatenate([back, back], axis=1)
    return lax.dynamic_slice_in_dim(back, rest - 1 - lax.axis_index("rest"), rest, 1).reshape(zones, zones)


def shards(od_cells, anchor_edges, edge_weight, mixing, dst_edges, dst_weight, out_bias):
    n_org = lax.axis_size("slow") * lax.axis_size("mid")
    n_dst = lax.axis_size("rest") * lax.axis_size("near") * lax.axis_size("core")
    own = edge_weight.shape[0] // (n_org * n_dst)
    everyone = ("slow", "mid", "rest", "near", "core")
    core = lax.axis_index("core")
    edges_t = anchor_edges.T
    plan = Plan(od_cells.shape[1], edge_weight.shape[0], own, lax.axis_size("rest"), lax.axis_size(LINE))
    firsts, seconds, roots = org_sums(lax.axis_index(LINE), od_cells, edges_t, edge_weight, plan)
    own_weight = lax.dynamic_slice_in_dim(edge_weight, lax.axis_index(everyone) * own, own, 0)
    weight_rows = jnp.broadcast_to(own_weight[:, None], (own, mixing.shape[0]))
    matrix = relative_columns(dest_operator(dst_edges, dst_weight))
    half = matrix.shape[0] // 2
    matrix = jnp.where(core == 0, matrix, jnp.concatenate([matrix[half:], matrix[:half]], axis=0))
    keep, give = table_rows(firsts, seconds, weight_rows, mixing, matrix, plan)
    longs, shorts = gather_table(keep, give)
    rows = anchor_edges.shape[0] // n_dst
    start = lax.axis_index(("rest", "near", "core")) * rows
    ids = lax.dynamic_slice_in_dim(edges_t, start, rows, 1)
    own_root = lax.dynamic_slice_in_dim(roots, start, rows, 1)
    bias = out_bias[None, :]
    other = 1 - core
    result = spread(core[None], places_of(ids, core, own), own_root, bias, longs, shorts)
    longs, shorts = [swapped(x) for x in longs], [swapped(x) for x in shorts]
    return spread(other[None], places_of(ids, other, own), own_root, bias, longs, shorts, result)


def solution(mesh):
    n_org, n_dst = mesh.devices.shape
    fine = Mesh(mesh.devices.reshape(n_org // 2, 2, n_dst // 4, 2, 2), ("slow", "mid", "rest", "near", "core"))
    org, dst = ("slow", "mid"), ("rest", "near", "core")
    in_specs = (P(org, dst, None), P(org, None), P(), P(), P(), P(), P())
    out_specs = P(org + dst, None, None)
    return jax.shard_map(shards, mesh=fine, in_specs=in_specs, out_specs=out_specs, check_vma=False)
```

```python
import functools

import jax
import jax.numpy as jnp
from jax import lax
from jax.experimental import pallas as pl
from jax.experimental.pallas import tpu as pltpu
from jax.sharding import Mesh, PartitionSpec as P

BF16 = jnp.bfloat16
F32 = jnp.float32
COUNT_BASE = 256.0
HEAD = 16


def corridor_table(edge_ids, edge_count):
    columns = jnp.arange(edge_count, dtype=jnp.int32)
    return jnp.sum((edge_ids[:, :, None] == columns[None, None, :]).astype(F32), axis=1)


def dest_operator(dst_edges, dst_weight):
    dst_member = corridor_table(dst_edges, dst_weight.shape[0])
    dst_degree = jnp.sum(dst_member * dst_weight[None, :], axis=1)
    edge_sizes = jnp.sum(dst_member, axis=0)
    left_factor = dst_member * lax.rsqrt(dst_degree)[:, None]
    right_factor = left_factor * (dst_weight / edge_sizes)[None, :]
    result = jnp.dot(right_factor, left_factor.T, precision=lax.Precision.HIGHEST)
    return result.astype(BF16)


class Plan:
    def __init__(self, zones, edges, own, rest, line):
        self.edges = edges
        self.own = own
        self.rest = rest
        self.line = line
        self.cut = zones // 2
        self.first_rows = self.cut * own
        self.second_rows = HEAD + (zones - self.cut) * own

        self.relative = own % 8 == 0

    def device(self, square, line):
        core, near, mid = square % 2, square // 2 % 2, square // 4
        if isinstance(line, int):
            slow, rest = line // self.rest, line % self.rest
        else:
            slow, rest = lax.div(line, self.rest), lax.rem(line, self.rest)
        return (((slow * 2 + mid) * self.rest + rest) * 2 + near) * 2 + core


def halves_of(counts):
    high = jnp.floor(counts * (1.0 / COUNT_BASE))
    return high, counts - high * COUNT_BASE


def head_rows(high, low):
    parts = [high, low]
    if high.shape[0] < HEAD // 2:
        pad = jnp.zeros((HEAD // 2 - high.shape[0], high.shape[1]), F32)
        parts = [high, pad, low, pad]
    return jnp.concatenate(parts, axis=0).astype(BF16)


def one_hot(edges_ref, weight_ref, edges, lanes):
    ids = edges_ref[...]
    rows = ids.shape[1]
    columns = lax.broadcasted_iota(jnp.int32, (edges, rows), 0)
    member = columns == ids[0:1, :]
    for j in range(1, ids.shape[0]):
        member = jnp.logical_or(member, columns == ids[j : j + 1, :])
    upright = jnp.transpose(jnp.broadcast_to(weight_ref[...], (lanes, edges)))
    upright = jnp.concatenate([upright] * (rows // lanes), axis=1)
    root = lax.rsqrt(jnp.sum(jnp.where(member, upright, 0.0), axis=0, keepdims=True))
    rounded = root.astype(BF16).astype(F32)
    weighted = jnp.where(member, rounded, 0.0).astype(BF16)
    hot = jnp.where(member, 1.0, 0.0).astype(BF16)
    return root, weighted, jnp.dot(hot, jnp.ones((rows, lanes), BF16), preferred_element_type=F32)


def accumulate(weighted, cells_ref, begin, zones, pitch, total_ref, wide_ref):
    rows, _, lanes = cells_ref.shape
    part = 32

    def widen(i, carry):
        first = i * part
        piece = cells_ref[pl.ds(first, part), begin : begin + zones, :].astype(F32)
        for j in range(part):
            wide_ref[pl.ds(pl.multiple_of((first + j) * pitch, 8), zones), :] = piece[j]
        return carry

    lax.fori_loop(0, rows // part, widen, 0)
    for pair in range(zones // 2):
        left = wide_ref[pl.ds(2 * pair, rows, stride=pitch), :].astype(BF16)
        right = wide_ref[pl.ds(2 * pair + 1, rows, stride=pitch), :].astype(BF16)
        both = jnp.concatenate([left, right], axis=1)
        total_ref[pair] += jnp.dot(weighted, both, preferred_element_type=F32)


def columns_of(total_ref, at, zones, lanes):
    data = []
    for d in range(zones):
        data.append(total_ref[d // 2, at, (d % 2) * lanes : (d % 2 + 1) * lanes])
    return jnp.concatenate(data, axis=0).astype(BF16)


def rows_for(plan, square, shift, line_ref):
    own = plan.own
    if plan.relative:
        device = plan.device(square, lax.rem(line_ref[0] + shift, plan.line))
        return pl.ds(pl.multiple_of(device * own, own), own)
    device = plan.device(square, shift)
    return slice(device * own, (device + 1) * own)


def second_kernel(plan, begin, zones, pitch, line_ref, edges_ref, weight_ref, cells_ref, *refs):
    out_refs = refs[: plan.line]
    root_ref, weighted_ref, total_ref, count_ref, wide_ref = refs[plan.line :]
    lanes = cells_ref.shape[2]

    @pl.when(pl.program_id(0) == 0)
    def _():
        total_ref[...] = jnp.zeros_like(total_ref)
        count_ref[...] = jnp.zeros_like(count_ref)

    root, weighted, counts = one_hot(edges_ref, weight_ref, total_ref.shape[1], lanes)
    root_ref[...] = root
    weighted_ref[...] = weighted
    count_ref[...] += counts
    accumulate(weighted, cells_ref, begin, zones, pitch, total_ref, wide_ref)

    @pl.when(pl.program_id(0) == pl.num_programs(0) - 1)
    def _():
        for square in range(8):
            for shift in range(plan.line):
                at = rows_for(plan, square, shift, line_ref)
                out_refs[shift][square, HEAD:, :] = columns_of(total_ref, at, zones, lanes)
                out_refs[shift][square, 0:HEAD, :] = head_rows(*halves_of(count_ref[at, :]))


def first_kernel(plan, begin, zones, pitch, line_ref, weighted_ref, cells_ref, out_ref, total_ref, wide_ref):
    @pl.when(pl.program_id(0) == 0)
    def _():
        total_ref[...] = jnp.zeros_like(total_ref)

    accumulate(weighted_ref[...], cells_ref, begin, zones, pitch, total_ref, wide_ref)

    @pl.when(pl.program_id(0) == pl.num_programs(0) - 1)
    def _():
        for square in range(8):
            for shift in range(plan.line):
                at = rows_for(plan, square, shift, line_ref)
                out_ref[square, shift] = columns_of(total_ref, at, zones, cells_ref.shape[2])


def fixed(shape):
    return pl.BlockSpec(shape, lambda i: (0,) * len(shape))


def half_sums(kernel, plan, part, line, cells, operands, specs, outs, out_specs, counted):
    anchors, zones, lanes = cells.shape
    edges = plan.edges
    half = zones // 2
    rows = min(512, anchors)
    pitch = -(-half // 8) * 8 + 8
    if half % 16 == 0:
        block, begin = pl.BlockSpec((rows, half, lanes), lambda i: (i, part, 0)), 0
    else:
        block, begin = pl.BlockSpec((rows, zones, lanes), lambda i: (i, 0, 0)), part * half
    counts = [pltpu.VMEM((edges, lanes), F32)] if counted else []
    return pl.pallas_call(
        functools.partial(kernel, plan, begin, half, pitch),
        grid=(anchors // rows,),
        in_specs=[pl.BlockSpec(memory_space=pltpu.SMEM)] + specs + [block],
        out_specs=out_specs,
        out_shape=outs,
        scratch_shapes=[pltpu.VMEM((half // 2, edges, 2 * lanes), F32)] + counts + [pltpu.VMEM((rows * pitch, lanes), F32)],
        compiler_params=pltpu.CompilerParams(vmem_limit_bytes=40 * 1024 * 1024),
        cost_estimate=pl.CostEstimate(
            flops=4 * anchors * edges * zones * lanes, bytes_accessed=2 * anchors * zones * lanes, transcendentals=0
        ),
    )(line[None], *operands, cells)


def second_sums(line, cells, edges_t, edge_weight, plan):
    anchors, _, lanes = cells.shape
    rows = min(512, anchors)
    edges = plan.edges
    shape = (8, plan.second_rows, lanes)
    outs = [jax.ShapeDtypeStruct(shape, BF16)] * plan.line
    outs += [jax.ShapeDtypeStruct((1, anchors), F32), jax.ShapeDtypeStruct((edges, anchors), BF16)]
    out_specs = [fixed(shape)] * plan.line
    out_specs += [pl.BlockSpec((1, rows), lambda i: (0, i)), pl.BlockSpec((edges, rows), lambda i: (0, i))]
    specs = [pl.BlockSpec((edges_t.shape[0], rows), lambda i: (0, i)), fixed((1, edges))]
    operands = (edges_t, edge_weight[None, :])
    *seconds, roots, weighted = half_sums(second_kernel, plan, 1, line, cells, operands, specs, outs, out_specs, True)
    if not plan.relative:
        seconds = jnp.stack(seconds * 2)
        seconds = [lax.dynamic_index_in_dim(seconds, line + k, 0, keepdims=False) for k in range(plan.line)]
    return seconds, roots, weighted


def first_sums(line, cells, weighted, plan):
    rows = min(512, cells.shape[0])
    shape = (8, plan.line, plan.first_rows, cells.shape[2])
    specs = [pl.BlockSpec((plan.edges, rows), lambda i: (0, i))]
    out = jax.ShapeDtypeStruct(shape, BF16)
    first = half_sums(first_kernel, plan, 0, line, cells, (weighted,), specs, out, fixed(shape), False)
    if not plan.relative:
        first = lax.dynamic_slice_in_dim(jnp.concatenate([first, first], axis=1), line, plan.line, 1)
    return first


def add_up(pieces):
    total = pieces[0].astype(F32)
    for piece in pieces[1:]:
        total = total + piece.astype(F32)
    return total


def fold_first_kernel(plan, part_ref, *outs):
    for shift in range(plan.line):
        for quarter in range(4):
            outs[shift][quarter] = add_up([part_ref[quarter, shift], part_ref[4 + quarter, shift]]).astype(BF16)


def fold_second_kernel(plan, *refs):
    parts, out_ref = refs[: plan.line], refs[plan.line]
    for square in range(8):
        for rest in range(plan.rest):
            total = add_up([parts[shift][square] for shift in range(rest, plan.line, plan.rest)])
            half = HEAD // 2
            out_ref[square, rest, 0:HEAD, :] = head_rows(*halves_of(total[0:half] * COUNT_BASE + total[half:HEAD]))
            out_ref[square, rest, HEAD:, :] = total[HEAD:].astype(BF16)


def fold(kernel, plan, parts, shapes):
    whole = pl.BlockSpec(memory_space=pltpu.VMEM)
    size = sum(part.size for part in parts)
    return pl.pallas_call(
        functools.partial(kernel, plan),
        in_specs=[whole] * len(parts),
        out_specs=[whole] * len(shapes),
        out_shape=[jax.ShapeDtypeStruct(shape, BF16) for shape in shapes],
        compiler_params=pltpu.CompilerParams(vmem_limit_bytes=16 * 1024 * 1024),
        cost_estimate=pl.CostEstimate(flops=size, bytes_accessed=size * 4, transcendentals=0),
    )(*parts)


def org_sums(line, cells, edges_t, edge_weight, plan):
    lanes = cells.shape[-1]
    seconds, roots, weighted = second_sums(line, cells, edges_t, edge_weight, plan)
    seconds = [shifted(part, shift) if shift else part for shift, part in enumerate(seconds)]
    first = first_sums(line, cells, weighted, plan)
    first, seconds[1] = lax.optimization_barrier((first, seconds[1]))
    first = lax.all_to_all(first, SQUARE, split_axis=0, concat_axis=0, tiled=True)
    firsts = fold(fold_first_kernel, plan, [first], [(4, plan.first_rows, lanes)] * plan.line)
    firsts = [shifted(part, shift) if shift else part for shift, part in enumerate(firsts)]
    *firsts[1:3], seconds[2] = lax.optimization_barrier((*firsts[1:3], seconds[2]))
    second = fold(fold_second_kernel, plan, seconds, [(8, plan.rest, plan.second_rows, lanes)])[0]
    second = lax.all_to_all(second, SQUARE, split_axis=0, concat_axis=0, tiled=True)
    return firsts, second, roots


def table_kernel(plan, weight_ref, mixing_ref, matrix_ref, *refs):
    firsts = refs[: plan.line]
    second_ref, keep_ref, give_ref, mixed_ref = refs[plan.line :]
    own = plan.own
    lanes = mixing_ref.shape[0]
    half = HEAD // 2
    head = add_up([second_ref[0, 0, 0:HEAD, :], second_ref[4, 0, 0:HEAD, :]])
    counts = head[0:half] * COUNT_BASE + head[half:HEAD]
    scale = weight_ref[...] / counts[0:own]
    rows = plan.first_rows + plan.second_rows - HEAD
    zones = rows // own
    n_dst = 4 * plan.rest
    for k in range(n_dst):
        rest, quarter = k // 4, k % 4
        first = add_up([firsts[shift][quarter] for shift in range(rest, plan.line, plan.rest)])
        second = add_up([second_ref[quarter, rest, HEAD:, :], second_ref[4 + quarter, rest, HEAD:, :]])
        start = k * rows
        for total in (first, second):
            size = total.shape[0]
            totals = (total * jnp.concatenate([scale] * (size // own), axis=0)).astype(BF16)
            mixed = jnp.dot(totals, mixing_ref[...], preferred_element_type=F32)
            mixed_ref[start : start + size, :] = mixed
            start += size
    whole = n_dst * zones
    for e in range(own):
        mixed = mixed_ref[pl.ds(e, whole, stride=own), :] if own > 1 else mixed_ref[...]
        high = mixed.astype(BF16)
        low = (mixed - high.astype(F32)).astype(BF16)
        both = jnp.dot(matrix_ref[...], jnp.concatenate([high, low], axis=1), preferred_element_type=F32)
        result = (both[:, 0:lanes] + both[:, lanes : 2 * lanes]).astype(BF16)
        keep_ref[e] = result[0 : whole // 2]
        give_ref[e] = result[whole // 2 :]


def table_rows(firsts, second, weight_rows, mixing, matrix, plan):
    zones = matrix.shape[0]
    lanes = mixing.shape[0]
    whole = pl.BlockSpec(memory_space=pltpu.VMEM)
    half = jax.ShapeDtypeStruct((plan.own, zones // 2, lanes), BF16)
    return pl.pallas_call(
        functools.partial(table_kernel, plan),
        in_specs=[whole] * (4 + len(firsts)),
        out_specs=[whole] * 2,
        out_shape=[half, half],
        scratch_shapes=[pltpu.VMEM((zones * plan.own, lanes), F32)],
        compiler_params=pltpu.CompilerParams(vmem_limit_bytes=32 * 1024 * 1024),
        cost_estimate=pl.CostEstimate(
            flops=8 * plan.own * zones * lanes * lanes, bytes_accessed=4 * zones * plan.own * lanes, transcendentals=0
        ),
    )(weight_rows, mixing, matrix, *firsts, second)


def spread_kernel(n_long, n_short, core_ref, places_ref, root_ref, bias_ref, *refs):
    pieces = refs[: 2 * (n_long + n_short)]
    out_ref, table_ref, ring_ref, sems, ring_sems = refs[-5:]
    slots, rows, zones, lanes = ring_ref.shape
    steps = out_ref.shape[0] // rows
    half = zones // 2
    copies = []

    def bring(source, first, start):
        size, height = source.shape[0], source.shape[1]
        place = table_ref.at[pl.ds(first, size), pl.ds(pl.multiple_of(start, 16), height), :]
        copies.append(pltpu.make_async_copy(source, place, sems.at[len(copies)]))

    for side in range(2):
        core = core_ref[0] if side == 0 else 1 - core_ref[0]
        longs = pieces[side * (n_long + n_short) :][:n_long]
        shorts = pieces[side * (n_long + n_short) + n_long :][:n_short]
        split = longs[0].shape[1]
        size = shorts[0].shape[0] // n_long
        for turn, source in enumerate(longs):
            square = turn if turn in (0, 3) else turn + core * (3 - 2 * turn)
            bring(source, square * (n_short * size), core * half)
        for shift, source in enumerate(shorts):
            for square in range(n_long):
                bring(source.at[pl.ds(square * size, size)], (square * n_short + shift) * size, core * half + split)
    for copy in copies:
        copy.start()
    for copy in copies:
        copy.wait()

    bias = bias_ref[...]
    count = places_ref.shape[0]
    tile = 16
    batch = min(4, rows)
    tiles = zones // tile

    def leaving(step, slot):
        return pltpu.make_async_copy(ring_ref.at[slot], out_ref.at[pl.ds(step * rows, rows)], ring_sems.at[slot])

    def one_step(step, carry):
        slot = lax.rem(step, slots)

        @pl.when(step >= slots)
        def _():
            leaving(step - slots, slot).wait()

        def several(group, inner):
            values = []
            for i in range(batch):
                at = step * rows + group * batch + i
                scale = root_ref[0, at]
                spots = [places_ref[j, at] for j in range(count)]
                for first in range(0, zones, tile):
                    parts = [table_ref[spot, first : first + tile, :] for spot in spots]
                    parts = [(a + b).astype(F32) for a, b in zip(parts[0::2], parts[1::2])]
                    total = sum(parts[1:], parts[0])
                    values.append(jnp.maximum((total * scale + bias).astype(BF16), BF16(0.0)))
            for n, value in enumerate(values):
                start = n % tiles * tile
                ring_ref[slot, group * batch + n // tiles, start : start + tile, :] = value
            return inner

        lax.fori_loop(0, rows // batch, several, 0)
        leaving(step, slot).start()
        return carry

    lax.fori_loop(0, steps, one_step, 0)
    for step in range(steps - slots, steps):
        leaving(step, step % slots).wait()


def spread(core, places, root, bias, near, far):
    anchors = places.shape[1]
    lanes = bias.shape[1]
    longs, shorts = near
    zones = 2 * (longs[0].shape[1] + shorts[0].shape[1])
    edges = len(longs) * longs[0].shape[0]
    rows = min(16, anchors // 8)
    slots = min(4, anchors // rows)
    smem = pl.BlockSpec(memory_space=pltpu.SMEM)
    anywhere = pl.BlockSpec(memory_space=pltpu.HBM)
    pieces = longs + shorts + far[0] + far[1]
    return pl.pallas_call(
        functools.partial(spread_kernel, len(longs), len(shorts)),
        in_specs=[smem, smem, smem, pl.BlockSpec(memory_space=pltpu.VMEM)] + [anywhere] * len(pieces),
        out_specs=anywhere,
        out_shape=jax.ShapeDtypeStruct((anchors, zones, lanes), BF16),
        scratch_shapes=[
            pltpu.VMEM((edges, zones, lanes), BF16),
            pltpu.VMEM((slots, rows, zones, lanes), BF16),
            pltpu.SemaphoreType.DMA((2 * len(longs) * (1 + len(shorts)),)),
            pltpu.SemaphoreType.DMA((slots,)),
        ],
        compiler_params=pltpu.CompilerParams(vmem_limit_bytes=12 * 1024 * 1024),
        cost_estimate=pl.CostEstimate(
            flops=4096 * anchors * zones * lanes, bytes_accessed=4 * anchors * zones * lanes, transcendentals=0
        ),
    )(core, places, root, bias, *pieces)


LINE = ("slow", "rest")
SQUARE = ("mid", "near", "core")


def shifted(x, amount):
    size = lax.axis_size(LINE)
    return lax.ppermute(x, LINE, [(i, (i + amount) % size) for i in range(size)])


def crossed(x, turn):
    pairs = []
    for device in range(8):
        core = device % 2
        pairs.append((device, device ^ (2 if core == turn else 4)))
    return lax.ppermute(x, SQUARE, pairs)


def masked(x, mask):
    return lax.ppermute(x, SQUARE, [(device, device ^ mask) for device in range(8)])


def swapped(x):
    return lax.ppermute(x, "core", [(0, 1), (1, 0)])


def gather_table(keep, give, core):
    size = lax.axis_size(LINE)
    got = swapped(give)
    block = jnp.concatenate([jnp.where(core == 0, keep, got), jnp.where(core == 0, got, keep)], axis=0)
    split = block.shape[1] * 3 // 4
    long, short = block[:, :split], block[:, split:]
    line = [long] + [shifted(long, k) for k in range(1, size)]
    short = jnp.concatenate([short, masked(short, 2), masked(short, 4), masked(short, 6)], axis=0)
    long = jnp.concatenate(line, axis=0)
    short, long = lax.optimization_barrier((short, long))
    first = crossed(long, 0)
    second = crossed(long, 1)
    shorts = [short] + [shifted(short, k) for k in range(1, size)]
    far_long, far_short = swapped(long), swapped(short)
    first, far_long, far_short, *shorts[1:-1] = lax.optimization_barrier((first, far_long, far_short, *shorts[1:-1]))
    both = crossed(first, 1)
    far_first, far_second = swapped(first), swapped(second)
    far_shorts = [far_short] + [swapped(x) for x in shorts[1:]]
    both, far_first, far_second, *far_shorts = lax.optimization_barrier((both, far_first, far_second, *far_shorts))
    return ([long, first, second, both], shorts), ([far_long, far_first, far_second, swapped(both)], far_shorts)


def places_of(ids, own):
    rest, size = lax.axis_size("rest"), lax.axis_size(LINE)
    owner = ids // own
    near = jnp.bitwise_xor(owner // 2 % 2, lax.axis_index("near"))
    mid = jnp.bitwise_xor(owner // (4 * rest) % 2, lax.axis_index("mid"))
    line = owner // (8 * rest) * rest + owner // 4 % rest
    line = lax.rem(lax.axis_index(LINE) - line + size, size)
    return ((2 * mid + near) * size + line) * (2 * own) + owner % 2 * own + ids % own


def relative_columns(matrix):
    zones, rest = matrix.shape[0], lax.axis_size("rest")
    if rest == 1:
        return matrix
    back = jnp.flip(matrix.reshape(zones, rest, -1), 1)
    back = jnp.concatenate([back, back], axis=1)
    return lax.dynamic_slice_in_dim(back, rest - 1 - lax.axis_index("rest"), rest, 1).reshape(zones, zones)


def shards(od_cells, anchor_edges, edge_weight, mixing, dst_edges, dst_weight, out_bias):
    n_org = lax.axis_size("slow") * lax.axis_size("mid")
    n_dst = lax.axis_size("rest") * lax.axis_size("near") * lax.axis_size("core")
    own = edge_weight.shape[0] // (n_org * n_dst)
    everyone = ("slow", "mid", "rest", "near", "core")
    core = lax.axis_index("core")
    edges_t = anchor_edges.T
    plan = Plan(od_cells.shape[1], edge_weight.shape[0], own, lax.axis_size("rest"), lax.axis_size(LINE))
    firsts, second, roots = org_sums(lax.axis_index(LINE), od_cells, edges_t, edge_weight, plan)
    own_weight = lax.dynamic_slice_in_dim(edge_weight, lax.axis_index(everyone) * own, own, 0)
    weight_rows = jnp.broadcast_to(own_weight[:, None], (own, mixing.shape[0]))
    matrix = relative_columns(dest_operator(dst_edges, dst_weight))
    half = matrix.shape[0] // 2
    matrix = jnp.where(core == 0, matrix, jnp.concatenate([matrix[half:], matrix[:half]], axis=0))
    keep, give = table_rows(firsts, second, weight_rows, mixing, matrix, plan)
    near, far = gather_table(keep, give, core)
    rows = anchor_edges.shape[0] // n_dst
    start = lax.axis_index(("rest", "near", "core")) * rows
    ids = lax.dynamic_slice_in_dim(edges_t, start, rows, 1)
    own_root = lax.dynamic_slice_in_dim(roots, start, rows, 1)
    return spread(core[None], places_of(ids, own), own_root, out_bias[None, :], near, far)


def solution(mesh):
    n_org, n_dst = mesh.devices.shape
    fine = Mesh(mesh.devices.reshape(n_org // 2, 2, n_dst // 4, 2, 2), ("slow", "mid", "rest", "near", "core"))
    org, dst = ("slow", "mid"), ("rest", "near", "core")
    in_specs = (P(org, dst, None), P(org, None), P(), P(), P(), P(), P())
    out_specs = P(org + dst, None, None)
    return jax.shard_map(shards, mesh=fine, in_specs=in_specs, out_specs=out_specs, check_vma=False)
```

```python
import functools

import jax
import jax.numpy as jnp
from jax import lax
from jax.experimental import pallas as pl
from jax.experimental.pallas import tpu as pltpu
from jax.sharding import Mesh, PartitionSpec as P

BF16 = jnp.bfloat16
F32 = jnp.float32
COUNT_BASE = 256.0
HEAD = 16


def corridor_table(edge_ids, edge_count):
    columns = jnp.arange(edge_count, dtype=jnp.int32)
    return jnp.sum((edge_ids[:, :, None] == columns[None, None, :]).astype(F32), axis=1)


def dest_operator(dst_edges, dst_weight):
    dst_member = corridor_table(dst_edges, dst_weight.shape[0])
    dst_degree = jnp.sum(dst_member * dst_weight[None, :], axis=1)
    edge_sizes = jnp.sum(dst_member, axis=0)
    left_factor = dst_member * lax.rsqrt(dst_degree)[:, None]
    right_factor = left_factor * (dst_weight / edge_sizes)[None, :]
    result = jnp.dot(right_factor, left_factor.T, precision=lax.Precision.HIGHEST)
    return result.astype(BF16)


class Plan:
    def __init__(self, zones, edges, own, rest, line):
        self.edges = edges
        self.own = own
        self.rest = rest
        self.line = line
        self.cut = zones // 2
        self.first_rows = self.cut * own
        self.second_rows = HEAD + (zones - self.cut) * own

        self.relative = own % 8 == 0

    def device(self, square, line):
        core, near, mid = square % 2, square // 2 % 2, square // 4
        if isinstance(line, int):
            slow, rest = line // self.rest, line % self.rest
        else:
            slow, rest = lax.div(line, self.rest), lax.rem(line, self.rest)
        return (((slow * 2 + mid) * self.rest + rest) * 2 + near) * 2 + core


def halves_of(counts):
    high = jnp.floor(counts * (1.0 / COUNT_BASE))
    return high, counts - high * COUNT_BASE


def head_rows(high, low):
    parts = [high, low]
    if high.shape[0] < HEAD // 2:
        pad = jnp.zeros((HEAD // 2 - high.shape[0], high.shape[1]), F32)
        parts = [high, pad, low, pad]
    return jnp.concatenate(parts, axis=0).astype(BF16)


def one_hot(edges_ref, weight_ref, edges, lanes):
    ids = edges_ref[...]
    rows = ids.shape[1]
    columns = lax.broadcasted_iota(jnp.int32, (edges, rows), 0)
    member = columns == ids[0:1, :]
    for j in range(1, ids.shape[0]):
        member = jnp.logical_or(member, columns == ids[j : j + 1, :])
    upright = jnp.transpose(jnp.broadcast_to(weight_ref[...], (lanes, edges)))
    upright = jnp.concatenate([upright] * (rows // lanes), axis=1)
    root = lax.rsqrt(jnp.sum(jnp.where(member, upright, 0.0), axis=0, keepdims=True))
    rounded = root.astype(BF16).astype(F32)
    weighted = jnp.where(member, rounded, 0.0).astype(BF16)
    hot = jnp.where(member, 1.0, 0.0).astype(BF16)
    return root, weighted, jnp.dot(hot, jnp.ones((rows, lanes), BF16), preferred_element_type=F32)


def accumulate(weighted, cells_ref, begin, zones, pitch, total_ref, wide_ref):
    rows, _, lanes = cells_ref.shape
    part = 32

    def widen(i, carry):
        first = i * part
        piece = cells_ref[pl.ds(first, part), begin : begin + zones, :].astype(F32)
        for j in range(part):
            wide_ref[pl.ds(pl.multiple_of((first + j) * pitch, 8), zones), :] = piece[j]
        return carry

    lax.fori_loop(0, rows // part, widen, 0)
    for pair in range(zones // 2):
        left = wide_ref[pl.ds(2 * pair, rows, stride=pitch), :].astype(BF16)
        right = wide_ref[pl.ds(2 * pair + 1, rows, stride=pitch), :].astype(BF16)
        both = jnp.concatenate([left, right], axis=1)
        total_ref[pair] += jnp.dot(weighted, both, preferred_element_type=F32)


def columns_of(total_ref, at, zones, lanes):
    data = []
    for d in range(zones):
        data.append(total_ref[d // 2, at, (d % 2) * lanes : (d % 2 + 1) * lanes])
    return jnp.concatenate(data, axis=0).astype(BF16)


def rows_for(plan, square, shift, line_ref):
    own = plan.own
    if plan.relative:
        device = plan.device(square, lax.rem(line_ref[0] + shift, plan.line))
        return pl.ds(pl.multiple_of(device * own, own), own)
    device = plan.device(square, shift)
    return slice(device * own, (device + 1) * own)


def second_kernel(plan, begin, zones, pitch, line_ref, edges_ref, weight_ref, cells_ref, *refs):
    out_refs = refs[: plan.line]
    root_ref, weighted_ref, total_ref, count_ref, wide_ref = refs[plan.line :]
    lanes = cells_ref.shape[2]

    @pl.when(pl.program_id(0) == 0)
    def _():
        total_ref[...] = jnp.zeros_like(total_ref)
        count_ref[...] = jnp.zeros_like(count_ref)

    root, weighted, counts = one_hot(edges_ref, weight_ref, total_ref.shape[1], lanes)
    root_ref[...] = root
    weighted_ref[...] = weighted
    count_ref[...] += counts
    accumulate(weighted, cells_ref, begin, zones, pitch, total_ref, wide_ref)

    @pl.when(pl.program_id(0) == pl.num_programs(0) - 1)
    def _():
        for square in range(8):
            for shift in range(plan.line):
                at = rows_for(plan, square, shift, line_ref)
                out_refs[shift][square, HEAD:, :] = columns_of(total_ref, at, zones, lanes)
                out_refs[shift][square, 0:HEAD, :] = head_rows(*halves_of(count_ref[at, :]))


def first_kernel(plan, begin, zones, pitch, line_ref, weighted_ref, cells_ref, out_ref, total_ref, wide_ref):
    @pl.when(pl.program_id(0) == 0)
    def _():
        total_ref[...] = jnp.zeros_like(total_ref)

    accumulate(weighted_ref[...], cells_ref, begin, zones, pitch, total_ref, wide_ref)

    @pl.when(pl.program_id(0) == pl.num_programs(0) - 1)
    def _():
        for square in range(8):
            for shift in range(plan.line):
                at = rows_for(plan, square, shift, line_ref)
                out_ref[square, shift] = columns_of(total_ref, at, zones, cells_ref.shape[2])


def fixed(shape):
    return pl.BlockSpec(shape, lambda i: (0,) * len(shape))


def half_sums(kernel, plan, part, line, cells, operands, specs, outs, out_specs, counted):
    anchors, zones, lanes = cells.shape
    edges = plan.edges
    half = zones // 2
    rows = min(512, anchors)
    pitch = -(-half // 8) * 8 + 8
    if half % 16 == 0:
        block, begin = pl.BlockSpec((rows, half, lanes), lambda i: (i, part, 0)), 0
    else:
        block, begin = pl.BlockSpec((rows, zones, lanes), lambda i: (i, 0, 0)), part * half
    counts = [pltpu.VMEM((edges, lanes), F32)] if counted else []
    return pl.pallas_call(
        functools.partial(kernel, plan, begin, half, pitch),
        grid=(anchors // rows,),
        in_specs=[pl.BlockSpec(memory_space=pltpu.SMEM)] + specs + [block],
        out_specs=out_specs,
        out_shape=outs,
        scratch_shapes=[pltpu.VMEM((half // 2, edges, 2 * lanes), F32)] + counts + [pltpu.VMEM((rows * pitch, lanes), F32)],
        compiler_params=pltpu.CompilerParams(vmem_limit_bytes=40 * 1024 * 1024),
        cost_estimate=pl.CostEstimate(
            flops=4 * anchors * edges * zones * lanes, bytes_accessed=2 * anchors * zones * lanes, transcendentals=0
        ),
    )(line[None], *operands, cells)


def second_sums(line, cells, edges_t, edge_weight, plan):
    anchors, _, lanes = cells.shape
    rows = min(512, anchors)
    edges = plan.edges
    shape = (8, plan.second_rows, lanes)
    outs = [jax.ShapeDtypeStruct(shape, BF16)] * plan.line
    outs += [jax.ShapeDtypeStruct((1, anchors), F32), jax.ShapeDtypeStruct((edges, anchors), BF16)]
    out_specs = [fixed(shape)] * plan.line
    out_specs += [pl.BlockSpec((1, rows), lambda i: (0, i)), pl.BlockSpec((edges, rows), lambda i: (0, i))]
    specs = [pl.BlockSpec((edges_t.shape[0], rows), lambda i: (0, i)), fixed((1, edges))]
    operands = (edges_t, edge_weight[None, :])
    *seconds, roots, weighted = half_sums(second_kernel, plan, 1, line, cells, operands, specs, outs, out_specs, True)
    if not plan.relative:
        seconds = jnp.stack(seconds * 2)
        seconds = [lax.dynamic_index_in_dim(seconds, line + k, 0, keepdims=False) for k in range(plan.line)]
    return seconds, roots, weighted


def first_sums(line, cells, weighted, plan):
    rows = min(512, cells.shape[0])
    shape = (8, plan.line, plan.first_rows, cells.shape[2])
    specs = [pl.BlockSpec((plan.edges, rows), lambda i: (0, i))]
    out = jax.ShapeDtypeStruct(shape, BF16)
    first = half_sums(first_kernel, plan, 0, line, cells, (weighted,), specs, out, fixed(shape), False)
    if not plan.relative:
        first = lax.dynamic_slice_in_dim(jnp.concatenate([first, first], axis=1), line, plan.line, 1)
    return first


def add_up(pieces):
    total = pieces[0].astype(F32)
    for piece in pieces[1:]:
        total = total + piece.astype(F32)
    return total


def fold_first_kernel(plan, part_ref, *outs):
    for shift in range(plan.line):
        for quarter in range(4):
            outs[shift][quarter] = add_up([part_ref[quarter, shift], part_ref[4 + quarter, shift]]).astype(BF16)


def fold_second_kernel(plan, *refs):
    parts, out_ref = refs[: plan.line], refs[plan.line]
    for square in range(8):
        for rest in range(plan.rest):
            total = add_up([parts[shift][square] for shift in range(rest, plan.line, plan.rest)])
            half = HEAD // 2
            out_ref[square, rest, 0:HEAD, :] = head_rows(*halves_of(total[0:half] * COUNT_BASE + total[half:HEAD]))
            out_ref[square, rest, HEAD:, :] = total[HEAD:].astype(BF16)


def fold(kernel, plan, parts, shapes):
    whole = pl.BlockSpec(memory_space=pltpu.VMEM)
    size = sum(part.size for part in parts)
    return pl.pallas_call(
        functools.partial(kernel, plan),
        in_specs=[whole] * len(parts),
        out_specs=[whole] * len(shapes),
        out_shape=[jax.ShapeDtypeStruct(shape, BF16) for shape in shapes],
        compiler_params=pltpu.CompilerParams(vmem_limit_bytes=16 * 1024 * 1024),
        cost_estimate=pl.CostEstimate(flops=size, bytes_accessed=size * 4, transcendentals=0),
    )(*parts)


def org_sums(line, cells, edges_t, edge_weight, plan):
    lanes = cells.shape[-1]
    seconds, roots, weighted = second_sums(line, cells, edges_t, edge_weight, plan)
    seconds = [shifted(part, shift) if shift else part for shift, part in enumerate(seconds)]
    first = first_sums(line, cells, weighted, plan)
    first, seconds[1] = lax.optimization_barrier((first, seconds[1]))
    first = lax.all_to_all(first, SQUARE, split_axis=0, concat_axis=0, tiled=True)
    firsts = fold(fold_first_kernel, plan, [first], [(4, plan.first_rows, lanes)] * plan.line)
    firsts = [shifted(part, shift) if shift else part for shift, part in enumerate(firsts)]
    *firsts[1:3], seconds[2] = lax.optimization_barrier((*firsts[1:3], seconds[2]))
    second = fold(fold_second_kernel, plan, seconds, [(8, plan.rest, plan.second_rows, lanes)])[0]
    second = lax.all_to_all(second, SQUARE, split_axis=0, concat_axis=0, tiled=True)
    return firsts, second, roots


def table_kernel(plan, weight_ref, mixing_ref, matrix_ref, *refs):
    firsts = refs[: plan.line]
    second_ref, keep_ref, give_ref, mixed_ref = refs[plan.line :]
    own = plan.own
    lanes = mixing_ref.shape[0]
    half = HEAD // 2
    head = add_up([second_ref[0, 0, 0:HEAD, :], second_ref[4, 0, 0:HEAD, :]])
    counts = head[0:half] * COUNT_BASE + head[half:HEAD]
    scale = weight_ref[...] / counts[0:own]
    rows = plan.first_rows + plan.second_rows - HEAD
    zones = rows // own
    n_dst = 4 * plan.rest
    for k in range(n_dst):
        rest, quarter = k // 4, k % 4
        first = add_up([firsts[shift][quarter] for shift in range(rest, plan.line, plan.rest)])
        second = add_up([second_ref[quarter, rest, HEAD:, :], second_ref[4 + quarter, rest, HEAD:, :]])
        start = k * rows
        for total in (first, second):
            size = total.shape[0]
            totals = (total * jnp.concatenate([scale] * (size // own), axis=0)).astype(BF16)
            mixed = jnp.dot(totals, mixing_ref[...], preferred_element_type=F32)
            mixed_ref[start : start + size, :] = mixed
            start += size
    whole = n_dst * zones
    for e in range(own):
        mixed = mixed_ref[pl.ds(e, whole, stride=own), :] if own > 1 else mixed_ref[...]
        high = mixed.astype(BF16)
        low = (mixed - high.astype(F32)).astype(BF16)
        both = jnp.dot(matrix_ref[...], jnp.concatenate([high, low], axis=1), preferred_element_type=F32)
        result = (both[:, 0:lanes] + both[:, lanes : 2 * lanes]).astype(BF16)
        keep_ref[e] = result[0 : whole // 2]
        give_ref[e] = result[whole // 2 :]


def table_rows(firsts, second, weight_rows, mixing, matrix, plan):
    zones = matrix.shape[0]
    lanes = mixing.shape[0]
    whole = pl.BlockSpec(memory_space=pltpu.VMEM)
    half = jax.ShapeDtypeStruct((plan.own, zones // 2, lanes), BF16)
    return pl.pallas_call(
        functools.partial(table_kernel, plan),
        in_specs=[whole] * (4 + len(firsts)),
        out_specs=[whole] * 2,
        out_shape=[half, half],
        scratch_shapes=[pltpu.VMEM((zones * plan.own, lanes), F32)],
        compiler_params=pltpu.CompilerParams(vmem_limit_bytes=32 * 1024 * 1024),
        cost_estimate=pl.CostEstimate(
            flops=8 * plan.own * zones * lanes * lanes, bytes_accessed=4 * zones * plan.own * lanes, transcendentals=0
        ),
    )(weight_rows, mixing, matrix, *firsts, second)


def spread_kernel(sides, n_pieces, stride, offset, halves_ref, places_ref, root_ref, bias_ref, *refs):
    pieces = refs[: len(refs) - 4 - sides]
    tables = refs[len(refs) - 3 - sides : len(refs) - 3]
    out_ref = refs[len(refs) - 4 - sides]
    ring_ref, sems, ring_sems = refs[-3:]
    slots, _, rows, zones, lanes = ring_ref.shape
    steps = out_ref.shape[0] // rows

    copies = []
    for side in range(sides):
        for i, source in enumerate(pieces[side * n_pieces :][:n_pieces]):
            size = source.shape[0]
            place = tables[side].at[pl.ds(i * size, size)]
            copies.append(pltpu.make_async_copy(source, place, sems.at[len(copies)]))
    for copy in copies:
        copy.start()
    for copy in copies:
        copy.wait()

    bias = bias_ref[...]
    count = places_ref.shape[0]
    tile = 16
    batch = min(8, rows)
    tiles = zones // tile

    def leaving(step, slot, side):
        first_zone = pl.multiple_of(halves_ref[side] * stride + offset, 16)
        place = out_ref.at[pl.ds(step * rows, rows), pl.ds(first_zone, zones), :]
        return pltpu.make_async_copy(ring_ref.at[slot, side], place, ring_sems.at[slot, side])

    def one_step(step, carry):
        slot = lax.rem(step, slots)

        @pl.when(step >= slots)
        def _():
            for side in range(sides):
                leaving(step - slots, slot, side).wait()

        def several(group, inner):
            values = []
            for i in range(batch):
                at = step * rows + group * batch + i
                scale = root_ref[0, at]
                spots = [places_ref[j, at] for j in range(count)]
                for side in range(sides):
                    for first in range(0, zones, tile):
                        parts = [tables[side][spot, first : first + tile, :] for spot in spots]
                        parts = [(a + b).astype(F32) for a, b in zip(parts[0::2], parts[1::2])]
                        total = sum(parts[1:], parts[0])
                        values.append(jnp.maximum((total * scale + bias).astype(BF16), BF16(0.0)))
            for n, value in enumerate(values):
                i, side, start = n // (sides * tiles), n // tiles % sides, n % tiles * tile
                ring_ref[slot, side, group * batch + i, start : start + tile, :] = value
            return inner

        lax.fori_loop(0, rows // batch, several, 0)
        for side in range(sides):
            leaving(step, slot, side).start()
        return carry

    lax.fori_loop(0, steps, one_step, 0)
    for step in range(steps - slots, steps):
        for side in range(sides):
            leaving(step, step % slots, side).wait()


def spread(halves, places, root, bias, pieces, offset, stride, before=None):
    sides = len(pieces)
    anchors = places.shape[1]
    lanes = bias.shape[1]
    count, zones = len(pieces[0]), pieces[0][0].shape[1]
    edges = count * pieces[0][0].shape[0]
    rows = min(16, anchors // 8)
    slots = min(8, anchors // rows)
    smem = pl.BlockSpec(memory_space=pltpu.SMEM)
    anywhere = pl.BlockSpec(memory_space=pltpu.HBM)
    operands = [halves, places, root, bias] + [piece for side in pieces for piece in side]
    specs = [smem, smem, smem, pl.BlockSpec(memory_space=pltpu.VMEM)] + [anywhere] * (sides * count)
    aliases = {}
    if before is not None:
        aliases = {len(operands): 0}
        operands.append(before)
        specs.append(anywhere)
    return pl.pallas_call(
        functools.partial(spread_kernel, sides, count, stride, offset),
        in_specs=specs,
        out_specs=anywhere,
        out_shape=jax.ShapeDtypeStruct((anchors, 2 * stride, lanes), BF16),
        scratch_shapes=[pltpu.VMEM((edges, zones, lanes), BF16)] * sides
        + [
            pltpu.VMEM((slots, sides, rows, zones, lanes), BF16),
            pltpu.SemaphoreType.DMA((sides * count,)),
            pltpu.SemaphoreType.DMA((slots, sides)),
        ],
        input_output_aliases=aliases,
        compiler_params=pltpu.CompilerParams(vmem_limit_bytes=24 * 1024 * 1024),
        cost_estimate=pl.CostEstimate(
            flops=4096 * anchors * zones * lanes, bytes_accessed=4 * anchors * zones * lanes, transcendentals=0
        ),
    )(*operands)


LINE = ("slow", "rest")
SQUARE = ("mid", "near", "core")


def shifted(x, amount):
    size = lax.axis_size(LINE)
    return lax.ppermute(x, LINE, [(i, (i + amount) % size) for i in range(size)])


def crossed(x, turn):
    pairs = []
    for device in range(8):
        core = device % 2
        pairs.append((device, device ^ (2 if core == turn else 4)))
    return lax.ppermute(x, SQUARE, pairs)


def masked(x, mask):
    return lax.ppermute(x, SQUARE, [(device, device ^ mask) for device in range(8)])


def swapped(x):
    return lax.ppermute(x, "core", [(0, 1), (1, 0)])


def gather_table(keep, give, core):
    size = lax.axis_size(LINE)
    got = swapped(give)
    block = jnp.concatenate([jnp.where(core == 0, keep, got), jnp.where(core == 0, got, keep)], axis=0)
    split = block.shape[1] * 3 // 4
    long, short = block[:, :split], block[:, split:]
    line = [long] + [shifted(long, k) for k in range(1, size)]
    short = jnp.concatenate([short, masked(short, 2), masked(short, 4), masked(short, 6)], axis=0)
    long = jnp.concatenate(line, axis=0)
    short, long = lax.optimization_barrier((short, long))
    first = crossed(long, 0)
    second = crossed(long, 1)
    shorts = [short] + [shifted(short, k) for k in range(1, size)]
    first, shorts[1] = lax.optimization_barrier((first, shorts[1]))
    return [long, first, second, crossed(first, 1)], shorts


def places_of(ids, core, own):
    rest, size = lax.axis_size("rest"), lax.axis_size(LINE)
    owner = ids // own
    slot = owner % 2 * own + ids % own
    near = jnp.bitwise_xor(owner // 2 % 2, lax.axis_index("near"))
    mid = jnp.bitwise_xor(owner // (4 * rest) % 2, lax.axis_index("mid"))
    line = owner // (8 * rest) * rest + owner // 4 % rest
    line = lax.rem(lax.axis_index(LINE) - line + size, size)
    square = jnp.where(core == 0, 2 * mid + near, 2 * near + mid)
    short = (line * 4 + 2 * mid + near) * (2 * own) + slot
    return (square * size + line) * (2 * own) + slot, short


def relative_columns(matrix):
    zones, rest = matrix.shape[0], lax.axis_size("rest")
    if rest == 1:
        return matrix
    back = jnp.flip(matrix.reshape(zones, rest, -1), 1)
    back = jnp.concatenate([back, back], axis=1)
    return lax.dynamic_slice_in_dim(back, rest - 1 - lax.axis_index("rest"), rest, 1).reshape(zones, zones)


def shards(od_cells, anchor_edges, edge_weight, mixing, dst_edges, dst_weight, out_bias):
    n_org = lax.axis_size("slow") * lax.axis_size("mid")
    n_dst = lax.axis_size("rest") * lax.axis_size("near") * lax.axis_size("core")
    own = edge_weight.shape[0] // (n_org * n_dst)
    everyone = ("slow", "mid", "rest", "near", "core")
    core = lax.axis_index("core")
    edges_t = anchor_edges.T
    plan = Plan(od_cells.shape[1], edge_weight.shape[0], own, lax.axis_size("rest"), lax.axis_size(LINE))
    firsts, second, roots = org_sums(lax.axis_index(LINE), od_cells, edges_t, edge_weight, plan)
    own_weight = lax.dynamic_slice_in_dim(edge_weight, lax.axis_index(everyone) * own, own, 0)
    weight_rows = jnp.broadcast_to(own_weight[:, None], (own, mixing.shape[0]))
    matrix = relative_columns(dest_operator(dst_edges, dst_weight))
    half = matrix.shape[0] // 2
    matrix = jnp.where(core == 0, matrix, jnp.concatenate([matrix[half:], matrix[:half]], axis=0))
    keep, give = table_rows(firsts, second, weight_rows, mixing, matrix, plan)
    longs, shorts = gather_table(keep, give, core)
    rows = anchor_edges.shape[0] // n_dst
    start = lax.axis_index(("rest", "near", "core")) * rows
    ids = lax.dynamic_slice_in_dim(edges_t, start, rows, 1)
    own_root = lax.dynamic_slice_in_dim(roots, start, rows, 1)
    bias = out_bias[None, :]
    other = 1 - core
    long_places, short_places = places_of(ids, core, own)
    far_long_places, _ = places_of(ids, other, own)
    split = longs[0].shape[1]
    far = [swapped(x) for x in shorts]
    result = spread(jnp.stack([core, other]), short_places, own_root, bias, [shorts, far], split, half)
    result = spread(core[None], long_places, own_root, bias, [longs], 0, half, result)
    far = [swapped(x) for x in longs]
    return spread(other[None], far_long_places, own_root, bias, [far], 0, half, result)


def solution(mesh):
    n_org, n_dst = mesh.devices.shape
    fine = Mesh(mesh.devices.reshape(n_org // 2, 2, n_dst // 4, 2, 2), ("slow", "mid", "rest", "near", "core"))
    org, dst = ("slow", "mid"), ("rest", "near", "core")
    in_specs = (P(org, dst, None), P(org, None), P(), P(), P(), P(), P())
    out_specs = P(org + dst, None, None)
    return jax.shard_map(shards, mesh=fine, in_specs=in_specs, out_specs=out_specs, check_vma=False)
```

```python
import functools

import jax
import jax.numpy as jnp
from jax import lax
from jax.experimental import pallas as pl
from jax.experimental.pallas import tpu as pltpu
from jax.sharding import Mesh, PartitionSpec as P

BF16 = jnp.bfloat16
F32 = jnp.float32
COUNT_BASE = 256.0
HEAD = 16


def corridor_table(edge_ids, edge_count):
    columns = jnp.arange(edge_count, dtype=jnp.int32)
    return jnp.sum((edge_ids[:, :, None] == columns[None, None, :]).astype(F32), axis=1)


def dest_operator(dst_edges, dst_weight):
    dst_member = corridor_table(dst_edges, dst_weight.shape[0])
    dst_degree = jnp.sum(dst_member * dst_weight[None, :], axis=1)
    edge_sizes = jnp.sum(dst_member, axis=0)
    left_factor = dst_member * lax.rsqrt(dst_degree)[:, None]
    right_factor = left_factor * (dst_weight / edge_sizes)[None, :]
    result = jnp.dot(right_factor, left_factor.T, precision=lax.Precision.HIGHEST)
    return result.astype(BF16)


class Plan:
    def __init__(self, zones, edges, own, rest, line):
        self.edges = edges
        self.own = own
        self.rest = rest
        self.line = line
        self.cut = zones // 2
        self.first_rows = self.cut * own
        self.second_rows = HEAD + (zones - self.cut) * own

        self.relative = own % 8 == 0

    def device(self, square, line):
        core, near, mid = square % 2, square // 2 % 2, square // 4
        if isinstance(line, int):
            slow, rest = line // self.rest, line % self.rest
        else:
            slow, rest = lax.div(line, self.rest), lax.rem(line, self.rest)
        return (((slow * 2 + mid) * self.rest + rest) * 2 + near) * 2 + core


def halves_of(counts):
    high = jnp.floor(counts * (1.0 / COUNT_BASE))
    return high, counts - high * COUNT_BASE


def head_rows(high, low):
    parts = [high, low]
    if high.shape[0] < HEAD // 2:
        pad = jnp.zeros((HEAD // 2 - high.shape[0], high.shape[1]), F32)
        parts = [high, pad, low, pad]
    return jnp.concatenate(parts, axis=0).astype(BF16)


def one_hot(edges_ref, weight_ref, edges, lanes):
    ids = edges_ref[...]
    rows = ids.shape[1]
    columns = lax.broadcasted_iota(jnp.int32, (edges, rows), 0)
    member = columns == ids[0:1, :]
    for j in range(1, ids.shape[0]):
        member = jnp.logical_or(member, columns == ids[j : j + 1, :])
    upright = jnp.transpose(jnp.broadcast_to(weight_ref[...], (lanes, edges)))
    upright = jnp.concatenate([upright] * (rows // lanes), axis=1)
    root = lax.rsqrt(jnp.sum(jnp.where(member, upright, 0.0), axis=0, keepdims=True))
    rounded = root.astype(BF16).astype(F32)
    weighted = jnp.where(member, rounded, 0.0).astype(BF16)
    hot = jnp.where(member, 1.0, 0.0).astype(BF16)
    return root, weighted, jnp.dot(hot, jnp.ones((rows, lanes), BF16), preferred_element_type=F32)


def accumulate(weighted, cells_ref, begin, zones, pitch, total_ref, wide_ref):
    rows, _, lanes = cells_ref.shape
    part = 32

    def widen(i, carry):
        first = i * part
        piece = cells_ref[pl.ds(first, part), begin : begin + zones, :].astype(F32)
        for j in range(part):
            wide_ref[pl.ds(pl.multiple_of((first + j) * pitch, 8), zones), :] = piece[j]
        return carry

    lax.fori_loop(0, rows // part, widen, 0, unroll=4)
    for pair in range(zones // 2):
        left = wide_ref[pl.ds(2 * pair, rows, stride=pitch), :].astype(BF16)
        right = wide_ref[pl.ds(2 * pair + 1, rows, stride=pitch), :].astype(BF16)
        both = jnp.concatenate([left, right], axis=1)
        total_ref[pair] += jnp.dot(weighted, both, preferred_element_type=F32)


def columns_of(total_ref, at, zones, lanes):
    data = []
    for d in range(zones):
        data.append(total_ref[d // 2, at, (d % 2) * lanes : (d % 2 + 1) * lanes])
    return jnp.concatenate(data, axis=0).astype(BF16)


def rows_for(plan, square, shift, line_ref):
    own = plan.own
    if plan.relative:
        device = plan.device(square, lax.rem(line_ref[0] + shift, plan.line))
        return pl.ds(pl.multiple_of(device * own, own), own)
    device = plan.device(square, shift)
    return slice(device * own, (device + 1) * own)


def second_kernel(plan, begin, zones, pitch, line_ref, edges_ref, weight_ref, cells_ref, *refs):
    out_refs = refs[: plan.line]
    root_ref, weighted_ref, total_ref, count_ref, wide_ref = refs[plan.line :]
    lanes = cells_ref.shape[2]

    @pl.when(pl.program_id(0) == 0)
    def _():
        total_ref[...] = jnp.zeros_like(total_ref)
        count_ref[...] = jnp.zeros_like(count_ref)

    root, weighted, counts = one_hot(edges_ref, weight_ref, total_ref.shape[1], lanes)
    root_ref[...] = root
    weighted_ref[...] = weighted
    count_ref[...] += counts
    accumulate(weighted, cells_ref, begin, zones, pitch, total_ref, wide_ref)

    @pl.when(pl.program_id(0) == pl.num_programs(0) - 1)
    def _():
        for square in range(8):
            for shift in range(plan.line):
                at = rows_for(plan, square, shift, line_ref)
                out_refs[shift][square, HEAD:, :] = columns_of(total_ref, at, zones, lanes)
                out_refs[shift][square, 0:HEAD, :] = head_rows(*halves_of(count_ref[at, :]))


def first_kernel(plan, begin, zones, pitch, line_ref, weighted_ref, cells_ref, out_ref, total_ref, wide_ref):
    @pl.when(pl.program_id(0) == 0)
    def _():
        total_ref[...] = jnp.zeros_like(total_ref)

    accumulate(weighted_ref[...], cells_ref, begin, zones, pitch, total_ref, wide_ref)

    @pl.when(pl.program_id(0) == pl.num_programs(0) - 1)
    def _():
        for square in range(8):
            for shift in range(plan.line):
                at = rows_for(plan, square, shift, line_ref)
                out_ref[square, shift] = columns_of(total_ref, at, zones, cells_ref.shape[2])


def fixed(shape):
    return pl.BlockSpec(shape, lambda i: (0,) * len(shape))


def half_sums(kernel, plan, part, line, cells, operands, specs, outs, out_specs, counted):
    anchors, zones, lanes = cells.shape
    edges = plan.edges
    half = zones // 2
    rows = min(512, anchors)
    pitch = -(-half // 8) * 8 + 8
    if half % 16 == 0:
        block, begin = pl.BlockSpec((rows, half, lanes), lambda i: (i, part, 0)), 0
    else:
        block, begin = pl.BlockSpec((rows, zones, lanes), lambda i: (i, 0, 0)), part * half
    counts = [pltpu.VMEM((edges, lanes), F32)] if counted else []
    return pl.pallas_call(
        functools.partial(kernel, plan, begin, half, pitch),
        grid=(anchors // rows,),
        in_specs=[pl.BlockSpec(memory_space=pltpu.SMEM)] + specs + [block],
        out_specs=out_specs,
        out_shape=outs,
        scratch_shapes=[pltpu.VMEM((half // 2, edges, 2 * lanes), F32)] + counts + [pltpu.VMEM((rows * pitch, lanes), F32)],
        compiler_params=pltpu.CompilerParams(vmem_limit_bytes=40 * 1024 * 1024),
        cost_estimate=pl.CostEstimate(
            flops=4 * anchors * edges * zones * lanes, bytes_accessed=2 * anchors * zones * lanes, transcendentals=0
        ),
    )(line[None], *operands, cells)


def second_sums(line, cells, edges_t, edge_weight, plan):
    anchors, _, lanes = cells.shape
    rows = min(512, anchors)
    edges = plan.edges
    shape = (8, plan.second_rows, lanes)
    outs = [jax.ShapeDtypeStruct(shape, BF16)] * plan.line
    outs += [jax.ShapeDtypeStruct((1, anchors), F32), jax.ShapeDtypeStruct((edges, anchors), BF16)]
    out_specs = [fixed(shape)] * plan.line
    out_specs += [pl.BlockSpec((1, rows), lambda i: (0, i)), pl.BlockSpec((edges, rows), lambda i: (0, i))]
    specs = [pl.BlockSpec((edges_t.shape[0], rows), lambda i: (0, i)), fixed((1, edges))]
    operands = (edges_t, edge_weight[None, :])
    *seconds, roots, weighted = half_sums(second_kernel, plan, 1, line, cells, operands, specs, outs, out_specs, True)
    if not plan.relative:
        seconds = jnp.stack(seconds * 2)
        seconds = [lax.dynamic_index_in_dim(seconds, line + k, 0, keepdims=False) for k in range(plan.line)]
    return seconds, roots, weighted


def first_sums(line, cells, weighted, plan):
    rows = min(512, cells.shape[0])
    shape = (8, plan.line, plan.first_rows, cells.shape[2])
    specs = [pl.BlockSpec((plan.edges, rows), lambda i: (0, i))]
    out = jax.ShapeDtypeStruct(shape, BF16)
    first = half_sums(first_kernel, plan, 0, line, cells, (weighted,), specs, out, fixed(shape), False)
    if not plan.relative:
        first = lax.dynamic_slice_in_dim(jnp.concatenate([first, first], axis=1), line, plan.line, 1)
    return first


def add_up(pieces):
    total = pieces[0].astype(F32)
    for piece in pieces[1:]:
        total = total + piece.astype(F32)
    return total


def fold_first_kernel(plan, part_ref, *outs):
    for shift in range(plan.line):
        for quarter in range(4):
            outs[shift][quarter] = add_up([part_ref[quarter, shift], part_ref[4 + quarter, shift]]).astype(BF16)


def fold_second_kernel(plan, *refs):
    parts, out_ref = refs[: plan.line], refs[plan.line]
    for square in range(8):
        for rest in range(plan.rest):
            total = add_up([parts[shift][square] for shift in range(rest, plan.line, plan.rest)])
            half = HEAD // 2
            out_ref[square, rest, 0:HEAD, :] = head_rows(*halves_of(total[0:half] * COUNT_BASE + total[half:HEAD]))
            out_ref[square, rest, HEAD:, :] = total[HEAD:].astype(BF16)


def fold(kernel, plan, parts, shapes):
    whole = pl.BlockSpec(memory_space=pltpu.VMEM)
    size = sum(part.size for part in parts)
    return pl.pallas_call(
        functools.partial(kernel, plan),
        in_specs=[whole] * len(parts),
        out_specs=[whole] * len(shapes),
        out_shape=[jax.ShapeDtypeStruct(shape, BF16) for shape in shapes],
        compiler_params=pltpu.CompilerParams(vmem_limit_bytes=16 * 1024 * 1024),
        cost_estimate=pl.CostEstimate(flops=size, bytes_accessed=size * 4, transcendentals=0),
    )(*parts)


def org_sums(line, cells, edges_t, edge_weight, plan):
    lanes = cells.shape[-1]
    seconds, roots, weighted = second_sums(line, cells, edges_t, edge_weight, plan)
    seconds = [shifted(part, shift) if shift else part for shift, part in enumerate(seconds)]
    first = first_sums(line, cells, weighted, plan)
    first, seconds[1] = lax.optimization_barrier((first, seconds[1]))
    first = lax.all_to_all(first, SQUARE, split_axis=0, concat_axis=0, tiled=True)
    firsts = fold(fold_first_kernel, plan, [first], [(4, plan.first_rows, lanes)] * plan.line)
    firsts = [shifted(part, shift) if shift else part for shift, part in enumerate(firsts)]
    *firsts[1:3], seconds[2] = lax.optimization_barrier((*firsts[1:3], seconds[2]))
    second = fold(fold_second_kernel, plan, seconds, [(8, plan.rest, plan.second_rows, lanes)])[0]
    second = lax.all_to_all(second, SQUARE, split_axis=0, concat_axis=0, tiled=True)
    return firsts, second, roots


def table_kernel(plan, weight_ref, mixing_ref, matrix_ref, *refs):
    firsts = refs[: plan.line]
    second_ref, keep_ref, give_ref, mixed_ref = refs[plan.line :]
    own = plan.own
    lanes = mixing_ref.shape[0]
    half = HEAD // 2
    head = add_up([second_ref[0, 0, 0:HEAD, :], second_ref[4, 0, 0:HEAD, :]])
    counts = head[0:half] * COUNT_BASE + head[half:HEAD]
    scale = weight_ref[...] / counts[0:own]
    rows = plan.first_rows + plan.second_rows - HEAD
    zones = rows // own
    n_dst = 4 * plan.rest
    for k in range(n_dst):
        rest, quarter = k // 4, k % 4
        first = add_up([firsts[shift][quarter] for shift in range(rest, plan.line, plan.rest)])
        second = add_up([second_ref[quarter, rest, HEAD:, :], second_ref[4 + quarter, rest, HEAD:, :]])
        start = k * rows
        for total in (first, second):
            size = total.shape[0]
            totals = (total * jnp.concatenate([scale] * (size // own), axis=0)).astype(BF16)
            mixed = jnp.dot(totals, mixing_ref[...], preferred_element_type=F32)
            mixed_ref[start : start + size, :] = mixed
            start += size
    whole = n_dst * zones
    for e in range(own):
        mixed = mixed_ref[pl.ds(e, whole, stride=own), :] if own > 1 else mixed_ref[...]
        high = mixed.astype(BF16)
        low = (mixed - high.astype(F32)).astype(BF16)
        both = jnp.dot(matrix_ref[...], jnp.concatenate([high, low], axis=1), preferred_element_type=F32)
        result = (both[:, 0:lanes] + both[:, lanes : 2 * lanes]).astype(BF16)
        keep_ref[e] = result[0 : whole // 2]
        give_ref[e] = result[whole // 2 :]


def table_rows(firsts, second, weight_rows, mixing, matrix, plan):
    zones = matrix.shape[0]
    lanes = mixing.shape[0]
    whole = pl.BlockSpec(memory_space=pltpu.VMEM)
    half = jax.ShapeDtypeStruct((plan.own, zones // 2, lanes), BF16)
    return pl.pallas_call(
        functools.partial(table_kernel, plan),
        in_specs=[whole] * (4 + len(firsts)),
        out_specs=[whole] * 2,
        out_shape=[half, half],
        scratch_shapes=[pltpu.VMEM((zones * plan.own, lanes), F32)],
        compiler_params=pltpu.CompilerParams(vmem_limit_bytes=32 * 1024 * 1024),
        cost_estimate=pl.CostEstimate(
            flops=8 * plan.own * zones * lanes * lanes, bytes_accessed=4 * zones * plan.own * lanes, transcendentals=0
        ),
    )(weight_rows, mixing, matrix, *firsts, second)


def spread_kernel(sides, n_pieces, stride, offset, halves_ref, places_ref, root_ref, bias_ref, *refs):
    pieces = refs[: len(refs) - 4 - sides]
    tables = refs[len(refs) - 3 - sides : len(refs) - 3]
    out_ref = refs[len(refs) - 4 - sides]
    ring_ref, sems, ring_sems = refs[-3:]
    slots, _, rows, zones, lanes = ring_ref.shape
    steps = out_ref.shape[0] // rows

    copies = []
    for side in range(sides):
        for i, source in enumerate(pieces[side * n_pieces :][:n_pieces]):
            size = source.shape[0]
            place = tables[side].at[pl.ds(i * size, size)]
            copies.append(pltpu.make_async_copy(source, place, sems.at[len(copies)]))
    for copy in copies:
        copy.start()
    for copy in copies:
        copy.wait()

    bias = bias_ref[...]
    count = places_ref.shape[0]
    tile = 16
    batch = min(8, rows)
    tiles = zones // tile

    def leaving(step, slot, side):
        first_zone = pl.multiple_of(halves_ref[side] * stride + offset, 16)
        place = out_ref.at[pl.ds(step * rows, rows), pl.ds(first_zone, zones), :]
        return pltpu.make_async_copy(ring_ref.at[slot, side], place, ring_sems.at[slot, side])

    def one_step(step, carry):
        slot = lax.rem(step, slots)

        @pl.when(step >= slots)
        def _():
            for side in range(sides):
                leaving(step - slots, slot, side).wait()

        def several(group, inner):
            values = []
            for i in range(batch):
                at = step * rows + group * batch + i
                scale = root_ref[0, at]
                spots = [places_ref[j, at] for j in range(count)]
                for side in range(sides):
                    for first in range(0, zones, tile):
                        parts = [tables[side][spot, first : first + tile, :] for spot in spots]
                        while len(parts) > 1:
                            parts = [sum(parts[n + 1 : n + 2], parts[n]) for n in range(0, len(parts), 2)]
                        total = parts[0].astype(F32)
                        values.append(jnp.maximum((total * scale + bias).astype(BF16), BF16(0.0)))
            for n, value in enumerate(values):
                i, side, start = n // (sides * tiles), n // tiles % sides, n % tiles * tile
                ring_ref[slot, side, group * batch + i, start : start + tile, :] = value
            return inner

        lax.fori_loop(0, rows // batch, several, 0)
        for side in range(sides):
            leaving(step, slot, side).start()
        return carry

    lax.fori_loop(0, steps, one_step, 0)
    for step in range(steps - slots, steps):
        for side in range(sides):
            leaving(step, step % slots, side).wait()


def spread(halves, places, root, bias, pieces, offset, stride, before=None):
    sides = len(pieces)
    anchors = places.shape[1]
    lanes = bias.shape[1]
    count, zones = len(pieces[0]), pieces[0][0].shape[1]
    edges = count * pieces[0][0].shape[0]
    rows = min(16, anchors // 8)
    slots = min(8, anchors // rows)
    smem = pl.BlockSpec(memory_space=pltpu.SMEM)
    anywhere = pl.BlockSpec(memory_space=pltpu.HBM)
    operands = [halves, places, root, bias] + [piece for side in pieces for piece in side]
    specs = [smem, smem, smem, pl.BlockSpec(memory_space=pltpu.VMEM)] + [anywhere] * (sides * count)
    aliases = {}
    if before is not None:
        aliases = {len(operands): 0}
        operands.append(before)
        specs.append(anywhere)
    return pl.pallas_call(
        functools.partial(spread_kernel, sides, count, stride, offset),
        in_specs=specs,
        out_specs=anywhere,
        out_shape=jax.ShapeDtypeStruct((anchors, 2 * stride, lanes), BF16),
        scratch_shapes=[pltpu.VMEM((edges, zones, lanes), BF16)] * sides
        + [
            pltpu.VMEM((slots, sides, rows, zones, lanes), BF16),
            pltpu.SemaphoreType.DMA((sides * count,)),
            pltpu.SemaphoreType.DMA((slots, sides)),
        ],
        input_output_aliases=aliases,
        compiler_params=pltpu.CompilerParams(vmem_limit_bytes=24 * 1024 * 1024),
        cost_estimate=pl.CostEstimate(
            flops=4096 * anchors * zones * lanes, bytes_accessed=4 * anchors * zones * lanes, transcendentals=0
        ),
    )(*operands)


LINE = ("slow", "rest")
SQUARE = ("mid", "near", "core")


def shifted(x, amount):
    size = lax.axis_size(LINE)
    return lax.ppermute(x, LINE, [(i, (i + amount) % size) for i in range(size)])


def crossed(x, turn):
    pairs = []
    for device in range(8):
        core = device % 2
        pairs.append((device, device ^ (2 if core == turn else 4)))
    return lax.ppermute(x, SQUARE, pairs)


def masked(x, mask):
    return lax.ppermute(x, SQUARE, [(device, device ^ mask) for device in range(8)])


def swapped(x):
    return lax.ppermute(x, "core", [(0, 1), (1, 0)])


def gather_table(keep, give, core):
    size = lax.axis_size(LINE)
    got = swapped(give)
    block = jnp.concatenate([jnp.where(core == 0, keep, got), jnp.where(core == 0, got, keep)], axis=0)
    split = block.shape[1] * 3 // 4
    long, short = block[:, :split], block[:, split:]
    line = [long] + [shifted(long, k) for k in range(1, size)]
    short = jnp.concatenate([short, masked(short, 2), masked(short, 4), masked(short, 6)], axis=0)
    long = jnp.concatenate(line, axis=0)
    short, long = lax.optimization_barrier((short, long))
    first = crossed(long, 0)
    second = crossed(long, 1)
    shorts = [short] + [shifted(short, k) for k in range(1, size)]
    first, shorts[1] = lax.optimization_barrier((first, shorts[1]))
    return [long, first, second, crossed(first, 1)], shorts


def places_of(ids, core, own):
    rest, size = lax.axis_size("rest"), lax.axis_size(LINE)
    owner = ids // own
    slot = owner % 2 * own + ids % own
    near = jnp.bitwise_xor(owner // 2 % 2, lax.axis_index("near"))
    mid = jnp.bitwise_xor(owner // (4 * rest) % 2, lax.axis_index("mid"))
    line = owner // (8 * rest) * rest + owner // 4 % rest
    line = lax.rem(lax.axis_index(LINE) - line + size, size)
    square = jnp.where(core == 0, 2 * mid + near, 2 * near + mid)
    short = (line * 4 + 2 * mid + near) * (2 * own) + slot
    return (square * size + line) * (2 * own) + slot, short


def relative_columns(matrix):
    zones, rest = matrix.shape[0], lax.axis_size("rest")
    if rest == 1:
        return matrix
    back = jnp.flip(matrix.reshape(zones, rest, -1), 1)
    back = jnp.concatenate([back, back], axis=1)
    return lax.dynamic_slice_in_dim(back, rest - 1 - lax.axis_index("rest"), rest, 1).reshape(zones, zones)


def shards(od_cells, anchor_edges, edge_weight, mixing, dst_edges, dst_weight, out_bias):
    n_org = lax.axis_size("slow") * lax.axis_size("mid")
    n_dst = lax.axis_size("rest") * lax.axis_size("near") * lax.axis_size("core")
    own = edge_weight.shape[0] // (n_org * n_dst)
    everyone = ("slow", "mid", "rest", "near", "core")
    core = lax.axis_index("core")
    edges_t = anchor_edges.T
    plan = Plan(od_cells.shape[1], edge_weight.shape[0], own, lax.axis_size("rest"), lax.axis_size(LINE))
    firsts, second, roots = org_sums(lax.axis_index(LINE), od_cells, edges_t, edge_weight, plan)
    own_weight = lax.dynamic_slice_in_dim(edge_weight, lax.axis_index(everyone) * own, own, 0)
    weight_rows = jnp.broadcast_to(own_weight[:, None], (own, mixing.shape[0]))
    matrix = relative_columns(dest_operator(dst_edges, dst_weight))
    half = matrix.shape[0] // 2
    matrix = jnp.where(core == 0, matrix, jnp.concatenate([matrix[half:], matrix[:half]], axis=0))
    keep, give = table_rows(firsts, second, weight_rows, mixing, matrix, plan)
    longs, shorts = gather_table(keep, give, core)
    rows = anchor_edges.shape[0] // n_dst
    start = lax.axis_index(("rest", "near", "core")) * rows
    ids = lax.dynamic_slice_in_dim(edges_t, start, rows, 1)
    own_root = lax.dynamic_slice_in_dim(roots, start, rows, 1)
    bias = out_bias[None, :]
    other = 1 - core
    long_places, short_places = places_of(ids, core, own)
    far_long_places, _ = places_of(ids, other, own)
    split = longs[0].shape[1]
    far = [swapped(x) for x in shorts]
    result = spread(jnp.stack([core, other]), short_places, own_root, bias, [shorts, far], split, half)
    result = spread(core[None], long_places, own_root, bias, [longs], 0, half, result)
    far = [swapped(x) for x in longs]
    return spread(other[None], far_long_places, own_root, bias, [far], 0, half, result)


def solution(mesh):
    n_org, n_dst = mesh.devices.shape
    fine = Mesh(mesh.devices.reshape(n_org // 2, 2, n_dst // 4, 2, 2), ("slow", "mid", "rest", "near", "core"))
    org, dst = ("slow", "mid"), ("rest", "near", "core")
    in_specs = (P(org, dst, None), P(org, None), P(), P(), P(), P(), P())
    out_specs = P(org + dst, None, None)
    return jax.shard_map(shards, mesh=fine, in_specs=in_specs, out_specs=out_specs, check_vma=False)
```

```python
import functools

import jax
import jax.numpy as jnp
from jax import lax
from jax.experimental import pallas as pl
from jax.experimental.pallas import tpu as pltpu
from jax.sharding import Mesh, PartitionSpec as P

BF16 = jnp.bfloat16
F32 = jnp.float32
COUNT_BASE = 256.0
HEAD = 16


def corridor_table(edge_ids, edge_count):
    columns = jnp.arange(edge_count, dtype=jnp.int32)
    return jnp.sum((edge_ids[:, :, None] == columns[None, None, :]).astype(F32), axis=1)


def dest_operator(dst_edges, dst_weight):
    dst_member = corridor_table(dst_edges, dst_weight.shape[0])
    dst_degree = jnp.sum(dst_member * dst_weight[None, :], axis=1)
    edge_sizes = jnp.sum(dst_member, axis=0)
    left_factor = dst_member * lax.rsqrt(dst_degree)[:, None]
    right_factor = left_factor * (dst_weight / edge_sizes)[None, :]
    result = jnp.dot(right_factor, left_factor.T, precision=lax.Precision.HIGHEST)
    return result.astype(BF16)


class Plan:
    def __init__(self, zones, edges, own, rest, line):
        self.edges = edges
        self.own = own
        self.rest = rest
        self.line = line
        self.cut = zones // 2
        self.first_rows = self.cut * own
        self.second_rows = HEAD + (zones - self.cut) * own

        self.relative = own % 8 == 0

    def device(self, square, line):
        core, near, mid = square % 2, square // 2 % 2, square // 4
        if isinstance(line, int):
            slow, rest = line // self.rest, line % self.rest
        else:
            slow, rest = lax.div(line, self.rest), lax.rem(line, self.rest)
        return (((slow * 2 + mid) * self.rest + rest) * 2 + near) * 2 + core


def halves_of(counts):
    high = jnp.floor(counts * (1.0 / COUNT_BASE))
    return high, counts - high * COUNT_BASE


def head_rows(high, low):
    parts = [high, low]
    if high.shape[0] < HEAD // 2:
        pad = jnp.zeros((HEAD // 2 - high.shape[0], high.shape[1]), F32)
        parts = [high, pad, low, pad]
    return jnp.concatenate(parts, axis=0).astype(BF16)


def one_hot(edges_ref, weight_ref, edges, lanes):
    ids = edges_ref[...]
    rows = ids.shape[1]
    columns = lax.broadcasted_iota(jnp.int32, (edges, rows), 0)
    member = columns == ids[0:1, :]
    for j in range(1, ids.shape[0]):
        member = jnp.logical_or(member, columns == ids[j : j + 1, :])
    upright = jnp.transpose(jnp.broadcast_to(weight_ref[...], (lanes, edges)))
    upright = jnp.concatenate([upright] * (rows // lanes), axis=1)
    root = lax.rsqrt(jnp.sum(jnp.where(member, upright, 0.0), axis=0, keepdims=True))
    rounded = root.astype(BF16).astype(F32)
    weighted = jnp.where(member, rounded, 0.0).astype(BF16)
    hot = jnp.where(member, 1.0, 0.0).astype(BF16)
    return root, weighted, jnp.dot(hot, jnp.ones((rows, lanes), BF16), preferred_element_type=F32)


def accumulate(weighted, cells_ref, begin, zones, pitch, total_ref, wide_ref):
    rows, _, lanes = cells_ref.shape
    part = 32

    def widen(i, carry):
        first = i * part
        piece = cells_ref[pl.ds(first, part), begin : begin + zones, :].astype(F32)
        for j in range(part):
            wide_ref[pl.ds(pl.multiple_of((first + j) * pitch, 8), zones), :] = piece[j]
        return carry

    lax.fori_loop(0, rows // part, widen, 0)
    for pair in range(zones // 2):
        left = wide_ref[pl.ds(2 * pair, rows, stride=pitch), :].astype(BF16)
        right = wide_ref[pl.ds(2 * pair + 1, rows, stride=pitch), :].astype(BF16)
        both = jnp.concatenate([left, right], axis=1)
        total_ref[pair] += jnp.dot(weighted, both, preferred_element_type=F32)


def columns_of(total_ref, at, zones, lanes):
    data = []
    for d in range(zones):
        data.append(total_ref[d // 2, at, (d % 2) * lanes : (d % 2 + 1) * lanes])
    return jnp.concatenate(data, axis=0).astype(BF16)


def rows_for(plan, square, shift, line_ref):
    own = plan.own
    if plan.relative:
        device = plan.device(square, lax.rem(line_ref[0] + shift, plan.line))
        return pl.ds(pl.multiple_of(device * own, own), own)
    device = plan.device(square, shift)
    return slice(device * own, (device + 1) * own)


def second_kernel(plan, begin, zones, pitch, line_ref, edges_ref, weight_ref, cells_ref, *refs):
    out_refs = refs[: plan.line]
    root_ref, weighted_ref, total_ref, count_ref, wide_ref = refs[plan.line :]
    lanes = cells_ref.shape[2]

    @pl.when(pl.program_id(0) == 0)
    def _():
        total_ref[...] = jnp.zeros_like(total_ref)
        count_ref[...] = jnp.zeros_like(count_ref)

    root, weighted, counts = one_hot(edges_ref, weight_ref, total_ref.shape[1], lanes)
    root_ref[...] = root
    weighted_ref[...] = weighted
    count_ref[...] += counts
    accumulate(weighted, cells_ref, begin, zones, pitch, total_ref, wide_ref)

    @pl.when(pl.program_id(0) == pl.num_programs(0) - 1)
    def _():
        for square in range(8):
            for shift in range(plan.line):
                at = rows_for(plan, square, shift, line_ref)
                out_refs[shift][square, HEAD:, :] = columns_of(total_ref, at, zones, lanes)
                out_refs[shift][square, 0:HEAD, :] = head_rows(*halves_of(count_ref[at, :]))


def first_kernel(plan, begin, zones, pitch, line_ref, weighted_ref, cells_ref, out_ref, total_ref, wide_ref):
    @pl.when(pl.program_id(0) == 0)
    def _():
        total_ref[...] = jnp.zeros_like(total_ref)

    accumulate(weighted_ref[...], cells_ref, begin, zones, pitch, total_ref, wide_ref)

    @pl.when(pl.program_id(0) == pl.num_programs(0) - 1)
    def _():
        for square in range(8):
            for shift in range(plan.line):
                at = rows_for(plan, square, shift, line_ref)
                out_ref[square, shift] = columns_of(total_ref, at, zones, cells_ref.shape[2])


def fixed(shape):
    return pl.BlockSpec(shape, lambda i: (0,) * len(shape))


def half_sums(kernel, plan, part, line, cells, operands, specs, outs, out_specs, counted):
    anchors, zones, lanes = cells.shape
    edges = plan.edges
    half = zones // 2
    rows = min(512, anchors)
    pitch = -(-half // 8) * 8 + 8
    if half % 16 == 0:
        block, begin = pl.BlockSpec((rows, half, lanes), lambda i: (i, part, 0)), 0
    else:
        block, begin = pl.BlockSpec((rows, zones, lanes), lambda i: (i, 0, 0)), part * half
    counts = [pltpu.VMEM((edges, lanes), F32)] if counted else []
    return pl.pallas_call(
        functools.partial(kernel, plan, begin, half, pitch),
        grid=(anchors // rows,),
        in_specs=[pl.BlockSpec(memory_space=pltpu.SMEM)] + specs + [block],
        out_specs=out_specs,
        out_shape=outs,
        scratch_shapes=[pltpu.VMEM((half // 2, edges, 2 * lanes), F32)] + counts + [pltpu.VMEM((rows * pitch, lanes), F32)],
        compiler_params=pltpu.CompilerParams(vmem_limit_bytes=60 * 1024 * 1024),
        cost_estimate=pl.CostEstimate(
            flops=4 * anchors * edges * zones * lanes, bytes_accessed=2 * anchors * zones * lanes, transcendentals=0
        ),
    )(line[None], *operands, cells)


def second_sums(line, cells, edges_t, edge_weight, plan):
    anchors, _, lanes = cells.shape
    rows = min(512, anchors)
    edges = plan.edges
    shape = (8, plan.second_rows, lanes)
    outs = [jax.ShapeDtypeStruct(shape, BF16)] * plan.line
    outs += [jax.ShapeDtypeStruct((1, anchors), F32), jax.ShapeDtypeStruct((edges, anchors), BF16)]
    out_specs = [fixed(shape)] * plan.line
    out_specs += [pl.BlockSpec((1, rows), lambda i: (0, i)), pl.BlockSpec((edges, rows), lambda i: (0, i))]
    specs = [pl.BlockSpec((edges_t.shape[0], rows), lambda i: (0, i)), fixed((1, edges))]
    operands = (edges_t, edge_weight[None, :])
    *seconds, roots, weighted = half_sums(second_kernel, plan, 1, line, cells, operands, specs, outs, out_specs, True)
    if not plan.relative:
        seconds = jnp.stack(seconds * 2)
        seconds = [lax.dynamic_index_in_dim(seconds, line + k, 0, keepdims=False) for k in range(plan.line)]
    return seconds, roots, weighted


def first_sums(line, cells, weighted, plan):
    rows = min(512, cells.shape[0])
    shape = (8, plan.line, plan.first_rows, cells.shape[2])
    specs = [pl.BlockSpec((plan.edges, rows), lambda i: (0, i))]
    out = jax.ShapeDtypeStruct(shape, BF16)
    first = half_sums(first_kernel, plan, 0, line, cells, (weighted,), specs, out, fixed(shape), False)
    if not plan.relative:
        first = lax.dynamic_slice_in_dim(jnp.concatenate([first, first], axis=1), line, plan.line, 1)
    return first


def add_up(pieces):
    total = pieces[0].astype(F32)
    for piece in pieces[1:]:
        total = total + piece.astype(F32)
    return total


def fold_first_kernel(plan, part_ref, *outs):
    for shift in range(plan.line):
        for quarter in range(4):
            outs[shift][quarter] = add_up([part_ref[quarter, shift], part_ref[4 + quarter, shift]]).astype(BF16)


def fold_second_kernel(plan, *refs):
    parts, out_ref = refs[: plan.line], refs[plan.line]
    for square in range(8):
        for rest in range(plan.rest):
            total = add_up([parts[shift][square] for shift in range(rest, plan.line, plan.rest)])
            half = HEAD // 2
            out_ref[square, rest, 0:HEAD, :] = head_rows(*halves_of(total[0:half] * COUNT_BASE + total[half:HEAD]))
            out_ref[square, rest, HEAD:, :] = total[HEAD:].astype(BF16)


def fold(kernel, plan, parts, shapes):
    whole = pl.BlockSpec(memory_space=pltpu.VMEM)
    size = sum(part.size for part in parts)
    return pl.pallas_call(
        functools.partial(kernel, plan),
        in_specs=[whole] * len(parts),
        out_specs=[whole] * len(shapes),
        out_shape=[jax.ShapeDtypeStruct(shape, BF16) for shape in shapes],
        compiler_params=pltpu.CompilerParams(vmem_limit_bytes=16 * 1024 * 1024),
        cost_estimate=pl.CostEstimate(flops=size, bytes_accessed=size * 4, transcendentals=0),
    )(*parts)


def org_sums(line, cells, edges_t, edge_weight, plan):
    lanes = cells.shape[-1]
    seconds, roots, weighted = second_sums(line, cells, edges_t, edge_weight, plan)
    seconds = [shifted(part, shift) if shift else part for shift, part in enumerate(seconds)]
    first = first_sums(line, cells, weighted, plan)
    first, seconds[1] = lax.optimization_barrier((first, seconds[1]))
    first = lax.all_to_all(first, SQUARE, split_axis=0, concat_axis=0, tiled=True)
    firsts = fold(fold_first_kernel, plan, [first], [(4, plan.first_rows, lanes)] * plan.line)
    firsts = [shifted(part, shift) if shift else part for shift, part in enumerate(firsts)]
    *firsts[1:3], seconds[2] = lax.optimization_barrier((*firsts[1:3], seconds[2]))
    second = fold(fold_second_kernel, plan, seconds, [(8, plan.rest, plan.second_rows, lanes)])[0]
    second = lax.all_to_all(second, SQUARE, split_axis=0, concat_axis=0, tiled=True)
    return firsts, second, roots


def table_kernel(plan, weight_ref, mixing_ref, matrix_ref, *refs):
    firsts = refs[: plan.line]
    second_ref, keep_ref, give_ref, mixed_ref = refs[plan.line :]
    own = plan.own
    lanes = mixing_ref.shape[0]
    half = HEAD // 2
    head = add_up([second_ref[0, 0, 0:HEAD, :], second_ref[4, 0, 0:HEAD, :]])
    counts = head[0:half] * COUNT_BASE + head[half:HEAD]
    scale = weight_ref[...] / counts[0:own]
    rows = plan.first_rows + plan.second_rows - HEAD
    zones = rows // own
    n_dst = 4 * plan.rest
    for k in range(n_dst):
        rest, quarter = k // 4, k % 4
        first = add_up([firsts[shift][quarter] for shift in range(rest, plan.line, plan.rest)])
        second = add_up([second_ref[quarter, rest, HEAD:, :], second_ref[4 + quarter, rest, HEAD:, :]])
        start = k * rows
        for total in (first, second):
            size = total.shape[0]
            totals = (total * jnp.concatenate([scale] * (size // own), axis=0)).astype(BF16)
            mixed = jnp.dot(totals, mixing_ref[...], preferred_element_type=F32)
            mixed_ref[start : start + size, :] = mixed
            start += size
    whole = n_dst * zones
    for e in range(own):
        mixed = mixed_ref[pl.ds(e, whole, stride=own), :] if own > 1 else mixed_ref[...]
        high = mixed.astype(BF16)
        low = (mixed - high.astype(F32)).astype(BF16)
        both = jnp.dot(matrix_ref[...], jnp.concatenate([high, low], axis=1), preferred_element_type=F32)
        result = (both[:, 0:lanes] + both[:, lanes : 2 * lanes]).astype(BF16)
        keep_ref[e] = result[0 : whole // 2]
        give_ref[e] = result[whole // 2 :]


def table_rows(firsts, second, weight_rows, mixing, matrix, plan):
    zones = matrix.shape[0]
    lanes = mixing.shape[0]
    whole = pl.BlockSpec(memory_space=pltpu.VMEM)
    half = jax.ShapeDtypeStruct((plan.own, zones // 2, lanes), BF16)
    return pl.pallas_call(
        functools.partial(table_kernel, plan),
        in_specs=[whole] * (4 + len(firsts)),
        out_specs=[whole] * 2,
        out_shape=[half, half],
        scratch_shapes=[pltpu.VMEM((zones * plan.own, lanes), F32)],
        compiler_params=pltpu.CompilerParams(vmem_limit_bytes=32 * 1024 * 1024),
        cost_estimate=pl.CostEstimate(
            flops=8 * plan.own * zones * lanes * lanes, bytes_accessed=4 * zones * plan.own * lanes, transcendentals=0
        ),
    )(weight_rows, mixing, matrix, *firsts, second)


def spread_kernel(sides, n_pieces, stride, offset, halves_ref, places_ref, root_ref, bias_ref, *refs):
    pieces = refs[: len(refs) - 4 - sides]
    tables = refs[len(refs) - 3 - sides : len(refs) - 3]
    out_ref = refs[len(refs) - 4 - sides]
    ring_ref, sems, ring_sems = refs[-3:]
    slots, _, rows, zones, lanes = ring_ref.shape
    steps = out_ref.shape[0] // rows

    copies = []
    for side in range(sides):
        for i, source in enumerate(pieces[side * n_pieces :][:n_pieces]):
            size = source.shape[0]
            place = tables[side].at[pl.ds(i * size, size)]
            copies.append(pltpu.make_async_copy(source, place, sems.at[len(copies)]))
    for copy in copies:
        copy.start()
    for copy in copies:
        copy.wait()

    bias = bias_ref[...]
    count = places_ref.shape[0]
    tile = 16
    batch = min(8, rows)
    tiles = zones // tile

    def leaving(step, slot, side):
        first_zone = pl.multiple_of(halves_ref[side] * stride + offset, 16)
        place = out_ref.at[pl.ds(step * rows, rows), pl.ds(first_zone, zones), :]
        return pltpu.make_async_copy(ring_ref.at[slot, side], place, ring_sems.at[slot, side])

    def one_step(step, carry):
        slot = lax.rem(step, slots)

        @pl.when(step >= slots)
        def _():
            for side in range(sides):
                leaving(step - slots, slot, side).wait()

        def several(group, inner):
            values = []
            for i in range(batch):
                at = step * rows + group * batch + i
                scale = root_ref[0, at]
                spots = [places_ref[j, at] for j in range(count)]
                for side in range(sides):
                    for first in range(0, zones, tile):
                        parts = [tables[side][spot, first : first + tile, :] for spot in spots]
                        parts = [(a + b).astype(F32) for a, b in zip(parts[0::2], parts[1::2])]
                        total = sum(parts[1:], parts[0])
                        values.append(jnp.maximum((total * scale + bias).astype(BF16), BF16(0.0)))
            for n, value in enumerate(values):
                i, side, start = n // (sides * tiles), n // tiles % sides, n % tiles * tile
                ring_ref[slot, side, group * batch + i, start : start + tile, :] = value
            return inner

        lax.fori_loop(0, rows // batch, several, 0)
        for side in range(sides):
            leaving(step, slot, side).start()
        return carry

    lax.fori_loop(0, steps, one_step, 0)
    for step in range(steps - slots, steps):
        for side in range(sides):
            leaving(step, step % slots, side).wait()


def spread(halves, places, root, bias, pieces, offset, stride, before=None):
    sides = len(pieces)
    anchors = places.shape[1]
    lanes = bias.shape[1]
    count, zones = len(pieces[0]), pieces[0][0].shape[1]
    edges = count * pieces[0][0].shape[0]
    rows = min(16, anchors // 8)
    slots = min(8, anchors // rows)
    smem = pl.BlockSpec(memory_space=pltpu.SMEM)
    anywhere = pl.BlockSpec(memory_space=pltpu.HBM)
    operands = [halves, places, root, bias] + [piece for side in pieces for piece in side]
    specs = [smem, smem, smem, pl.BlockSpec(memory_space=pltpu.VMEM)] + [anywhere] * (sides * count)
    aliases = {}
    if before is not None:
        aliases = {len(operands): 0}
        operands.append(before)
        specs.append(anywhere)
    return pl.pallas_call(
        functools.partial(spread_kernel, sides, count, stride, offset),
        in_specs=specs,
        out_specs=anywhere,
        out_shape=jax.ShapeDtypeStruct((anchors, 2 * stride, lanes), BF16),
        scratch_shapes=[pltpu.VMEM((edges, zones, lanes), BF16)] * sides
        + [
            pltpu.VMEM((slots, sides, rows, zones, lanes), BF16),
            pltpu.SemaphoreType.DMA((sides * count,)),
            pltpu.SemaphoreType.DMA((slots, sides)),
        ],
        input_output_aliases=aliases,
        compiler_params=pltpu.CompilerParams(vmem_limit_bytes=24 * 1024 * 1024),
        cost_estimate=pl.CostEstimate(
            flops=4096 * anchors * zones * lanes, bytes_accessed=4 * anchors * zones * lanes, transcendentals=0
        ),
    )(*operands)


LINE = ("slow", "rest")
SQUARE = ("mid", "near", "core")


def shifted(x, amount):
    size = lax.axis_size(LINE)
    return lax.ppermute(x, LINE, [(i, (i + amount) % size) for i in range(size)])


def crossed(x, turn):
    pairs = []
    for device in range(8):
        core = device % 2
        pairs.append((device, device ^ (2 if core == turn else 4)))
    return lax.ppermute(x, SQUARE, pairs)


def masked(x, mask):
    return lax.ppermute(x, SQUARE, [(device, device ^ mask) for device in range(8)])


def swapped(x):
    return lax.ppermute(x, "core", [(0, 1), (1, 0)])


def gather_table(keep, give, core):
    size = lax.axis_size(LINE)
    got = swapped(give)
    block = jnp.concatenate([jnp.where(core == 0, keep, got), jnp.where(core == 0, got, keep)], axis=0)
    split = block.shape[1] * 3 // 4
    long, short = block[:, :split], block[:, split:]
    line = [long] + [shifted(long, k) for k in range(1, size)]
    short = jnp.concatenate([short, masked(short, 2), masked(short, 4), masked(short, 6)], axis=0)
    long = jnp.concatenate(line, axis=0)
    short, long = lax.optimization_barrier((short, long))
    first = crossed(long, 0)
    second = crossed(long, 1)
    shorts = [short] + [shifted(short, k) for k in range(1, size)]
    first, shorts[1] = lax.optimization_barrier((first, shorts[1]))
    return [long, first, second, crossed(first, 1)], shorts


def places_of(ids, core, own):
    rest, size = lax.axis_size("rest"), lax.axis_size(LINE)
    owner = ids // own
    slot = owner % 2 * own + ids % own
    near = jnp.bitwise_xor(owner // 2 % 2, lax.axis_index("near"))
    mid = jnp.bitwise_xor(owner // (4 * rest) % 2, lax.axis_index("mid"))
    line = owner // (8 * rest) * rest + owner // 4 % rest
    line = lax.rem(lax.axis_index(LINE) - line + size, size)
    square = jnp.where(core == 0, 2 * mid + near, 2 * near + mid)
    short = (line * 4 + 2 * mid + near) * (2 * own) + slot
    return (square * size + line) * (2 * own) + slot, short


def relative_columns(matrix):
    zones, rest = matrix.shape[0], lax.axis_size("rest")
    if rest == 1:
        return matrix
    back = jnp.flip(matrix.reshape(zones, rest, -1), 1)
    back = jnp.concatenate([back, back], axis=1)
    return lax.dynamic_slice_in_dim(back, rest - 1 - lax.axis_index("rest"), rest, 1).reshape(zones, zones)


def shards(od_cells, anchor_edges, edge_weight, mixing, dst_edges, dst_weight, out_bias):
    n_org = lax.axis_size("slow") * lax.axis_size("mid")
    n_dst = lax.axis_size("rest") * lax.axis_size("near") * lax.axis_size("core")
    own = edge_weight.shape[0] // (n_org * n_dst)
    everyone = ("slow", "mid", "rest", "near", "core")
    core = lax.axis_index("core")
    edges_t = anchor_edges.T
    plan = Plan(od_cells.shape[1], edge_weight.shape[0], own, lax.axis_size("rest"), lax.axis_size(LINE))
    firsts, second, roots = org_sums(lax.axis_index(LINE), od_cells, edges_t, edge_weight, plan)
    own_weight = lax.dynamic_slice_in_dim(edge_weight, lax.axis_index(everyone) * own, own, 0)
    weight_rows = jnp.broadcast_to(own_weight[:, None], (own, mixing.shape[0]))
    matrix = relative_columns(dest_operator(dst_edges, dst_weight))
    half = matrix.shape[0] // 2
    matrix = jnp.where(core == 0, matrix, jnp.concatenate([matrix[half:], matrix[:half]], axis=0))
    keep, give = table_rows(firsts, second, weight_rows, mixing, matrix, plan)
    longs, shorts = gather_table(keep, give, core)
    rows = anchor_edges.shape[0] // n_dst
    start = lax.axis_index(("rest", "near", "core")) * rows
    ids = lax.dynamic_slice_in_dim(edges_t, start, rows, 1)
    own_root = lax.dynamic_slice_in_dim(roots, start, rows, 1)
    bias = out_bias[None, :]
    other = 1 - core
    long_places, short_places = places_of(ids, core, own)
    far_long_places, _ = places_of(ids, other, own)
    split = longs[0].shape[1]
    far = [swapped(x) for x in shorts]
    result = spread(jnp.stack([core, other]), short_places, own_root, bias, [shorts, far], split, half)
    result = spread(core[None], long_places, own_root, bias, [longs], 0, half, result)
    far = [swapped(x) for x in longs]
    return spread(other[None], far_long_places, own_root, bias, [far], 0, half, result)


def solution(mesh):
    n_org, n_dst = mesh.devices.shape
    fine = Mesh(mesh.devices.reshape(n_org // 2, 2, n_dst // 4, 2, 2), ("slow", "mid", "rest", "near", "core"))
    org, dst = ("slow", "mid"), ("rest", "near", "core")
    in_specs = (P(org, dst, None), P(org, None), P(), P(), P(), P(), P())
    out_specs = P(org + dst, None, None)
    return jax.shard_map(shards, mesh=fine, in_specs=in_specs, out_specs=out_specs, check_vma=False)
```

```python
import functools

import jax
import jax.numpy as jnp
from jax import lax
from jax.experimental import pallas as pl
from jax.experimental.pallas import tpu as pltpu
from jax.sharding import Mesh, PartitionSpec as P

BF16 = jnp.bfloat16
F32 = jnp.float32
COUNT_BASE = 256.0
HEAD = 16


def corridor_table(edge_ids, edge_count):
    columns = jnp.arange(edge_count, dtype=jnp.int32)
    return jnp.sum((edge_ids[:, :, None] == columns[None, None, :]).astype(F32), axis=1)


def dest_operator(dst_edges, dst_weight):
    dst_member = corridor_table(dst_edges, dst_weight.shape[0])
    dst_degree = jnp.sum(dst_member * dst_weight[None, :], axis=1)
    edge_sizes = jnp.sum(dst_member, axis=0)
    left_factor = dst_member * lax.rsqrt(dst_degree)[:, None]
    right_factor = left_factor * (dst_weight / edge_sizes)[None, :]
    result = jnp.dot(right_factor, left_factor.T, precision=lax.Precision.HIGHEST)
    return result.astype(BF16)


class Plan:
    def __init__(self, zones, edges, own, rest, line):
        self.edges = edges
        self.own = own
        self.rest = rest
        self.line = line
        self.cut = zones // 2
        self.first_rows = self.cut * own
        self.second_rows = HEAD + (zones - self.cut) * own

        self.relative = own % 8 == 0

    def device(self, square, line):
        core, near, mid = square % 2, square // 2 % 2, square // 4
        if isinstance(line, int):
            slow, rest = line // self.rest, line % self.rest
        else:
            slow, rest = lax.div(line, self.rest), lax.rem(line, self.rest)
        return (((slow * 2 + mid) * self.rest + rest) * 2 + near) * 2 + core


def halves_of(counts):
    high = jnp.floor(counts * (1.0 / COUNT_BASE))
    return high, counts - high * COUNT_BASE


def head_rows(high, low):
    parts = [high, low]
    if high.shape[0] < HEAD // 2:
        pad = jnp.zeros((HEAD // 2 - high.shape[0], high.shape[1]), F32)
        parts = [high, pad, low, pad]
    return jnp.concatenate(parts, axis=0).astype(BF16)


def one_hot(edges_ref, weight_ref, edges, lanes):
    ids = edges_ref[...]
    rows = ids.shape[1]
    columns = lax.broadcasted_iota(jnp.int32, (edges, rows), 0)
    member = columns == ids[0:1, :]
    for j in range(1, ids.shape[0]):
        member = jnp.logical_or(member, columns == ids[j : j + 1, :])
    upright = jnp.transpose(jnp.broadcast_to(weight_ref[...], (lanes, edges)))
    upright = jnp.concatenate([upright] * (rows // lanes), axis=1)
    root = lax.rsqrt(jnp.sum(jnp.where(member, upright, 0.0), axis=0, keepdims=True))
    rounded = root.astype(BF16).astype(F32)
    weighted = jnp.where(member, rounded, 0.0).astype(BF16)
    hot = jnp.where(member, 1.0, 0.0).astype(BF16)
    return root, weighted, jnp.dot(hot, jnp.ones((rows, lanes), BF16), preferred_element_type=F32)


def accumulate(weighted, cells_ref, begin, zones, pitch, total_ref, wide_ref):
    rows, _, lanes = cells_ref.shape
    part = 32

    def widen(i, carry):
        first = i * part
        piece = cells_ref[pl.ds(first, part), begin : begin + zones, :].astype(F32)
        for j in range(part):
            wide_ref[pl.ds(pl.multiple_of((first + j) * pitch, 8), zones), :] = piece[j]
        return carry

    lax.fori_loop(0, rows // part, widen, 0)
    for pair in range(zones // 2):
        left = wide_ref[pl.ds(2 * pair, rows, stride=pitch), :].astype(BF16)
        right = wide_ref[pl.ds(2 * pair + 1, rows, stride=pitch), :].astype(BF16)
        both = jnp.concatenate([left, right], axis=1)
        total_ref[pair] += jnp.dot(weighted, both, preferred_element_type=F32)


def columns_of(total_ref, at, zones, lanes):
    data = []
    for d in range(zones):
        data.append(total_ref[d // 2, at, (d % 2) * lanes : (d % 2 + 1) * lanes])
    return jnp.concatenate(data, axis=0).astype(BF16)


def rows_for(plan, square, shift, line_ref):
    own = plan.own
    if plan.relative:
        device = plan.device(square, lax.rem(line_ref[0] + shift, plan.line))
        return pl.ds(pl.multiple_of(device * own, own), own)
    device = plan.device(square, shift)
    return slice(device * own, (device + 1) * own)


def second_kernel(plan, begin, zones, pitch, line_ref, edges_ref, weight_ref, cells_ref, *refs):
    out_refs = refs[: plan.line]
    root_ref, weighted_ref, total_ref, count_ref, wide_ref = refs[plan.line :]
    lanes = cells_ref.shape[2]

    @pl.when(pl.program_id(0) == 0)
    def _():
        total_ref[...] = jnp.zeros_like(total_ref)
        count_ref[...] = jnp.zeros_like(count_ref)

    root, weighted, counts = one_hot(edges_ref, weight_ref, total_ref.shape[1], lanes)
    root_ref[...] = root
    weighted_ref[...] = weighted
    count_ref[...] += counts
    accumulate(weighted, cells_ref, begin, zones, pitch, total_ref, wide_ref)

    @pl.when(pl.program_id(0) == pl.num_programs(0) - 1)
    def _():
        for square in range(8):
            for shift in range(plan.line):
                at = rows_for(plan, square, shift, line_ref)
                out_refs[shift][square, HEAD:, :] = columns_of(total_ref, at, zones, lanes)
                out_refs[shift][square, 0:HEAD, :] = head_rows(*halves_of(count_ref[at, :]))


def first_kernel(plan, begin, zones, pitch, line_ref, weighted_ref, cells_ref, out_ref, total_ref, wide_ref):
    @pl.when(pl.program_id(0) == 0)
    def _():
        total_ref[...] = jnp.zeros_like(total_ref)

    accumulate(weighted_ref[...], cells_ref, begin, zones, pitch, total_ref, wide_ref)

    @pl.when(pl.program_id(0) == pl.num_programs(0) - 1)
    def _():
        for square in range(8):
            for shift in range(plan.line):
                at = rows_for(plan, square, shift, line_ref)
                out_ref[square, shift] = columns_of(total_ref, at, zones, cells_ref.shape[2])


def fixed(shape):
    return pl.BlockSpec(shape, lambda i: (0,) * len(shape))


def half_sums(kernel, plan, part, line, cells, operands, specs, outs, out_specs, counted):
    anchors, zones, lanes = cells.shape
    edges = plan.edges
    half = zones // 2
    rows = min(512, anchors)
    pitch = -(-half // 8) * 8 + 8
    if half % 16 == 0:
        block, begin = pl.BlockSpec((rows, half, lanes), lambda i: (i, part, 0)), 0
    else:
        block, begin = pl.BlockSpec((rows, zones, lanes), lambda i: (i, 0, 0)), part * half
    counts = [pltpu.VMEM((edges, lanes), F32)] if counted else []
    return pl.pallas_call(
        functools.partial(kernel, plan, begin, half, pitch),
        grid=(anchors // rows,),
        in_specs=[pl.BlockSpec(memory_space=pltpu.SMEM)] + specs + [block],
        out_specs=out_specs,
        out_shape=outs,
        scratch_shapes=[pltpu.VMEM((half // 2, edges, 2 * lanes), F32)] + counts + [pltpu.VMEM((rows * pitch, lanes), F32)],
        compiler_params=pltpu.CompilerParams(vmem_limit_bytes=60 * 1024 * 1024),
        cost_estimate=pl.CostEstimate(
            flops=4 * anchors * edges * zones * lanes, bytes_accessed=2 * anchors * zones * lanes, transcendentals=0
        ),
    )(line[None], *operands, cells)


def second_sums(line, cells, edges_t, edge_weight, plan):
    anchors, _, lanes = cells.shape
    rows = min(512, anchors)
    edges = plan.edges
    shape = (8, plan.second_rows, lanes)
    outs = [jax.ShapeDtypeStruct(shape, BF16)] * plan.line
    outs += [jax.ShapeDtypeStruct((1, anchors), F32), jax.ShapeDtypeStruct((edges, anchors), BF16)]
    out_specs = [fixed(shape)] * plan.line
    out_specs += [pl.BlockSpec((1, rows), lambda i: (0, i)), pl.BlockSpec((edges, rows), lambda i: (0, i))]
    specs = [pl.BlockSpec((edges_t.shape[0], rows), lambda i: (0, i)), fixed((1, edges))]
    operands = (edges_t, edge_weight[None, :])
    *seconds, roots, weighted = half_sums(second_kernel, plan, 1, line, cells, operands, specs, outs, out_specs, True)
    if not plan.relative:
        seconds = jnp.stack(seconds * 2)
        seconds = [lax.dynamic_index_in_dim(seconds, line + k, 0, keepdims=False) for k in range(plan.line)]
    return seconds, roots, weighted


def first_sums(line, cells, weighted, plan):
    rows = min(512, cells.shape[0])
    shape = (8, plan.line, plan.first_rows, cells.shape[2])
    specs = [pl.BlockSpec((plan.edges, rows), lambda i: (0, i))]
    out = jax.ShapeDtypeStruct(shape, BF16)
    first = half_sums(first_kernel, plan, 0, line, cells, (weighted,), specs, out, fixed(shape), False)
    if not plan.relative:
        first = lax.dynamic_slice_in_dim(jnp.concatenate([first, first], axis=1), line, plan.line, 1)
    return first


def add_up(pieces):
    total = pieces[0].astype(F32)
    for piece in pieces[1:]:
        total = total + piece.astype(F32)
    return total


def fold_first_kernel(plan, part_ref, *outs):
    for shift in range(plan.line):
        for quarter in range(4):
            outs[shift][quarter] = add_up([part_ref[quarter, shift], part_ref[4 + quarter, shift]]).astype(BF16)


def fold_second_kernel(plan, *refs):
    parts, out_ref = refs[: plan.line], refs[plan.line]
    for square in range(8):
        for rest in range(plan.rest):
            total = add_up([parts[shift][square] for shift in range(rest, plan.line, plan.rest)])
            half = HEAD // 2
            out_ref[square, rest, 0:HEAD, :] = head_rows(*halves_of(total[0:half] * COUNT_BASE + total[half:HEAD]))
            out_ref[square, rest, HEAD:, :] = total[HEAD:].astype(BF16)


def fold(kernel, plan, parts, shapes):
    whole = pl.BlockSpec(memory_space=pltpu.VMEM)
    size = sum(part.size for part in parts)
    return pl.pallas_call(
        functools.partial(kernel, plan),
        in_specs=[whole] * len(parts),
        out_specs=[whole] * len(shapes),
        out_shape=[jax.ShapeDtypeStruct(shape, BF16) for shape in shapes],
        compiler_params=pltpu.CompilerParams(vmem_limit_bytes=16 * 1024 * 1024),
        cost_estimate=pl.CostEstimate(flops=size, bytes_accessed=size * 4, transcendentals=0),
    )(*parts)


def org_sums(line, cells, edges_t, edge_weight, plan):
    lanes = cells.shape[-1]
    seconds, roots, weighted = second_sums(line, cells, edges_t, edge_weight, plan)
    seconds = [shifted(part, shift) if shift else part for shift, part in enumerate(seconds)]
    first = first_sums(line, cells, weighted, plan)
    first, seconds[1] = lax.optimization_barrier((first, seconds[1]))
    first = lax.all_to_all(first, SQUARE, split_axis=0, concat_axis=0, tiled=True)
    firsts = fold(fold_first_kernel, plan, [first], [(4, plan.first_rows, lanes)] * plan.line)
    firsts = [shifted(part, shift) if shift else part for shift, part in enumerate(firsts)]
    *firsts[1:3], seconds[2] = lax.optimization_barrier((*firsts[1:3], seconds[2]))
    second = fold(fold_second_kernel, plan, seconds, [(8, plan.rest, plan.second_rows, lanes)])[0]
    second = lax.all_to_all(second, SQUARE, split_axis=0, concat_axis=0, tiled=True)
    return firsts, second, roots


def table_kernel(plan, weight_ref, mixing_ref, matrix_ref, *refs):
    firsts = refs[: plan.line]
    second_ref, keep_ref, give_ref, mixed_ref = refs[plan.line :]
    own = plan.own
    lanes = mixing_ref.shape[0]
    half = HEAD // 2
    head = add_up([second_ref[0, 0, 0:HEAD, :], second_ref[4, 0, 0:HEAD, :]])
    counts = head[0:half] * COUNT_BASE + head[half:HEAD]
    scale = weight_ref[...] / counts[0:own]
    rows = plan.first_rows + plan.second_rows - HEAD
    zones = rows // own
    n_dst = 4 * plan.rest
    for k in range(n_dst):
        rest, quarter = k // 4, k % 4
        first = add_up([firsts[shift][quarter] for shift in range(rest, plan.line, plan.rest)])
        second = add_up([second_ref[quarter, rest, HEAD:, :], second_ref[4 + quarter, rest, HEAD:, :]])
        start = k * rows
        for total in (first, second):
            size = total.shape[0]
            totals = (total * jnp.concatenate([scale] * (size // own), axis=0)).astype(BF16)
            mixed = jnp.dot(totals, mixing_ref[...], preferred_element_type=F32)
            mixed_ref[start : start + size, :] = mixed
            start += size
    whole = n_dst * zones
    for e in range(own):
        mixed = mixed_ref[pl.ds(e, whole, stride=own), :] if own > 1 else mixed_ref[...]
        high = mixed.astype(BF16)
        low = (mixed - high.astype(F32)).astype(BF16)
        both = jnp.dot(matrix_ref[...], jnp.concatenate([high, low], axis=1), preferred_element_type=F32)
        result = (both[:, 0:lanes] + both[:, lanes : 2 * lanes]).astype(BF16)
        keep_ref[e] = result[0 : whole // 2]
        give_ref[e] = result[whole // 2 :]


def table_rows(firsts, second, weight_rows, mixing, matrix, plan):
    zones = matrix.shape[0]
    lanes = mixing.shape[0]
    whole = pl.BlockSpec(memory_space=pltpu.VMEM)
    half = jax.ShapeDtypeStruct((plan.own, zones // 2, lanes), BF16)
    return pl.pallas_call(
        functools.partial(table_kernel, plan),
        in_specs=[whole] * (4 + len(firsts)),
        out_specs=[whole] * 2,
        out_shape=[half, half],
        scratch_shapes=[pltpu.VMEM((zones * plan.own, lanes), F32)],
        compiler_params=pltpu.CompilerParams(vmem_limit_bytes=32 * 1024 * 1024),
        cost_estimate=pl.CostEstimate(
            flops=8 * plan.own * zones * lanes * lanes, bytes_accessed=4 * zones * plan.own * lanes, transcendentals=0
        ),
    )(weight_rows, mixing, matrix, *firsts, second)


def spread_kernel(sides, n_pieces, stride, offset, halves_ref, places_ref, root_ref, bias_ref, *refs):
    pieces = refs[: len(refs) - 4 - sides]
    tables = refs[len(refs) - 3 - sides : len(refs) - 3]
    out_ref = refs[len(refs) - 4 - sides]
    ring_ref, sems, ring_sems = refs[-3:]
    slots, _, rows, zones, lanes = ring_ref.shape
    steps = out_ref.shape[0] // rows

    copies = []
    for side in range(sides):
        for i, source in enumerate(pieces[side * n_pieces :][:n_pieces]):
            size = source.shape[0]
            place = tables[side].at[pl.ds(i * size, size)]
            copies.append(pltpu.make_async_copy(source, place, sems.at[len(copies)]))
    for copy in copies:
        copy.start()
    for copy in copies:
        copy.wait()

    bias = bias_ref[...]
    count = places_ref.shape[0]
    tile = 16
    batch = min(16, rows)
    tiles = zones // tile

    def leaving(step, slot, side):
        first_zone = pl.multiple_of(halves_ref[side] * stride + offset, 16)
        place = out_ref.at[pl.ds(step * rows, rows), pl.ds(first_zone, zones), :]
        return pltpu.make_async_copy(ring_ref.at[slot, side], place, ring_sems.at[slot, side])

    def one_step(step, carry):
        slot = lax.rem(step, slots)

        @pl.when(step >= slots)
        def _():
            for side in range(sides):
                leaving(step - slots, slot, side).wait()

        def several(group, inner):
            values = []
            for i in range(batch):
                at = step * rows + group * batch + i
                scale = root_ref[0, at]
                spots = [places_ref[j, at] for j in range(count)]
                for side in range(sides):
                    for first in range(0, zones, tile):
                        parts = [tables[side][spot, first : first + tile, :] for spot in spots]
                        parts = [(a + b).astype(F32) for a, b in zip(parts[0::2], parts[1::2])]
                        total = sum(parts[1:], parts[0])
                        values.append(jnp.maximum((total * scale + bias).astype(BF16), BF16(0.0)))
            for n, value in enumerate(values):
                i, side, start = n // (sides * tiles), n // tiles % sides, n % tiles * tile
                ring_ref[slot, side, group * batch + i, start : start + tile, :] = value
            return inner

        lax.fori_loop(0, rows // batch, several, 0)
        for side in range(sides):
            leaving(step, slot, side).start()
        return carry

    lax.fori_loop(0, steps, one_step, 0)
    for step in range(steps - slots, steps):
        for side in range(sides):
            leaving(step, step % slots, side).wait()


def spread(halves, places, root, bias, pieces, offset, stride, before=None):
    sides = len(pieces)
    anchors = places.shape[1]
    lanes = bias.shape[1]
    count, zones = len(pieces[0]), pieces[0][0].shape[1]
    edges = count * pieces[0][0].shape[0]
    rows = min(16, anchors // 8)
    slots = min(8, anchors // rows)
    smem = pl.BlockSpec(memory_space=pltpu.SMEM)
    anywhere = pl.BlockSpec(memory_space=pltpu.HBM)
    operands = [halves, places, root, bias] + [piece for side in pieces for piece in side]
    specs = [smem, smem, smem, pl.BlockSpec(memory_space=pltpu.VMEM)] + [anywhere] * (sides * count)
    aliases = {}
    if before is not None:
        aliases = {len(operands): 0}
        operands.append(before)
        specs.append(anywhere)
    return pl.pallas_call(
        functools.partial(spread_kernel, sides, count, stride, offset),
        in_specs=specs,
        out_specs=anywhere,
        out_shape=jax.ShapeDtypeStruct((anchors, 2 * stride, lanes), BF16),
        scratch_shapes=[pltpu.VMEM((edges, zones, lanes), BF16)] * sides
        + [
            pltpu.VMEM((slots, sides, rows, zones, lanes), BF16),
            pltpu.SemaphoreType.DMA((sides * count,)),
            pltpu.SemaphoreType.DMA((slots, sides)),
        ],
        input_output_aliases=aliases,
        compiler_params=pltpu.CompilerParams(vmem_limit_bytes=24 * 1024 * 1024),
        cost_estimate=pl.CostEstimate(
            flops=4096 * anchors * zones * lanes, bytes_accessed=4 * anchors * zones * lanes, transcendentals=0
        ),
    )(*operands)


LINE = ("slow", "rest")
SQUARE = ("mid", "near", "core")


def shifted(x, amount):
    size = lax.axis_size(LINE)
    return lax.ppermute(x, LINE, [(i, (i + amount) % size) for i in range(size)])


def crossed(x, turn):
    pairs = []
    for device in range(8):
        core = device % 2
        pairs.append((device, device ^ (2 if core == turn else 4)))
    return lax.ppermute(x, SQUARE, pairs)


def masked(x, mask):
    return lax.ppermute(x, SQUARE, [(device, device ^ mask) for device in range(8)])


def swapped(x):
    return lax.ppermute(x, "core", [(0, 1), (1, 0)])


def gather_table(keep, give, core):
    size = lax.axis_size(LINE)
    got = swapped(give)
    block = jnp.concatenate([jnp.where(core == 0, keep, got), jnp.where(core == 0, got, keep)], axis=0)
    split = block.shape[1] * 3 // 4
    long, short = block[:, :split], block[:, split:]
    line = [long] + [shifted(long, k) for k in range(1, size)]
    short = jnp.concatenate([short, masked(short, 2), masked(short, 4), masked(short, 6)], axis=0)
    long = jnp.concatenate(line, axis=0)
    short, long = lax.optimization_barrier((short, long))
    first = crossed(long, 0)
    second = crossed(long, 1)
    shorts = [short] + [shifted(short, k) for k in range(1, size)]
    first, shorts[1] = lax.optimization_barrier((first, shorts[1]))
    return [long, first, second, crossed(first, 1)], shorts


def places_of(ids, core, own):
    rest, size = lax.axis_size("rest"), lax.axis_size(LINE)
    owner = ids // own
    slot = owner % 2 * own + ids % own
    near = jnp.bitwise_xor(owner // 2 % 2, lax.axis_index("near"))
    mid = jnp.bitwise_xor(owner // (4 * rest) % 2, lax.axis_index("mid"))
    line = owner // (8 * rest) * rest + owner // 4 % rest
    line = lax.rem(lax.axis_index(LINE) - line + size, size)
    square = jnp.where(core == 0, 2 * mid + near, 2 * near + mid)
    short = (line * 4 + 2 * mid + near) * (2 * own) + slot
    return (square * size + line) * (2 * own) + slot, short


def relative_columns(matrix):
    zones, rest = matrix.shape[0], lax.axis_size("rest")
    if rest == 1:
        return matrix
    back = jnp.flip(matrix.reshape(zones, rest, -1), 1)
    back = jnp.concatenate([back, back], axis=1)
    return lax.dynamic_slice_in_dim(back, rest - 1 - lax.axis_index("rest"), rest, 1).reshape(zones, zones)


def shards(od_cells, anchor_edges, edge_weight, mixing, dst_edges, dst_weight, out_bias):
    n_org = lax.axis_size("slow") * lax.axis_size("mid")
    n_dst = lax.axis_size("rest") * lax.axis_size("near") * lax.axis_size("core")
    own = edge_weight.shape[0] // (n_org * n_dst)
    everyone = ("slow", "mid", "rest", "near", "core")
    core = lax.axis_index("core")
    edges_t = anchor_edges.T
    plan = Plan(od_cells.shape[1], edge_weight.shape[0], own, lax.axis_size("rest"), lax.axis_size(LINE))
    firsts, second, roots = org_sums(lax.axis_index(LINE), od_cells, edges_t, edge_weight, plan)
    own_weight = lax.dynamic_slice_in_dim(edge_weight, lax.axis_index(everyone) * own, own, 0)
    weight_rows = jnp.broadcast_to(own_weight[:, None], (own, mixing.shape[0]))
    matrix = relative_columns(dest_operator(dst_edges, dst_weight))
    half = matrix.shape[0] // 2
    matrix = jnp.where(core == 0, matrix, jnp.concatenate([matrix[half:], matrix[:half]], axis=0))
    keep, give = table_rows(firsts, second, weight_rows, mixing, matrix, plan)
    longs, shorts = gather_table(keep, give, core)
    rows = anchor_edges.shape[0] // n_dst
    start = lax.axis_index(("rest", "near", "core")) * rows
    ids = lax.dynamic_slice_in_dim(edges_t, start, rows, 1)
    own_root = lax.dynamic_slice_in_dim(roots, start, rows, 1)
    bias = out_bias[None, :]
    other = 1 - core
    long_places, short_places = places_of(ids, core, own)
    far_long_places, _ = places_of(ids, other, own)
    split = longs[0].shape[1]
    far = [swapped(x) for x in shorts]
    result = spread(jnp.stack([core, other]), short_places, own_root, bias, [shorts, far], split, half)
    result = spread(core[None], long_places, own_root, bias, [longs], 0, half, result)
    far = [swapped(x) for x in longs]
    return spread(other[None], far_long_places, own_root, bias, [far], 0, half, result)


def solution(mesh):
    n_org, n_dst = mesh.devices.shape
    fine = Mesh(mesh.devices.reshape(n_org // 2, 2, n_dst // 4, 2, 2), ("slow", "mid", "rest", "near", "core"))
    org, dst = ("slow", "mid"), ("rest", "near", "core")
    in_specs = (P(org, dst, None), P(org, None), P(), P(), P(), P(), P())
    out_specs = P(org + dst, None, None)
    return jax.shard_map(shards, mesh=fine, in_specs=in_specs, out_specs=out_specs, check_vma=False)
```

```python
import functools

import jax
import jax.numpy as jnp
from jax import lax
from jax.experimental import pallas as pl
from jax.experimental.pallas import tpu as pltpu
from jax.sharding import Mesh, PartitionSpec as P

BF16 = jnp.bfloat16
F32 = jnp.float32
COUNT_BASE = 256.0
HEAD = 16


def corridor_table(edge_ids, edge_count):
    columns = jnp.arange(edge_count, dtype=jnp.int32)
    return jnp.sum((edge_ids[:, :, None] == columns[None, None, :]).astype(F32), axis=1)


def dest_operator(dst_edges, dst_weight):
    dst_member = corridor_table(dst_edges, dst_weight.shape[0])
    dst_degree = jnp.sum(dst_member * dst_weight[None, :], axis=1)
    edge_sizes = jnp.sum(dst_member, axis=0)
    left_factor = dst_member * lax.rsqrt(dst_degree)[:, None]
    right_factor = left_factor * (dst_weight / edge_sizes)[None, :]
    result = jnp.dot(right_factor, left_factor.T, precision=lax.Precision.HIGHEST)
    return result.astype(BF16)


class Plan:
    def __init__(self, zones, edges, own, rest, line):
        self.edges = edges
        self.own = own
        self.rest = rest
        self.line = line
        self.cut = zones // 2
        self.first_rows = self.cut * own
        self.second_rows = HEAD + (zones - self.cut) * own

        self.relative = own % 8 == 0

    def device(self, square, line):
        core, near, mid = square % 2, square // 2 % 2, square // 4
        if isinstance(line, int):
            slow, rest = line // self.rest, line % self.rest
        else:
            slow, rest = lax.div(line, self.rest), lax.rem(line, self.rest)
        return (((slow * 2 + mid) * self.rest + rest) * 2 + near) * 2 + core


def halves_of(counts):
    high = jnp.floor(counts * (1.0 / COUNT_BASE))
    return high, counts - high * COUNT_BASE


def head_rows(high, low):
    parts = [high, low]
    if high.shape[0] < HEAD // 2:
        pad = jnp.zeros((HEAD // 2 - high.shape[0], high.shape[1]), F32)
        parts = [high, pad, low, pad]
    return jnp.concatenate(parts, axis=0).astype(BF16)


def one_hot(edges_ref, weight_ref, edges, lanes):
    ids = edges_ref[...]
    rows = ids.shape[1]
    columns = lax.broadcasted_iota(jnp.int32, (edges, rows), 0)
    member = columns == ids[0:1, :]
    for j in range(1, ids.shape[0]):
        member = jnp.logical_or(member, columns == ids[j : j + 1, :])
    upright = jnp.transpose(jnp.broadcast_to(weight_ref[...], (lanes, edges)))
    upright = jnp.concatenate([upright] * (rows // lanes), axis=1)
    root = lax.rsqrt(jnp.sum(jnp.where(member, upright, 0.0), axis=0, keepdims=True))
    rounded = root.astype(BF16).astype(F32)
    weighted = jnp.where(member, rounded, 0.0).astype(BF16)
    hot = jnp.where(member, 1.0, 0.0).astype(BF16)
    return root, weighted, jnp.dot(hot, jnp.ones((rows, lanes), BF16), preferred_element_type=F32)


def accumulate(weighted, cells_ref, begin, zones, pitch, total_ref, wide_ref):
    rows, _, lanes = cells_ref.shape
    part = 32

    def widen(i, carry):
        first = i * part
        piece = cells_ref[pl.ds(first, part), begin : begin + zones, :].astype(F32)
        for j in range(part):
            wide_ref[pl.ds(pl.multiple_of((first + j) * pitch, 8), zones), :] = piece[j]
        return carry

    lax.fori_loop(0, rows // part, widen, 0)
    for pair in range(zones // 2):
        left = wide_ref[pl.ds(2 * pair, rows, stride=pitch), :].astype(BF16)
        right = wide_ref[pl.ds(2 * pair + 1, rows, stride=pitch), :].astype(BF16)
        both = jnp.concatenate([left, right], axis=1)
        total_ref[pair] += jnp.dot(weighted, both, preferred_element_type=F32)


def columns_of(total_ref, at, zones, lanes):
    data = []
    for d in range(zones):
        data.append(total_ref[d // 2, at, (d % 2) * lanes : (d % 2 + 1) * lanes])
    return jnp.concatenate(data, axis=0).astype(BF16)


def rows_for(plan, square, shift, line_ref):
    own = plan.own
    if plan.relative:
        device = plan.device(square, lax.rem(line_ref[0] + shift, plan.line))
        return pl.ds(pl.multiple_of(device * own, own), own)
    device = plan.device(square, shift)
    return slice(device * own, (device + 1) * own)


def second_kernel(plan, begin, zones, pitch, line_ref, edges_ref, weight_ref, cells_ref, *refs):
    out_refs = refs[: plan.line]
    root_ref, weighted_ref, total_ref, count_ref, wide_ref = refs[plan.line :]
    lanes = cells_ref.shape[2]

    @pl.when(pl.program_id(0) == 0)
    def _():
        total_ref[...] = jnp.zeros_like(total_ref)
        count_ref[...] = jnp.zeros_like(count_ref)

    root, weighted, counts = one_hot(edges_ref, weight_ref, total_ref.shape[1], lanes)
    root_ref[...] = root
    weighted_ref[...] = weighted
    count_ref[...] += counts
    accumulate(weighted, cells_ref, begin, zones, pitch, total_ref, wide_ref)

    @pl.when(pl.program_id(0) == pl.num_programs(0) - 1)
    def _():
        for square in range(8):
            for shift in range(plan.line):
                at = rows_for(plan, square, shift, line_ref)
                out_refs[shift][square, HEAD:, :] = columns_of(total_ref, at, zones, lanes)
                out_refs[shift][square, 0:HEAD, :] = head_rows(*halves_of(count_ref[at, :]))


def first_kernel(plan, begin, zones, pitch, line_ref, weighted_ref, cells_ref, out_ref, total_ref, wide_ref):
    @pl.when(pl.program_id(0) == 0)
    def _():
        total_ref[...] = jnp.zeros_like(total_ref)

    accumulate(weighted_ref[...], cells_ref, begin, zones, pitch, total_ref, wide_ref)

    @pl.when(pl.program_id(0) == pl.num_programs(0) - 1)
    def _():
        for square in range(8):
            for shift in range(plan.line):
                at = rows_for(plan, square, shift, line_ref)
                out_ref[square, shift] = columns_of(total_ref, at, zones, cells_ref.shape[2])


def fixed(shape):
    return pl.BlockSpec(shape, lambda i: (0,) * len(shape))


def half_sums(kernel, plan, part, line, cells, operands, specs, outs, out_specs, counted):
    anchors, zones, lanes = cells.shape
    edges = plan.edges
    half = zones // 2
    rows = min(512, anchors)
    pitch = -(-half // 8) * 8 + 8
    if half % 16 == 0:
        block, begin = pl.BlockSpec((rows, half, lanes), lambda i: (i, part, 0)), 0
    else:
        block, begin = pl.BlockSpec((rows, zones, lanes), lambda i: (i, 0, 0)), part * half
    counts = [pltpu.VMEM((edges, lanes), F32)] if counted else []
    return pl.pallas_call(
        functools.partial(kernel, plan, begin, half, pitch),
        grid=(anchors // rows,),
        in_specs=[pl.BlockSpec(memory_space=pltpu.SMEM)] + specs + [block],
        out_specs=out_specs,
        out_shape=outs,
        scratch_shapes=[pltpu.VMEM((half // 2, edges, 2 * lanes), F32)] + counts + [pltpu.VMEM((rows * pitch, lanes), F32)],
        compiler_params=pltpu.CompilerParams(vmem_limit_bytes=60 * 1024 * 1024),
        cost_estimate=pl.CostEstimate(
            flops=4 * anchors * edges * zones * lanes, bytes_accessed=2 * anchors * zones * lanes, transcendentals=0
        ),
    )(line[None], *operands, cells)


def second_sums(line, cells, edges_t, edge_weight, plan):
    anchors, _, lanes = cells.shape
    rows = min(512, anchors)
    edges = plan.edges
    shape = (8, plan.second_rows, lanes)
    outs = [jax.ShapeDtypeStruct(shape, BF16)] * plan.line
    outs += [jax.ShapeDtypeStruct((1, anchors), F32), jax.ShapeDtypeStruct((edges, anchors), BF16)]
    out_specs = [fixed(shape)] * plan.line
    out_specs += [pl.BlockSpec((1, rows), lambda i: (0, i)), pl.BlockSpec((edges, rows), lambda i: (0, i))]
    specs = [pl.BlockSpec((edges_t.shape[0], rows), lambda i: (0, i)), fixed((1, edges))]
    operands = (edges_t, edge_weight[None, :])
    *seconds, roots, weighted = half_sums(second_kernel, plan, 1, line, cells, operands, specs, outs, out_specs, True)
    if not plan.relative:
        seconds = jnp.stack(seconds * 2)
        seconds = [lax.dynamic_index_in_dim(seconds, line + k, 0, keepdims=False) for k in range(plan.line)]
    return seconds, roots, weighted


def first_sums(line, cells, weighted, plan):
    rows = min(512, cells.shape[0])
    shape = (8, plan.line, plan.first_rows, cells.shape[2])
    specs = [pl.BlockSpec((plan.edges, rows), lambda i: (0, i))]
    out = jax.ShapeDtypeStruct(shape, BF16)
    first = half_sums(first_kernel, plan, 0, line, cells, (weighted,), specs, out, fixed(shape), False)
    if not plan.relative:
        first = lax.dynamic_slice_in_dim(jnp.concatenate([first, first], axis=1), line, plan.line, 1)
    return first


def add_up(pieces):
    total = pieces[0].astype(F32)
    for piece in pieces[1:]:
        total = total + piece.astype(F32)
    return total


def fold_first_kernel(plan, part_ref, *outs):
    for shift in range(plan.line):
        for quarter in range(4):
            outs[shift][quarter] = add_up([part_ref[quarter, shift], part_ref[4 + quarter, shift]]).astype(BF16)


def fold_second_kernel(plan, *refs):
    parts, out_ref = refs[: plan.line], refs[plan.line]
    for square in range(8):
        for rest in range(plan.rest):
            total = add_up([parts[shift][square] for shift in range(rest, plan.line, plan.rest)])
            half = HEAD // 2
            out_ref[square, rest, 0:HEAD, :] = head_rows(*halves_of(total[0:half] * COUNT_BASE + total[half:HEAD]))
            out_ref[square, rest, HEAD:, :] = total[HEAD:].astype(BF16)


def fold(kernel, plan, parts, shapes):
    whole = pl.BlockSpec(memory_space=pltpu.VMEM)
    size = sum(part.size for part in parts)
    return pl.pallas_call(
        functools.partial(kernel, plan),
        in_specs=[whole] * len(parts),
        out_specs=[whole] * len(shapes),
        out_shape=[jax.ShapeDtypeStruct(shape, BF16) for shape in shapes],
        compiler_params=pltpu.CompilerParams(vmem_limit_bytes=16 * 1024 * 1024),
        cost_estimate=pl.CostEstimate(flops=size, bytes_accessed=size * 4, transcendentals=0),
    )(*parts)


def org_sums(line, cells, edges_t, edge_weight, plan):
    lanes = cells.shape[-1]
    seconds, roots, weighted = second_sums(line, cells, edges_t, edge_weight, plan)
    seconds = [shifted(part, shift) if shift else part for shift, part in enumerate(seconds)]
    first = first_sums(line, cells, weighted, plan)
    first, seconds[1] = lax.optimization_barrier((first, seconds[1]))
    first = lax.all_to_all(first, SQUARE, split_axis=0, concat_axis=0, tiled=True)
    firsts = fold(fold_first_kernel, plan, [first], [(4, plan.first_rows, lanes)] * plan.line)
    firsts = [shifted(part, shift) if shift else part for shift, part in enumerate(firsts)]
    *firsts[1:], seconds[2] = lax.optimization_barrier((*firsts[1:], seconds[2]))
    second = fold(fold_second_kernel, plan, seconds, [(8, plan.rest, plan.second_rows, lanes)])[0]
    second = lax.all_to_all(second, SQUARE, split_axis=0, concat_axis=0, tiled=True)
    return firsts, second, roots


def table_kernel(plan, weight_ref, mixing_ref, matrix_ref, *refs):
    firsts = refs[: plan.line]
    second_ref, keep_ref, give_ref, mixed_ref = refs[plan.line :]
    own = plan.own
    lanes = mixing_ref.shape[0]
    half = HEAD // 2
    head = add_up([second_ref[0, 0, 0:HEAD, :], second_ref[4, 0, 0:HEAD, :]])
    counts = head[0:half] * COUNT_BASE + head[half:HEAD]
    scale = weight_ref[...] / counts[0:own]
    rows = plan.first_rows + plan.second_rows - HEAD
    zones = rows // own
    n_dst = 4 * plan.rest
    for k in range(n_dst):
        rest, quarter = k // 4, k % 4
        first = add_up([firsts[shift][quarter] for shift in range(rest, plan.line, plan.rest)])
        second = add_up([second_ref[quarter, rest, HEAD:, :], second_ref[4 + quarter, rest, HEAD:, :]])
        start = k * rows
        for total in (first, second):
            size = total.shape[0]
            totals = (total * jnp.concatenate([scale] * (size // own), axis=0)).astype(BF16)
            mixed = jnp.dot(totals, mixing_ref[...], preferred_element_type=F32)
            mixed_ref[start : start + size, :] = mixed
            start += size
    whole = n_dst * zones
    for e in range(own):
        mixed = mixed_ref[pl.ds(e, whole, stride=own), :] if own > 1 else mixed_ref[...]
        high = mixed.astype(BF16)
        low = (mixed - high.astype(F32)).astype(BF16)
        both = jnp.dot(matrix_ref[...], jnp.concatenate([high, low], axis=1), preferred_element_type=F32)
        result = (both[:, 0:lanes] + both[:, lanes : 2 * lanes]).astype(BF16)
        keep_ref[e] = result[0 : whole // 2]
        give_ref[e] = result[whole // 2 :]


def table_rows(firsts, second, weight_rows, mixing, matrix, plan):
    zones = matrix.shape[0]
    lanes = mixing.shape[0]
    whole = pl.BlockSpec(memory_space=pltpu.VMEM)
    half = jax.ShapeDtypeStruct((plan.own, zones // 2, lanes), BF16)
    return pl.pallas_call(
        functools.partial(table_kernel, plan),
        in_specs=[whole] * (4 + len(firsts)),
        out_specs=[whole] * 2,
        out_shape=[half, half],
        scratch_shapes=[pltpu.VMEM((zones * plan.own, lanes), F32)],
        compiler_params=pltpu.CompilerParams(vmem_limit_bytes=32 * 1024 * 1024),
        cost_estimate=pl.CostEstimate(
            flops=8 * plan.own * zones * lanes * lanes, bytes_accessed=4 * zones * plan.own * lanes, transcendentals=0
        ),
    )(weight_rows, mixing, matrix, *firsts, second)


def spread_kernel(sides, n_pieces, stride, offset, halves_ref, places_ref, root_ref, bias_ref, *refs):
    pieces = refs[: len(refs) - 4 - sides]
    tables = refs[len(refs) - 3 - sides : len(refs) - 3]
    out_ref = refs[len(refs) - 4 - sides]
    ring_ref, sems, ring_sems = refs[-3:]
    slots, _, rows, zones, lanes = ring_ref.shape
    steps = out_ref.shape[0] // rows

    copies = []
    for side in range(sides):
        for i, source in enumerate(pieces[side * n_pieces :][:n_pieces]):
            size = source.shape[0]
            place = tables[side].at[pl.ds(i * size, size)]
            copies.append(pltpu.make_async_copy(source, place, sems.at[len(copies)]))
    for copy in copies:
        copy.start()
    for copy in copies:
        copy.wait()

    bias = bias_ref[...]
    count = places_ref.shape[0]
    tile = 16
    batch = min(16, rows)
    tiles = zones // tile

    def leaving(step, slot, side):
        first_zone = pl.multiple_of(halves_ref[side] * stride + offset, 16)
        place = out_ref.at[pl.ds(step * rows, rows), pl.ds(first_zone, zones), :]
        return pltpu.make_async_copy(ring_ref.at[slot, side], place, ring_sems.at[slot, side])

    def one_step(step, carry):
        slot = lax.rem(step, slots)

        @pl.when(step >= slots)
        def _():
            for side in range(sides):
                leaving(step - slots, slot, side).wait()

        def several(group, inner):
            values = []
            for i in range(batch):
                at = step * rows + group * batch + i
                scale = root_ref[0, at]
                spots = [places_ref[j, at] for j in range(count)]
                for side in range(sides):
                    for first in range(0, zones, tile):
                        parts = [tables[side][spot, first : first + tile, :] for spot in spots]
                        parts = [(a + b).astype(F32) for a, b in zip(parts[0::2], parts[1::2])]
                        total = sum(parts[1:], parts[0])
                        values.append(jnp.maximum((total * scale + bias).astype(BF16), BF16(0.0)))
            for n, value in enumerate(values):
                i, side, start = n // (sides * tiles), n // tiles % sides, n % tiles * tile
                ring_ref[slot, side, group * batch + i, start : start + tile, :] = value
            return inner

        lax.fori_loop(0, rows // batch, several, 0)
        for side in range(sides):
            leaving(step, slot, side).start()
        return carry

    lax.fori_loop(0, steps, one_step, 0)
    for step in range(steps - slots, steps):
        for side in range(sides):
            leaving(step, step % slots, side).wait()


def spread(halves, places, root, bias, pieces, offset, stride, before=None):
    sides = len(pieces)
    anchors = places.shape[1]
    lanes = bias.shape[1]
    count, zones = len(pieces[0]), pieces[0][0].shape[1]
    edges = count * pieces[0][0].shape[0]
    rows = min(16, anchors // 8)
    slots = min(8, anchors // rows)
    smem = pl.BlockSpec(memory_space=pltpu.SMEM)
    anywhere = pl.BlockSpec(memory_space=pltpu.HBM)
    operands = [halves, places, root, bias] + [piece for side in pieces for piece in side]
    specs = [smem, smem, smem, pl.BlockSpec(memory_space=pltpu.VMEM)] + [anywhere] * (sides * count)
    aliases = {}
    if before is not None:
        aliases = {len(operands): 0}
        operands.append(before)
        specs.append(anywhere)
    return pl.pallas_call(
        functools.partial(spread_kernel, sides, count, stride, offset),
        in_specs=specs,
        out_specs=anywhere,
        out_shape=jax.ShapeDtypeStruct((anchors, 2 * stride, lanes), BF16),
        scratch_shapes=[pltpu.VMEM((edges, zones, lanes), BF16)] * sides
        + [
            pltpu.VMEM((slots, sides, rows, zones, lanes), BF16),
            pltpu.SemaphoreType.DMA((sides * count,)),
            pltpu.SemaphoreType.DMA((slots, sides)),
        ],
        input_output_aliases=aliases,
        compiler_params=pltpu.CompilerParams(vmem_limit_bytes=24 * 1024 * 1024),
        cost_estimate=pl.CostEstimate(
            flops=4096 * anchors * zones * lanes, bytes_accessed=4 * anchors * zones * lanes, transcendentals=0
        ),
    )(*operands)


LINE = ("slow", "rest")
SQUARE = ("mid", "near", "core")


def shifted(x, amount):
    size = lax.axis_size(LINE)
    return lax.ppermute(x, LINE, [(i, (i + amount) % size) for i in range(size)])


def crossed(x, turn):
    pairs = []
    for device in range(8):
        core = device % 2
        pairs.append((device, device ^ (2 if core == turn else 4)))
    return lax.ppermute(x, SQUARE, pairs)


def masked(x, mask):
    return lax.ppermute(x, SQUARE, [(device, device ^ mask) for device in range(8)])


def swapped(x):
    return lax.ppermute(x, "core", [(0, 1), (1, 0)])


def gather_table(keep, give, core):
    size = lax.axis_size(LINE)
    got = swapped(give)
    block = jnp.concatenate([jnp.where(core == 0, keep, got), jnp.where(core == 0, got, keep)], axis=0)
    split = block.shape[1] * 3 // 4
    long, short = block[:, :split], block[:, split:]
    line = [long] + [shifted(long, k) for k in range(1, size)]
    short = jnp.concatenate([short, masked(short, 2), masked(short, 4), masked(short, 6)], axis=0)
    long = jnp.concatenate(line, axis=0)
    short, long = lax.optimization_barrier((short, long))
    first = crossed(long, 0)
    second = crossed(long, 1)
    shorts = [short] + [shifted(short, k) for k in range(1, size)]
    first, shorts[1] = lax.optimization_barrier((first, shorts[1]))
    return [long, first, second, crossed(first, 1)], shorts


def places_of(ids, core, own):
    rest, size = lax.axis_size("rest"), lax.axis_size(LINE)
    owner = ids // own
    slot = owner % 2 * own + ids % own
    near = jnp.bitwise_xor(owner // 2 % 2, lax.axis_index("near"))
    mid = jnp.bitwise_xor(owner // (4 * rest) % 2, lax.axis_index("mid"))
    line = owner // (8 * rest) * rest + owner // 4 % rest
    line = lax.rem(lax.axis_index(LINE) - line + size, size)
    square = jnp.where(core == 0, 2 * mid + near, 2 * near + mid)
    short = (line * 4 + 2 * mid + near) * (2 * own) + slot
    return (square * size + line) * (2 * own) + slot, short


def relative_columns(matrix):
    zones, rest = matrix.shape[0], lax.axis_size("rest")
    if rest == 1:
        return matrix
    back = jnp.flip(matrix.reshape(zones, rest, -1), 1)
    back = jnp.concatenate([back, back], axis=1)
    return lax.dynamic_slice_in_dim(back, rest - 1 - lax.axis_index("rest"), rest, 1).reshape(zones, zones)


def shards(od_cells, anchor_edges, edge_weight, mixing, dst_edges, dst_weight, out_bias):
    n_org = lax.axis_size("slow") * lax.axis_size("mid")
    n_dst = lax.axis_size("rest") * lax.axis_size("near") * lax.axis_size("core")
    own = edge_weight.shape[0] // (n_org * n_dst)
    everyone = ("slow", "mid", "rest", "near", "core")
    core = lax.axis_index("core")
    edges_t = anchor_edges.T
    plan = Plan(od_cells.shape[1], edge_weight.shape[0], own, lax.axis_size("rest"), lax.axis_size(LINE))
    firsts, second, roots = org_sums(lax.axis_index(LINE), od_cells, edges_t, edge_weight, plan)
    own_weight = lax.dynamic_slice_in_dim(edge_weight, lax.axis_index(everyone) * own, own, 0)
    weight_rows = jnp.broadcast_to(own_weight[:, None], (own, mixing.shape[0]))
    matrix = relative_columns(dest_operator(dst_edges, dst_weight))
    half = matrix.shape[0] // 2
    matrix = jnp.where(core == 0, matrix, jnp.concatenate([matrix[half:], matrix[:half]], axis=0))
    keep, give = table_rows(firsts, second, weight_rows, mixing, matrix, plan)
    longs, shorts = gather_table(keep, give, core)
    rows = anchor_edges.shape[0] // n_dst
    start = lax.axis_index(("rest", "near", "core")) * rows
    ids = lax.dynamic_slice_in_dim(edges_t, start, rows, 1)
    own_root = lax.dynamic_slice_in_dim(roots, start, rows, 1)
    bias = out_bias[None, :]
    other = 1 - core
    long_places, short_places = places_of(ids, core, own)
    far_long_places, _ = places_of(ids, other, own)
    split = longs[0].shape[1]
    far = [swapped(x) for x in shorts]
    result = spread(jnp.stack([core, other]), short_places, own_root, bias, [shorts, far], split, half)
    result = spread(core[None], long_places, own_root, bias, [longs], 0, half, result)
    far = [swapped(x) for x in longs]
    return spread(other[None], far_long_places, own_root, bias, [far], 0, half, result)


def solution(mesh):
    n_org, n_dst = mesh.devices.shape
    fine = Mesh(mesh.devices.reshape(n_org // 2, 2, n_dst // 4, 2, 2), ("slow", "mid", "rest", "near", "core"))
    org, dst = ("slow", "mid"), ("rest", "near", "core")
    in_specs = (P(org, dst, None), P(org, None), P(), P(), P(), P(), P())
    out_specs = P(org + dst, None, None)
    return jax.shard_map(shards, mesh=fine, in_specs=in_specs, out_specs=out_specs, check_vma=False)
```
